32 devices in a mesh: var: 8 (over z, y), samp: 4 (over x, core).
Axes of the slice: x: 2, y: 2, z: 4, core: 2. Of those that a mesh axis runs over, the one named last changes fastest.
Arguments:
- dosage: bfloat16 [16384, 4096], P('samp', 'var'), may hold values from 0 to 2
- pair_offsets: int32 [8, 3], P('var'), may hold values from -1 to 2, as said below
- live_counts: int32 [8], P('var'), may hold values from 256 to 512, as said below
Outputs:
- ld_upper: bfloat16 [8, 3, 512, 512], P('var', None, 'samp')
- ld_mirror: bfloat16 [8, 2, 512, 512], P('var', None, 'samp')
The draws below stay inside these ranges and needn't reach their ends.
Inputs may be any that keep to these rules, and one draw needn't show every extreme that they name: `pair_offsets`: row i lists distinct offsets in increasing order, first always 0, each with i + offset < 8; unused slots at the end hold -1. The first live_counts[i] variants of block i are real, the rest of the block is padding and is left out.
All inputs are finite; a program needn't handle non-finite values.
Results may differ from the reference program's by a relative error of at most 0.0034.
Values may be sent and summed in bfloat16 or wider, within the bound.
No kernel may reach another device: no remote copies, remote signals or barrier semaphores. Data moves between devices by JAX's collectives and lax.ppermute only.
A program may use at most 320 MiB of HBM per device.

```python
import jax
import jax.numpy as jnp
from jax import lax

BLK = 512
BAND = 2
SLOTS = 3
NBLK = 8
VARIANTS = 4096
SAMPLES = 16384


def draw_dosage(key, part):
    key = jax.random.fold_in(key, 11)
    keys = jax.random.split(key, 9)
    noise = jax.random.normal(keys[0], (SAMPLES, VARIANTS), jnp.float32)
    ramp_lo = 0.6
    ramp_hi = 1.8
    drift = 0.4
    fine = max(BLK // 16, 1)
    reach_blocks = 8
    factor_fine = jnp.repeat(jax.random.normal(keys[1], (SAMPLES, VARIANTS // fine), jnp.float32), fine, axis=1)
    factor_block = jnp.repeat(jax.random.normal(keys[2], (SAMPLES, VARIANTS // BLK), jnp.float32), BLK, axis=1)
    latent = jax.random.normal(keys[3], (SAMPLES, NBLK + reach_blocks - 1), jnp.float32)
    moving = latent[:, 0:NBLK]
    for lag in range(1, reach_blocks):
        moving = moving + latent[:, lag:lag + NBLK]
    moving = moving * (1.0 / reach_blocks ** 0.5)
    factor_wide = jnp.repeat(moving, BLK, axis=1)
    load_fine = jax.random.uniform(keys[4], (1, VARIANTS), jnp.float32, 0.2, 1.0)
    load_block = jax.random.uniform(keys[5], (1, VARIANTS), jnp.float32, 0.2, 1.0)
    load_wide = jax.random.uniform(keys[7], (1, VARIANTS), jnp.float32, 0.3, 1.0)
    mixed = noise + load_fine * factor_fine + load_block * factor_block + load_wide * factor_wide
    place = (jnp.arange(SAMPLES, dtype=jnp.float32) / max(SAMPLES - 1, 1))[:, None]
    ramp = ramp_lo + (ramp_hi - ramp_lo) * place
    shift = jax.random.uniform(keys[8], (1, VARIANTS), jnp.float32, -drift, drift)
    centre = 1.0 + shift * (place - 0.5)
    return jnp.clip(centre + 0.3 * ramp * mixed, 0.0, 2.0).astype(jnp.bfloat16)


def draw_pair_offsets(key, part):
    key = jax.random.fold_in(key, 23)
    flags = jax.random.randint(key, (NBLK, BAND), 0, 3) > 0
    steps = jnp.arange(1, BAND + 1, dtype=jnp.int32)
    blocks = jnp.arange(NBLK, dtype=jnp.int32)
    inside = blocks[:, None] + steps[None, :] < NBLK
    flags = (flags | (blocks[:, None] == 0)) & inside
    keys = jnp.where(flags, steps[None, :], SLOTS + steps[None, :])
    keys = jnp.concatenate([jnp.zeros((NBLK, 1), jnp.int32), keys], axis=1)
    ordered = jnp.sort(keys, axis=1)
    return jnp.where(ordered < SLOTS, ordered, -1).astype(jnp.int32)


def draw_live_counts(key, part):
    key = jax.random.fold_in(key, 37)
    counts = jax.random.randint(key, (NBLK,), BLK // 2, BLK + 1)
    counts = counts.at[0].set(BLK)
    counts = counts.at[1].set(BLK // 2)
    return counts.astype(jnp.int32)


def setup_inputs(seed: int = 0) -> dict:
    key_of = jax.random.split(jax.random.key(seed), 4)
    return {
        "dosage": draw_dosage(jax.random.fold_in(key_of[3], 71), 0),
        "pair_offsets": draw_pair_offsets(jax.random.fold_in(key_of[3], 71), 0),
        "live_counts": draw_live_counts(jax.random.fold_in(key_of[3], 71), 0),
    }


def reference(dosage, pair_offsets, live_counts):
    values = dosage.astype(jnp.float32)
    mean = lax.optimization_barrier(jnp.mean(values, axis=0))
    centered = values - mean
    spread = lax.optimization_barrier(jnp.mean(centered * centered, axis=0))
    position = jnp.arange(BLK, dtype=jnp.int32)
    live = (position[None, :] < live_counts[:, None]).reshape(VARIANTS)
    std_dose = jnp.where(live, centered * lax.rsqrt(spread + 1e-05), 0.0).astype(jnp.bfloat16)
    blocks = std_dose.reshape(SAMPLES, NBLK, BLK)

    def one_block(index):
        index = index.astype(jnp.int32)
        own = lax.dynamic_index_in_dim(blocks, index, 1, keepdims=False).astype(jnp.float32)
        tiles = []
        for slot in range(SLOTS):
            offset = pair_offsets[index, slot]
            other = jnp.minimum(index + jnp.maximum(offset, 0), NBLK - 1).astype(jnp.int32)
            partner = lax.dynamic_index_in_dim(blocks, other, 1, keepdims=False).astype(jnp.float32)
            tile = jnp.dot(own.T, partner, preferred_element_type=jnp.float32) / SAMPLES
            tiles.append(jnp.where(offset >= 0, tile, 0.0).astype(jnp.bfloat16))
        return jnp.stack(tiles)
    ld_upper = lax.map(one_block, jnp.arange(NBLK, dtype=jnp.int32))
    mirrors = []
    for step in range(1, BAND + 1):
        moved = jnp.concatenate([jnp.zeros((step, SLOTS, BLK, BLK), ld_upper.dtype), ld_upper[:-step]], axis=0)
        moved_offsets = jnp.concatenate([jnp.full((step, SLOTS), -1, jnp.int32), pair_offsets[:-step]], axis=0)
        picked = jnp.zeros((NBLK, BLK, BLK), ld_upper.dtype)
        for slot in range(SLOTS):
            picked = jnp.where((moved_offsets[:, slot] == step)[:, None, None], moved[:, slot], picked)
        mirrors.append(jnp.swapaxes(picked, 1, 2))
    ld_mirror = jnp.stack(mirrors, axis=1)
    return (ld_upper, ld_mirror)
```

```python
import functools

import jax
import jax.numpy as jnp
from jax import lax
from jax.experimental import pallas as pl
from jax.experimental.pallas import tpu as pltpu
from jax.sharding import PartitionSpec as P

SLOTS = 3
AXES = ("var", "samp")
F32 = jnp.float32
BF16 = jnp.bfloat16
VMEM = pl.BlockSpec(memory_space=pltpu.VMEM)
SMEM = pl.BlockSpec(memory_space=pltpu.SMEM)


def dot(a, b):
    return jnp.dot(a, b, preferred_element_type=F32)


def standardized(raw, mean, inv):
    return ((raw.astype(F32) - mean) * inv).astype(BF16)


def own_kernel(x_ref, stat_ref, turned_ref, tile_ref, acc):
    step = pl.program_id(0)
    z = standardized(x_ref[...], stat_ref[0:1, :], stat_ref[1:2, :])
    zt = z.T
    turned_ref[...] = zt
    part = dot(zt, z)

    @pl.when(step == 0)
    def _():
        acc[...] = part

    @pl.when(step > 0)
    def _():
        acc[...] += part

    @pl.when(step == pl.num_programs(0) - 1)
    def _():
        tile_ref[...] = acc[...]


def pair_kernel(pos_ref, scale_ref, turned_ref, y_ref, w_ref, ystat_ref, wstat_ref,
                keep_c, send_c, keep_bd, send_bd, acc):
    step = pl.program_id(0)
    last = pl.num_programs(0) - 1
    active = pos_ref[1]
    half = acc.shape[1] // 2

    @pl.when(step == 0)
    def _():
        acc[...] = jnp.zeros_like(acc)

    zt = turned_ref[...]
    w = standardized(w_ref[...], wstat_ref[0:1, :], wstat_ref[1:2, :])
    acc[1] += dot(zt, w)

    @pl.when(active == 1)
    def _():
        y = standardized(y_ref[...], ystat_ref[0:1, :], ystat_ref[1:2, :])
        acc[0] += dot(zt, y)
        acc[2] += dot(y.T, w)

    @pl.when(step == last)
    def _():
        here = pl.multiple_of(pos_ref[0] * half, half)
        there = pl.multiple_of((1 - pos_ref[0]) * half, half)

        def quarters(tile, keep, send):
            scale = scale_ref[tile]
            ours = ((here, here), (here, there), (there, here))
            theirs = ((there, there), (there, here), (here, there))
            for index in range(3):
                for (row, col), out in ((ours[index], keep), (theirs[index], send)):
                    out[index] = acc[tile, pl.ds(row, half), pl.ds(col, half)] * scale

        quarters(1, keep_c.at[0], send_c.at[0])

        @pl.when(active == 1)
        def _():
            quarters(0, keep_bd.at[0], send_bd.at[0])
            quarters(2, keep_bd.at[1], send_bd.at[1])


def strips_kernel(pos_ref, keep_c, got_c, keep_bd, got_bd, own, sib, y_same, y_cross, z_same, z_cross, turn):
    half = keep_c.shape[-1]
    rows = half // 2
    here = pl.multiple_of(pos_ref[0] * half, half)
    there = pl.multiple_of((1 - pos_ref[0]) * half, half)
    mine = pl.multiple_of(pos_ref[2] * rows, rows)
    other = pl.multiple_of((1 - pos_ref[2]) * rows, rows)

    def cut(keep, got, row_out, col_out):
        turn[0, :, pl.ds(here, half)] = keep[0] + got[0]
        turn[0, :, pl.ds(there, half)] = keep[1] + got[1]
        turn[1, :, pl.ds(here, half)] = (keep[0] + got[0]).T
        turn[1, :, pl.ds(there, half)] = (keep[2] + got[2]).T
        for which, outs in ((0, row_out), (1, col_out)):
            for start, out in zip((mine, other), outs):
                out[...] = turn[which, pl.ds(start, rows), :]

    cut(keep_c.at[0], got_c.at[0], (own.at[1], sib.at[1]), (z_same.at[0], z_cross.at[0]))

    @pl.when(pos_ref[1] == 1)
    def _():
        cut(keep_bd.at[0], got_bd.at[0], (own.at[0], sib.at[0]), (y_same.at[0], y_cross.at[0]))
        cut(keep_bd.at[1], got_bd.at[1], (y_same.at[1], y_cross.at[1]), (z_same.at[1], z_cross.at[1]))


def finish_kernel(pos_ref, offsets_ref, diag, own, sib, y_a, y_b, z_same, z_cross, upper, mirror):
    active = pos_ref[1] == 1
    first_core = pos_ref[2] == 0
    even = pos_ref[3] == 0
    count_inv = pos_ref[4]

    def pick(cond, a, b):
        return jnp.where(cond, a, b)

    side = pick(active, y_b[0], y_a[0])
    side_d = pick(active, y_b[1], y_a[1])
    below_c = pick(first_core, z_same[0], z_cross[0])
    above_c = pick(first_core, z_cross[0], z_same[0])
    near_d = pick(first_core == even, z_same[1], z_cross[1])
    held = pick(active, own[0], sib[0]) + side
    far = side_d + near_d
    upper_1 = pick(even, held, far)
    mirror_1 = pick(even, far, held)
    upper_2 = pick(first_core, own[1], sib[1]) + above_c
    mirror_2 = pick(first_core, sib[1], own[1]) + below_c
    mirror[0, 0] = mirror_1.astype(BF16)
    mirror[0, 1] = mirror_2.astype(BF16)
    self_tile = diag[...] * (1.0 / count_inv.astype(F32))
    for slot in range(SLOTS):
        offset = offsets_ref[0, slot]
        tile = pick(offset == 0, self_tile, pick(offset == 1, upper_1, pick(offset == 2, upper_2, 0.0)))
        upper[0, slot] = tile.astype(BF16)


def body(dosage, pair_offsets, live_counts):
    n_var = lax.axis_size("var")
    n_samp = lax.axis_size("samp")
    depth, width = dosage.shape
    half = width // 2
    strip = width // n_samp
    samples_all = depth * n_samp
    v = lax.axis_index("var")
    s = lax.axis_index("samp")
    x, core, odd = s // 2, s % 2, v % 2
    active = (core == odd).astype(jnp.int32)

    def at(var, samp):
        return var * n_samp + samp

    def active_on(var, samp):
        return var % 2 == samp % 2

    everyone = [(var, samp) for var in range(n_var) for samp in range(n_samp)]
    z_same = [(at(a, b), at(a - 2 if b % 2 == 0 else a + 2, b)) for a, b in everyone
              if 0 <= (a - 2 if b % 2 == 0 else a + 2) < n_var]
    y_same = [(at(a, b), at(a ^ 1, b)) for a, b in everyone if not active_on(a, b)]

    def send(value, pairs):
        return lax.ppermute(value, AXES, pairs)

    w_raw = send(dosage, z_same)
    y_raw = send(dosage, y_same)

    values = dosage.astype(F32)
    mean = lax.psum(jnp.sum(values, axis=0), "samp") / samples_all
    centered = values - mean
    spread = lax.psum(jnp.sum(centered * centered, axis=0), "samp") / samples_all
    live = jnp.arange(width, dtype=jnp.int32) < live_counts[0]
    inv = jnp.where(live, lax.rsqrt(spread + 1e-05), 0.0)
    lists = [jnp.any(pair_offsets[0] == step).astype(F32) for step in (1, 2)]
    stat = jnp.stack([mean, inv] + [jnp.full((width,), flag) for flag in lists])
    w_stat = send(stat, z_same)
    y_stat = send(stat, y_same)
    first = core == 0
    scale = jnp.stack([
        jnp.where(first, lists[0], y_stat[2, 0]),
        jnp.where(first, lists[1], w_stat[3, 0]),
        jnp.where(first, y_stat[2, 0], w_stat[2, 0]),
    ]) / samples_all
    pos = jnp.stack([x, active, core, odd, jnp.int32(samples_all)]).astype(jnp.int32)

    step_rows = min(512, depth)
    steps = depth // step_rows
    turned, tile = pl.pallas_call(
        own_kernel,
        grid=(steps,),
        in_specs=[pl.BlockSpec((step_rows, width), lambda k: (k, 0)), pl.BlockSpec((4, width), lambda k: (0, 0))],
        out_specs=[pl.BlockSpec((width, step_rows), lambda k: (0, k)), pl.BlockSpec((width, width), lambda k: (0, 0))],
        out_shape=[jax.ShapeDtypeStruct((width, depth), BF16), jax.ShapeDtypeStruct((width, width), F32)],
        scratch_shapes=[pltpu.VMEM((width, width), F32)],
        compiler_params=pltpu.CompilerParams(vmem_limit_bytes=24 << 20),
        cost_estimate=pl.CostEstimate(flops=2 * depth * width * width, bytes_accessed=4 * depth * width, transcendentals=0),
        name="own_tile",
    )(dosage, stat)
    diag = lax.psum_scatter(tile, "samp", scatter_dimension=0, tiled=True)

    quarter = lambda n: jax.ShapeDtypeStruct((n, 3, half, half), F32)
    whole = lambda n: pl.BlockSpec((n, 3, half, half), lambda k: (0, 0, 0, 0))
    keep_c, send_c, keep_bd, send_bd = pl.pallas_call(
        pair_kernel,
        grid=(steps,),
        in_specs=[SMEM, SMEM, pl.BlockSpec((width, step_rows), lambda k: (0, k)),
                  pl.BlockSpec((step_rows, width), lambda k: (k, 0)), pl.BlockSpec((step_rows, width), lambda k: (k, 0)),
                  pl.BlockSpec((4, width), lambda k: (0, 0)), pl.BlockSpec((4, width), lambda k: (0, 0))],
        out_specs=[whole(1), whole(1), whole(2), whole(2)],
        out_shape=[quarter(1), quarter(1), quarter(2), quarter(2)],
        scratch_shapes=[pltpu.VMEM((3, width, width), F32)],
        compiler_params=pltpu.CompilerParams(vmem_limit_bytes=32 << 20),
        cost_estimate=pl.CostEstimate(flops=6 * depth * width * width, bytes_accessed=6 * depth * width, transcendentals=0),
        name="pair_tiles",
    )(pos, scale, turned, y_raw, w_raw, y_stat, w_stat)

    across = [(at(a, b), at(a, b ^ 2)) for a, b in everyone]
    across_active = [(at(a, b), at(a, b ^ 2)) for a, b in everyone if active_on(a, b)]
    got_c = send(send_c, across)
    got_bd = send(send_bd, across_active)

    two = jax.ShapeDtypeStruct((2, strip, width), F32)
    own, sib, to_y_same, to_y_cross, to_z_same, to_z_cross = pl.pallas_call(
        strips_kernel,
        in_specs=[SMEM] + [VMEM] * 4,
        out_specs=[VMEM] * 6,
        out_shape=[two] * 6,
        scratch_shapes=[pltpu.VMEM((2, half, width), F32)],
        compiler_params=pltpu.CompilerParams(vmem_limit_bytes=24 << 20),
        name="strips",
    )(pos, keep_c, got_c, keep_bd, got_bd)

    got_sib = send(sib, [(at(a, b), at(a, b ^ 1)) for a, b in everyone])
    got_y_same = send(to_y_same, [(at(a, b), at(a ^ 1, b)) for a, b in everyone if active_on(a, b)])
    got_y_cross = send(to_y_cross, [(at(a, b), at(a ^ 1, b ^ 1)) for a, b in everyone if active_on(a, b)])
    z_up_down = [(a, b, a + 2 if b % 2 == 0 else a - 2) for a, b in everyone]
    got_z_same = send(to_z_same, [(at(a, b), at(t, b)) for a, b, t in z_up_down if 0 <= t < n_var])
    got_z_cross = send(to_z_cross, [(at(a, b), at(t, b ^ 1)) for a, b, t in z_up_down if 0 <= t < n_var])

    return pl.pallas_call(
        finish_kernel,
        in_specs=[SMEM, SMEM] + [VMEM] * 7,
        out_specs=[VMEM, VMEM],
        out_shape=[jax.ShapeDtypeStruct((1, SLOTS, strip, width), BF16),
                   jax.ShapeDtypeStruct((1, 2, strip, width), BF16)],
        compiler_params=pltpu.CompilerParams(vmem_limit_bytes=24 << 20),
        name="finish",
    )(pos, pair_offsets, diag, own, got_sib, got_y_same, got_y_cross, got_z_same, got_z_cross)


def solution(mesh):
    in_specs = (P("samp", "var"), P("var", None), P("var"))
    out_specs = (P("var", None, "samp", None), P("var", None, "samp", None))
    return jax.shard_map(body, mesh=mesh, in_specs=in_specs, out_specs=out_specs, check_vma=False)
```

```python
import jax
import jax.numpy as jnp
from jax import lax
from jax.experimental import pallas as pl
from jax.experimental.pallas import tpu as pltpu
from jax.sharding import PartitionSpec as P

SLOTS = 3
AXES = ("var", "samp")
F32 = jnp.float32
BF16 = jnp.bfloat16
VMEM = pl.BlockSpec(memory_space=pltpu.VMEM)
SMEM = pl.BlockSpec(memory_space=pltpu.SMEM)
BIG = pltpu.CompilerParams(vmem_limit_bytes=56 << 20)
D_BLOCKS = {0: [(0, 0)], 1: [(0, 1), (1, 0), (1, 1)]}


def dot(a, b):
    return jnp.dot(a, b, preferred_element_type=F32)


def standardized(raw, stat_ref):
    return ((raw.astype(F32) - stat_ref[0:1, :]) * stat_ref[1:2, :]).astype(BF16)


def stats_kernel(x_ref, out_ref):
    step = pl.program_id(0)
    rows = x_ref.shape[0]
    x = x_ref[...].astype(F32)
    mean = jnp.sum(x, axis=0, keepdims=True) * (1.0 / rows)
    centered = x - mean
    square = jnp.sum(centered * centered, axis=0, keepdims=True)

    @pl.when(step == 0)
    def _():
        out_ref[0:1, :] = mean
        out_ref[1:2, :] = square

    @pl.when(step > 0)
    def _():
        before = step.astype(F32)
        share = 1.0 / (before + 1.0)
        delta = mean - out_ref[0:1, :]
        out_ref[0:1, :] += delta * share
        out_ref[1:2, :] += square + delta * delta * (rows * before * share)


def own_kernel(pos_ref, x_ref, stat_ref, turned_ref, keep_ref, send_ref, acc):
    step = pl.program_id(0)
    z = standardized(x_ref[...], stat_ref)
    zt = z.T
    turned_ref[...] = zt
    part = dot(zt, z)

    @pl.when(step == 0)
    def _():
        acc[...] = part

    @pl.when(step > 0)
    def _():
        acc[...] += part

    @pl.when(step == pl.num_programs(0) - 1)
    def _():
        half = keep_ref.shape[0]
        keep_ref[...] = acc[pl.ds(pl.multiple_of(pos_ref[0] * half, half), half), :]
        send_ref[...] = acc[pl.ds(pl.multiple_of((1 - pos_ref[0]) * half, half), half), :]


def diag_kernel(pos_ref, keep_ref, got_ref, mine_ref, other_ref):
    rows = mine_ref.shape[0]
    for core, out in ((pos_ref[2], mine_ref), (1 - pos_ref[2], other_ref)):
        at = pl.ds(pl.multiple_of(core * rows, rows), rows)
        out[...] = keep_ref[at, :] + got_ref[at, :]


def put_blocks(x, source, base, out_keep, out_send, first, parts):
    size = out_keep.shape[-1]
    for out, near in ((out_keep, x), (out_send, 1 - x)):
        index = first
        for r, h in ((near, near), (near, 1 - near), (1 - near, near)):
            for part in range(parts):
                row = pl.multiple_of(r * parts * size + part * size, size)
                col = pl.multiple_of(base + h * size, size)
                out[index] = source[pl.ds(row, size), pl.ds(col, size)]
                index += 1


def pair_kernel(chunk, *refs):
    (pos_ref, scale_ref, turned_ref, y_ref, w_ref, ystat_ref, wstat_ref), refs = refs[:7], refs[7:]
    if chunk == 0:
        keep_c, send_c, keep_bd, send_bd, yt_out, w_out, acc_b, acc_c, acc_d = refs
    else:
        yt_old, w_old, keep_c, send_c, keep_bd, send_bd, acc_b, acc_c, acc_d, acc_e = refs
    step = pl.program_id(0)
    last = pl.num_programs(0) - 1
    x = pos_ref[0]
    active = pos_ref[1] == 1
    size = keep_c.shape[-1]

    @pl.when(step == 0)
    def _():
        for acc in (acc_b, acc_c, acc_d) + (() if chunk == 0 else (acc_e,)):
            acc[...] = jnp.zeros_like(acc)

    zt = turned_ref[...]
    w = standardized(w_ref[...], wstat_ref)
    acc_c[...] += dot(zt, w)
    if chunk == 0:
        w_out[...] = w

    @pl.when(active)
    def _():
        y = standardized(y_ref[...], ystat_ref)
        yt = y.T
        acc_b[...] += dot(zt, y)
        if chunk == 0:
            yt_out[...] = yt
            acc_d[...] += dot(yt, w)
        else:
            acc_e[...] += dot(yt_old[...], w)
            acc_d[:, :2 * size] += dot(yt, w_old[...])
            acc_d[:, 2 * size:] += dot(yt, w)

    @pl.when(step == last)
    def _():
        acc_c[...] *= scale_ref[1]
        put_blocks(x, acc_c, 0, keep_c, send_c, 0, 2)

        @pl.when(active)
        def _():
            acc_b[...] *= scale_ref[0]
            acc_d[...] *= scale_ref[2]
            put_blocks(x, acc_b, 0, keep_bd, send_bd, 0, 2)
            if chunk == 0:
                put_blocks(x, acc_d, 0, keep_bd, send_bd, 6, 1)
            else:
                acc_e[...] *= scale_ref[2]
                put_blocks(x, acc_e, 0, keep_bd, send_bd, 6, 1)
                put_blocks(x, acc_d, 0, keep_bd, send_bd, 9, 1)
                put_blocks(x, acc_d, 2 * size, keep_bd, send_bd, 12, 1)


def strips_kernel(pos_ref, keep_c0, got_c0, keep_bd0, got_bd0, keep_c1, got_c1, keep_bd1, got_bd1,
                  own, sib, y_same, y_cross, z_same, z_cross):
    size = keep_c0.shape[-1]
    x = pos_ref[0]

    def columns(half, part):
        return pl.ds(pl.multiple_of(half * 2 * size + part * size, size), size)

    def wide(keeps, gots, mine, row_out, col_out):
        for core, rows, cols in ((mine, row_out[0], col_out[0]), (1 - mine, row_out[1], col_out[1])):
            for part in range(2):
                rows[:, columns(x, part)] = keeps[part][core] + gots[part][core]
                rows[:, columns(1 - x, part)] = keeps[part][2 + core] + gots[part][2 + core]
                cols[:, columns(x, part)] = (keeps[core][part] + gots[core][part]).T
                cols[:, columns(1 - x, part)] = (keeps[core][4 + part] + gots[core][4 + part]).T

    def cross(keeps, gots, mine, row_out, col_out):
        def block(a, b, which):
            chunk = max(a, b)
            index = 6 + 3 * D_BLOCKS[chunk].index((a, b)) + which
            return keeps[chunk][index] + gots[chunk][index]

        for core, rows, cols in ((mine, row_out[0], col_out[0]), (1 - mine, row_out[1], col_out[1])):
            for part in range(2):
                rows[:, columns(x, part)] = block(core, part, 0)
                rows[:, columns(1 - x, part)] = block(core, part, 1)
                cols[:, columns(x, part)] = block(part, core, 0).T
                cols[:, columns(1 - x, part)] = block(part, core, 2).T

    for mine in range(2):
        @pl.when(pos_ref[2] == mine)
        def _():
            wide((keep_c0, keep_c1), (got_c0, got_c1), mine, (own.at[1], sib.at[1]), (z_same.at[0], z_cross.at[0]))

            @pl.when(pos_ref[1] == 1)
            def _():
                keeps, gots = (keep_bd0, keep_bd1), (got_bd0, got_bd1)
                wide(keeps, gots, mine, (own.at[0], sib.at[0]), (y_same.at[0], y_cross.at[0]))
                cross(keeps, gots, mine, (y_same.at[1], y_cross.at[1]), (z_same.at[1], z_cross.at[1]))


def finish_kernel(pos_ref, offsets_ref, diag_mine, diag_got, own, sib, y_a, y_b, z_same, z_cross, upper, mirror):
    active = pos_ref[1] == 1
    first_core = pos_ref[2] == 0
    even = pos_ref[3] == 0
    pick = jnp.where
    side = pick(active, y_b[0], y_a[0])
    side_d = pick(active, y_b[1], y_a[1])
    below_c = pick(first_core, z_same[0], z_cross[0])
    above_c = pick(first_core, z_cross[0], z_same[0])
    near_d = pick(first_core == even, z_same[1], z_cross[1])
    held = pick(active, own[0], sib[0]) + side
    far = side_d + near_d
    upper_1 = pick(even, held, far)
    mirror_1 = pick(even, far, held)
    upper_2 = pick(first_core, own[1], sib[1]) + above_c
    mirror_2 = pick(first_core, sib[1], own[1]) + below_c
    mirror[0, 0] = mirror_1.astype(BF16)
    mirror[0, 1] = mirror_2.astype(BF16)
    self_tile = (diag_mine[...] + diag_got[...]) * (1.0 / pos_ref[4].astype(F32))
    for slot in range(SLOTS):
        offset = offsets_ref[0, slot]
        tile = pick(offset == 0, self_tile, pick(offset == 1, upper_1, pick(offset == 2, upper_2, 0.0)))
        upper[0, slot] = tile.astype(BF16)


def body(dosage, pair_offsets, live_counts):
    n_var = lax.axis_size("var")
    n_samp = lax.axis_size("samp")
    depth, width = dosage.shape
    half = width // 2
    strip = width // n_samp
    samples_all = depth * n_samp
    v = lax.axis_index("var")
    s = lax.axis_index("samp")
    x, core, odd = s // 2, s % 2, v % 2
    active = (core == odd).astype(jnp.int32)

    def at(var, samp):
        return var * n_samp + samp

    def active_on(var, samp):
        return var % 2 == samp % 2

    everyone = [(var, samp) for var in range(n_var) for samp in range(n_samp)]
    z_main = [(at(a, b), at(a - 2 if b % 2 == 0 else a + 2, b)) for a, b in everyone
              if 0 <= (a - 2 if b % 2 == 0 else a + 2) < n_var]
    y_main = [(at(a, b), at(a ^ 1, b)) for a, b in everyone if not active_on(a, b)]
    across = [(at(a, b), at(a, b ^ 2)) for a, b in everyone]
    across_active = [(at(a, b), at(a, b ^ 2)) for a, b in everyone if active_on(a, b)]
    sibling = [(at(a, b), at(a, b ^ 1)) for a, b in everyone]

    def send(value, pairs):
        return lax.ppermute(value, AXES, pairs)

    chunks = []
    for part in range(2):
        pieces = [dosage[:, h * half + part * strip:h * half + (part + 1) * strip] for h in range(2)]
        chunks.append(jnp.concatenate(pieces, axis=1))
    w_raw = [send(chunk, z_main) for chunk in chunks]
    y_raw = [send(chunk, y_main) for chunk in chunks]

    step_rows = min(512, depth)
    local = pl.pallas_call(
        stats_kernel,
        grid=(depth // step_rows,),
        in_specs=[pl.BlockSpec((step_rows, width), lambda k: (k, 0))],
        out_specs=pl.BlockSpec((2, width), lambda k: (0, 0)),
        out_shape=jax.ShapeDtypeStruct((2, width), F32),
        compiler_params=BIG,
        cost_estimate=pl.CostEstimate(flops=5 * depth * width, bytes_accessed=2 * depth * width, transcendentals=0),
        name="local_stats",
    )(dosage)
    mask = (jnp.arange(n_samp) == s).astype(F32)
    gathered = lax.psum(mask[:, None, None] * local[None], "samp")
    mean = jnp.sum(gathered[:, 0], axis=0) * (1.0 / n_samp)
    between = jnp.sum(jnp.square(gathered[:, 0] - mean), axis=0) * depth
    spread = (jnp.sum(gathered[:, 1], axis=0) + between) / samples_all
    live = jnp.arange(width, dtype=jnp.int32) < live_counts[0]
    inv = jnp.where(live, lax.rsqrt(spread + 1e-05), 0.0)
    lists = [jnp.any(pair_offsets[0] == step).astype(F32) for step in (1, 2)]
    stat = jnp.stack([mean, inv] + [jnp.full((width,), flag) for flag in lists])
    z_step = [(a, b, a + 2 if b % 2 == 0 else a - 2) for a, b in everyone]
    z_cross = [(at(a, b), at(t, b ^ 1)) for a, b, t in z_step if 0 <= t < n_var]
    y_cross = [(at(a, b), at(a ^ 1, b ^ 1)) for a, b in everyone if active_on(a, b)]
    w_stat, y_stat = send(stat, z_cross), send(stat, y_cross)

    first = core == 0
    scale = jnp.stack([
        jnp.where(first, lists[0], y_stat[2, 0]),
        jnp.where(first, lists[1], w_stat[3, 0]),
        jnp.where(first, y_stat[2, 0], w_stat[2, 0]),
    ]) / samples_all
    pos = jnp.stack([x, active, core, odd, jnp.int32(samples_all)]).astype(jnp.int32)

    def by_chunk(table):
        perm = [h * half + part * strip for part in range(2) for h in range(2)]
        return [jnp.concatenate([table[:, at:at + strip] for at in perm[2 * part:2 * part + 2]], axis=1)
                for part in range(2)]

    w_stats, y_stats = by_chunk(w_stat), by_chunk(y_stat)

    turned, diag_keep, diag_send = pl.pallas_call(
        own_kernel,
        grid=(depth // step_rows,),
        in_specs=[SMEM, pl.BlockSpec((step_rows, width), lambda k: (k, 0)), pl.BlockSpec((4, width), lambda k: (0, 0))],
        out_specs=[pl.BlockSpec((width, step_rows), lambda k: (0, k))]
        + [pl.BlockSpec((half, width), lambda k: (0, 0))] * 2,
        out_shape=[jax.ShapeDtypeStruct((width, depth), BF16)] + [jax.ShapeDtypeStruct((half, width), F32)] * 2,
        scratch_shapes=[pltpu.VMEM((width, width), F32)],
        compiler_params=BIG,
        cost_estimate=pl.CostEstimate(flops=2 * depth * width * width, bytes_accessed=4 * depth * width, transcendentals=0),
        name="own_tile",
    )(pos, dosage, stat)
    diag_across = send(diag_send, across)
    pair_rows = min(1024, depth)
    steps = depth // pair_rows
    blocks = lambda n: jax.ShapeDtypeStruct((n, strip, strip), F32)
    whole = lambda *shape: pl.BlockSpec(shape, lambda k: (0,) * len(shape))
    tall = pl.BlockSpec((pair_rows, half), lambda k: (k, 0))
    flat = lambda rows: pl.BlockSpec((rows, pair_rows), lambda k: (0, k))
    keeps, arrived, passed, before = [], [], [], [diag_across]
    for part in range(2):
        n_bd = 6 + 3 * len(D_BLOCKS[part])
        in_specs = [SMEM, SMEM, flat(width), tall, tall, whole(4, half), whole(4, half)]
        out_specs = [whole(6, strip, strip)] * 2 + [whole(n_bd, strip, strip)] * 2
        out_shape = [blocks(6)] * 2 + [blocks(n_bd)] * 2
        scratch = [pltpu.VMEM((width, half), F32)] * 2
        if part == 0:
            out_specs += [flat(half), tall]
            out_shape += [jax.ShapeDtypeStruct((half, depth), BF16), jax.ShapeDtypeStruct((depth, half), BF16)]
            scratch += [pltpu.VMEM((half, half), F32)]
        else:
            in_specs += [flat(half), tall]
            scratch += [pltpu.VMEM((half, width), F32), pltpu.VMEM((half, half), F32)]
        keep_c, send_c, keep_bd, send_bd, *passed = pl.pallas_call(
            lambda *refs, part=part: pair_kernel(part, *refs),
            grid=(steps,),
            in_specs=in_specs,
            out_specs=out_specs,
            out_shape=out_shape,
            scratch_shapes=scratch,
            compiler_params=BIG,
            cost_estimate=pl.CostEstimate(flops=3 * depth * width * width, bytes_accessed=4 * depth * width, transcendentals=0),
            name=f"pair_tiles_{part}",
        )(pos, scale, turned, y_raw[part], w_raw[part], y_stats[part], w_stats[part], *passed)
        send_bd, send_c, *before = lax.optimization_barrier((send_bd, send_c, *before))
        arrived += before
        before = [send(send_bd, across_active), send(send_c, across)]
        keeps.append((keep_bd, keep_c))
    arrived += before

    diag_mine, diag_other = pl.pallas_call(
        diag_kernel,
        in_specs=[SMEM, VMEM, VMEM],
        out_specs=[VMEM, VMEM],
        out_shape=[jax.ShapeDtypeStruct((strip, width), F32)] * 2,
        name="diag_strips",
    )(pos, diag_keep, arrived[0])
    diag_got = send(diag_other, sibling)

    held = []
    for part, (keep_bd, keep_c) in enumerate(keeps):
        held += [keep_c, arrived[2 + 2 * part], keep_bd, arrived[1 + 2 * part]]
    two = jax.ShapeDtypeStruct((2, strip, width), F32)
    own, sib, to_y_same, to_y_cross, to_z_same, to_z_cross = pl.pallas_call(
        strips_kernel,
        in_specs=[SMEM] + [VMEM] * 8,
        out_specs=[VMEM] * 6,
        out_shape=[two] * 6,
        name="strips",
    )(pos, *held)

    got_z_cross = send(to_z_cross, z_cross)
    got_z_same = send(to_z_same, [(at(a, b), at(t, b)) for a, b, t in z_step if 0 <= t < n_var])
    got_y_same = send(to_y_same, [(at(a, b), at(a ^ 1, b)) for a, b in everyone if active_on(a, b)])
    got_y_cross = send(to_y_cross, y_cross)
    got_sib = send(sib, sibling)

    return pl.pallas_call(
        finish_kernel,
        in_specs=[SMEM, SMEM] + [VMEM] * 8,
        out_specs=[VMEM, VMEM],
        out_shape=[jax.ShapeDtypeStruct((1, SLOTS, strip, width), BF16),
                   jax.ShapeDtypeStruct((1, 2, strip, width), BF16)],
        name="finish",
    )(pos, pair_offsets, diag_mine, diag_got, own, got_sib, got_y_same, got_y_cross, got_z_same, got_z_cross)


def solution(mesh):
    in_specs = (P("samp", "var"), P("var", None), P("var"))
    out_specs = (P("var", None, "samp", None), P("var", None, "samp", None))
    return jax.shard_map(body, mesh=mesh, in_specs=in_specs, out_specs=out_specs, check_vma=False)
```

```python
import jax
import jax.numpy as jnp
from jax import lax
from jax.experimental import pallas as pl
from jax.experimental.pallas import tpu as pltpu
from jax.sharding import PartitionSpec as P

SLOTS = 3
AXES = ("var", "samp")
F32 = jnp.float32
BF16 = jnp.bfloat16
VMEM = pl.BlockSpec(memory_space=pltpu.VMEM)
SMEM = pl.BlockSpec(memory_space=pltpu.SMEM)
BIG = pltpu.CompilerParams(vmem_limit_bytes=56 << 20)
D_BLOCKS = {0: [(0, 0)], 1: [(0, 1), (1, 0), (1, 1)]}


def dot(a, b):
    return jnp.dot(a, b, preferred_element_type=F32)


def standardized(raw, stat_ref):
    return ((raw.astype(F32) - stat_ref[0:1, :]) * stat_ref[1:2, :]).astype(BF16)


def first_kernel(steps, pos_ref, x_ref, chunk_0, chunk_1, out_ref, center, total, square):
    step = pl.program_id(0)
    rows, width = x_ref.shape
    strip = chunk_0.shape[1] // 2
    group = min(64, rows)
    for part, out in enumerate((chunk_0, chunk_1)):
        for half in range(2):
            start = (2 * half + part) * strip
            out[:, half * strip:(half + 1) * strip] = x_ref[:, start:start + strip]

    @pl.when(step == 0)
    def _():
        center[...] = jnp.mean(x_ref[:group, :].astype(F32), axis=0, keepdims=True)
        total[...] = jnp.zeros_like(total)
        square[...] = jnp.zeros_like(square)

    middle = center[...]

    def add(i, sums):
        x = x_ref[pl.ds(pl.multiple_of(i * group, group), group), :].astype(F32) - middle
        x = x.reshape(group // 8, 8, width)
        return sums[0] + jnp.sum(x, axis=0), sums[1] + jnp.sum(x * x, axis=0)

    sums = lax.fori_loop(0, rows // group, add, (total[...], square[...]))
    total[...], square[...] = sums

    @pl.when(step == pl.num_programs(0) - 1)
    def _():
        count = float(rows * steps)
        shift = jnp.sum(total[...], axis=0, keepdims=True) * (1.0 / count)
        around = jnp.sum(square[...], axis=0, keepdims=True) - shift * shift * count
        row = lax.broadcasted_iota(jnp.int32, out_ref.shape, 0)
        groups = out_ref.shape[0] // 2
        out_ref[...] = jnp.where(row == pos_ref[5], middle + shift,
                                 jnp.where(row == pos_ref[5] + groups, jnp.maximum(around, 0.0), 0.0))


def stat_kernel(pos_ref, live_ref, offsets_ref, gathered_ref, plain_ref, chunked_ref):
    groups, width = gathered_ref.shape[0] // 2, gathered_ref.shape[1]
    strip = width // 4
    means = gathered_ref[0:groups, :]
    samples = pos_ref[4].astype(F32)
    mean = jnp.sum(means, axis=0, keepdims=True) * (1.0 / groups)
    between = jnp.sum(jnp.square(means - mean), axis=0, keepdims=True) * (samples * (1.0 / groups))
    spread = (jnp.sum(gathered_ref[groups:, :], axis=0, keepdims=True) + between) / samples
    live = lax.broadcasted_iota(jnp.int32, (1, width), 1) < live_ref[0]
    plain_ref[0:1, :] = mean
    plain_ref[1:2, :] = jnp.where(live, lax.rsqrt(spread + 1e-05), 0.0)
    for step in (1, 2):
        listed = offsets_ref[0, 0] == step
        for slot in range(1, SLOTS):
            listed = jnp.logical_or(listed, offsets_ref[0, slot] == step)
        plain_ref[1 + step:2 + step, :] = jnp.full((1, width), jnp.where(listed, 1.0, 0.0), F32)
    for part in range(2):
        for half in range(2):
            start, to = (2 * half + part) * strip, (2 * part + half) * strip
            chunked_ref[:, to:to + strip] = plain_ref[:, start:start + strip]


def own_kernel(pos_ref, x_ref, stat_ref, turned_ref, keep_ref, send_ref, acc):
    step = pl.program_id(0)
    z = standardized(x_ref[...], stat_ref)
    zt = z.T
    turned_ref[...] = zt
    part = dot(zt, z)

    @pl.when(step == 0)
    def _():
        acc[...] = part

    @pl.when(step > 0)
    def _():
        acc[...] += part

    @pl.when(step == pl.num_programs(0) - 1)
    def _():
        half = keep_ref.shape[0]
        keep_ref[...] = acc[pl.ds(pl.multiple_of(pos_ref[0] * half, half), half), :]
        send_ref[...] = acc[pl.ds(pl.multiple_of((1 - pos_ref[0]) * half, half), half), :]


def diag_kernel(pos_ref, keep_ref, got_ref, mine_ref, other_ref):
    rows = mine_ref.shape[0]
    for core, out in ((pos_ref[2], mine_ref), (1 - pos_ref[2], other_ref)):
        at = pl.ds(pl.multiple_of(core * rows, rows), rows)
        out[...] = keep_ref[at, :] + got_ref[at, :]


def put_blocks(x, source, base, out_keep, out_send, first, parts):
    size = out_keep.shape[-1]
    for out, near in ((out_keep, x), (out_send, 1 - x)):
        index = first
        for r, h in ((near, near), (near, 1 - near), (1 - near, near)):
            for part in range(parts):
                row = pl.multiple_of(r * parts * size + part * size, size)
                col = pl.multiple_of(base + h * size, size)
                out[index] = source[pl.ds(row, size), pl.ds(col, size)]
                index += 1


def pair_kernel(chunk, *refs):
    (pos_ref, turned_ref, y_ref, w_ref, stat_ref, ystat_ref, wstat_ref), refs = refs[:7], refs[7:]
    if chunk == 0:
        keep_c, send_c, keep_bd, send_bd, yt_out, w_out, acc_b, acc_c, acc_d = refs
    else:
        yt_old, w_old, keep_c, send_c, keep_bd, send_bd, acc_b, acc_c, acc_d, acc_e = refs
    step = pl.program_id(0)
    last = pl.num_programs(0) - 1
    x = pos_ref[0]
    active = pos_ref[1] == 1
    size = keep_c.shape[-1]

    @pl.when(step == 0)
    def _():
        for acc in (acc_b, acc_c, acc_d) + (() if chunk == 0 else (acc_e,)):
            acc[...] = jnp.zeros_like(acc)

    zt = turned_ref[...]
    w = standardized(w_ref[...], wstat_ref)
    acc_c[...] += dot(zt, w)
    if chunk == 0:
        w_out[...] = w

    @pl.when(active)
    def _():
        y = standardized(y_ref[...], ystat_ref)
        yt = y.T
        acc_b[...] += dot(zt, y)
        if chunk == 0:
            yt_out[...] = yt
            acc_d[...] += dot(yt, w)
        else:
            acc_e[...] += dot(yt_old[...], w)
            acc_d[:, :2 * size] += dot(yt, w_old[...])
            acc_d[:, 2 * size:] += dot(yt, w)

    @pl.when(step == last)
    def _():
        first = pos_ref[2] == 0
        share = 1.0 / pos_ref[4].astype(F32)
        acc_c[...] *= jnp.where(first, stat_ref[3:4, :], wstat_ref[3:4, :]) * share
        put_blocks(x, acc_c, 0, keep_c, send_c, 0, 2)

        @pl.when(active)
        def _():
            acc_b[...] *= jnp.where(first, stat_ref[2:3, :], ystat_ref[2:3, :]) * share
            put_blocks(x, acc_b, 0, keep_bd, send_bd, 0, 2)
            scale = jnp.where(first, ystat_ref[2:3, :], wstat_ref[2:3, :]) * share
            acc_d[:, :2 * size] *= scale
            if chunk == 0:
                put_blocks(x, acc_d, 0, keep_bd, send_bd, 6, 1)
            else:
                acc_d[:, 2 * size:] *= scale
                acc_e[...] *= scale
                put_blocks(x, acc_e, 0, keep_bd, send_bd, 6, 1)
                put_blocks(x, acc_d, 0, keep_bd, send_bd, 9, 1)
                put_blocks(x, acc_d, 2 * size, keep_bd, send_bd, 12, 1)


def strips_kernel(pos_ref, keep_c0, got_c0, keep_bd0, got_bd0, keep_c1, got_c1, keep_bd1, got_bd1,
                  own, sib, y_same, y_cross, z_same, z_cross):
    size = keep_c0.shape[-1]
    x = pos_ref[0]

    def columns(half, part):
        return pl.ds(pl.multiple_of(half * 2 * size + part * size, size), size)

    def wide(keeps, gots, mine, row_out, col_out):
        for core, rows, cols in ((mine, row_out[0], col_out[0]), (1 - mine, row_out[1], col_out[1])):
            for part in range(2):
                rows[:, columns(x, part)] = keeps[part][core] + gots[part][core]
                rows[:, columns(1 - x, part)] = keeps[part][2 + core] + gots[part][2 + core]
                cols[:, columns(x, part)] = (keeps[core][part] + gots[core][part]).T
                cols[:, columns(1 - x, part)] = (keeps[core][4 + part] + gots[core][4 + part]).T

    def cross(keeps, gots, mine, row_out, col_out):
        def block(a, b, which):
            chunk = max(a, b)
            index = 6 + 3 * D_BLOCKS[chunk].index((a, b)) + which
            return keeps[chunk][index] + gots[chunk][index]

        for core, rows, cols in ((mine, row_out[0], col_out[0]), (1 - mine, row_out[1], col_out[1])):
            for part in range(2):
                rows[:, columns(x, part)] = block(core, part, 0)
                rows[:, columns(1 - x, part)] = block(core, part, 1)
                cols[:, columns(x, part)] = block(part, core, 0).T
                cols[:, columns(1 - x, part)] = block(part, core, 2).T

    for mine in range(2):
        @pl.when(pos_ref[2] == mine)
        def _():
            wide((keep_c0, keep_c1), (got_c0, got_c1), mine, (own.at[1], sib.at[1]), (z_same.at[0], z_cross.at[0]))

            @pl.when(pos_ref[1] == 1)
            def _():
                keeps, gots = (keep_bd0, keep_bd1), (got_bd0, got_bd1)
                wide(keeps, gots, mine, (own.at[0], sib.at[0]), (y_same.at[0], y_cross.at[0]))
                cross(keeps, gots, mine, (y_same.at[1], y_cross.at[1]), (z_same.at[1], z_cross.at[1]))


def finish_kernel(pos_ref, offsets_ref, diag_mine, diag_got, own, sib, y_a, y_b, z_same, z_cross, upper, mirror):
    active = pos_ref[1] == 1
    first_core = pos_ref[2] == 0
    even = pos_ref[3] == 0
    pick = jnp.where
    side = pick(active, y_b[0], y_a[0])
    side_d = pick(active, y_b[1], y_a[1])
    below_c = pick(first_core, z_same[0], z_cross[0])
    above_c = pick(first_core, z_cross[0], z_same[0])
    near_d = pick(first_core == even, z_same[1], z_cross[1])
    held = pick(active, own[0], sib[0]) + side
    far = side_d + near_d
    upper_1 = pick(even, held, far)
    mirror_1 = pick(even, far, held)
    upper_2 = pick(first_core, own[1], sib[1]) + above_c
    mirror_2 = pick(first_core, sib[1], own[1]) + below_c
    mirror[0, 0] = mirror_1.astype(BF16)
    mirror[0, 1] = mirror_2.astype(BF16)
    self_tile = (diag_mine[...] + diag_got[...]) * (1.0 / pos_ref[4].astype(F32))
    for slot in range(SLOTS):
        offset = offsets_ref[0, slot]
        tile = pick(offset == 0, self_tile, pick(offset == 1, upper_1, pick(offset == 2, upper_2, 0.0)))
        upper[0, slot] = tile.astype(BF16)


def body(dosage, pair_offsets, live_counts):
    n_var = lax.axis_size("var")
    n_samp = lax.axis_size("samp")
    depth, width = dosage.shape
    half = width // 2
    strip = width // n_samp
    samples_all = depth * n_samp
    v = lax.axis_index("var")
    s = lax.axis_index("samp")
    x, core, odd = s // 2, s % 2, v % 2
    active = (core == odd).astype(jnp.int32)

    def at(var, samp):
        return var * n_samp + samp

    def active_on(var, samp):
        return var % 2 == samp % 2

    everyone = [(var, samp) for var in range(n_var) for samp in range(n_samp)]
    z_main = [(at(a, b), at(a - 2 if b % 2 == 0 else a + 2, b)) for a, b in everyone
              if 0 <= (a - 2 if b % 2 == 0 else a + 2) < n_var]
    y_main = [(at(a, b), at(a ^ 1, b)) for a, b in everyone if not active_on(a, b)]
    across = [(at(a, b), at(a, b ^ 2)) for a, b in everyone]
    across_active = [(at(a, b), at(a, b ^ 2)) for a, b in everyone if active_on(a, b)]
    sibling = [(at(a, b), at(a, b ^ 1)) for a, b in everyone]

    def send(value, pairs):
        return lax.ppermute(value, AXES, pairs)

    pos = jnp.stack([x, active, core, odd, jnp.int32(samples_all), s]).astype(jnp.int32)
    step_rows = min(1024, depth)
    steps = depth // step_rows
    tall = pl.BlockSpec((step_rows, half), lambda k: (k, 0))
    wide = pl.BlockSpec((step_rows, width), lambda k: (k, 0))
    flat = lambda rows: pl.BlockSpec((rows, step_rows), lambda k: (0, k))
    whole = lambda *shape: pl.BlockSpec(shape, lambda k: (0,) * len(shape))

    chunk_0, chunk_1, local = pl.pallas_call(
        lambda *refs: first_kernel(steps, *refs),
        grid=(steps,),
        in_specs=[SMEM, wide],
        out_specs=[tall, tall, whole(2 * n_samp, width)],
        out_shape=[jax.ShapeDtypeStruct((depth, half), BF16)] * 2 + [jax.ShapeDtypeStruct((2 * n_samp, width), F32)],
        scratch_shapes=[pltpu.VMEM((1, width), F32)] + [pltpu.VMEM((8, width), F32)] * 2,
        compiler_params=BIG,
        cost_estimate=pl.CostEstimate(flops=5 * depth * width, bytes_accessed=4 * depth * width, transcendentals=0),
        name="chunks_and_local_stats",
    )(pos, dosage)
    w_raw, y_raw = [send(chunk_0, z_main)], [send(chunk_0, y_main)]
    gathered = lax.psum(local, "samp")
    gathered, chunk_1 = lax.optimization_barrier((gathered, chunk_1))
    w_raw.append(send(chunk_1, z_main))
    y_raw.append(send(chunk_1, y_main))
    stat, stat_chunked = pl.pallas_call(
        stat_kernel,
        in_specs=[SMEM, SMEM, SMEM, VMEM],
        out_specs=[VMEM, VMEM],
        out_shape=[jax.ShapeDtypeStruct((4, width), F32)] * 2,
        name="stats",
    )(pos, live_counts, pair_offsets, gathered)
    z_step = [(a, b, a + 2 if b % 2 == 0 else a - 2) for a, b in everyone]
    z_cross = [(at(a, b), at(t, b ^ 1)) for a, b, t in z_step if 0 <= t < n_var]
    y_cross = [(at(a, b), at(a ^ 1, b ^ 1)) for a, b in everyone if active_on(a, b)]
    w_stat, y_stat = send(stat_chunked, z_cross), send(stat_chunked, y_cross)

    turned, diag_keep, diag_send = pl.pallas_call(
        own_kernel,
        grid=(steps,),
        in_specs=[SMEM, wide, whole(4, width)],
        out_specs=[flat(width)] + [whole(half, width)] * 2,
        out_shape=[jax.ShapeDtypeStruct((width, depth), BF16)] + [jax.ShapeDtypeStruct((half, width), F32)] * 2,
        scratch_shapes=[pltpu.VMEM((width, width), F32)],
        compiler_params=BIG,
        cost_estimate=pl.CostEstimate(flops=2 * depth * width * width, bytes_accessed=4 * depth * width, transcendentals=0),
        name="own_tile",
    )(pos, dosage, stat)
    diag_across = send(diag_send, across)
    blocks = lambda n: jax.ShapeDtypeStruct((n, strip, strip), F32)
    keeps, arrived, passed, before = [], [], [], [diag_across]
    for part in range(2):
        n_bd = 6 + 3 * len(D_BLOCKS[part])
        in_specs = [SMEM, flat(width), tall, tall] + [pl.BlockSpec((4, half), lambda k, part=part: (0, part))] * 3
        out_specs = [whole(6, strip, strip)] * 2 + [whole(n_bd, strip, strip)] * 2
        out_shape = [blocks(6)] * 2 + [blocks(n_bd)] * 2
        scratch = [pltpu.VMEM((width, half), F32)] * 2
        if part == 0:
            out_specs += [flat(half), tall]
            out_shape += [jax.ShapeDtypeStruct((half, depth), BF16), jax.ShapeDtypeStruct((depth, half), BF16)]
            scratch += [pltpu.VMEM((half, half), F32)]
        else:
            in_specs += [flat(half), tall]
            scratch += [pltpu.VMEM((half, width), F32), pltpu.VMEM((half, half), F32)]
        keep_c, send_c, keep_bd, send_bd, *passed = pl.pallas_call(
            lambda *refs, part=part: pair_kernel(part, *refs),
            grid=(steps,),
            in_specs=in_specs,
            out_specs=out_specs,
            out_shape=out_shape,
            scratch_shapes=scratch,
            compiler_params=BIG,
            cost_estimate=pl.CostEstimate(flops=3 * depth * width * width, bytes_accessed=4 * depth * width, transcendentals=0),
            name=f"pair_tiles_{part}",
        )(pos, turned, y_raw[part], w_raw[part], stat_chunked, y_stat, w_stat, *passed)
        send_bd, send_c, *before = lax.optimization_barrier((send_bd, send_c, *before))
        arrived += before
        before = [send(send_bd, across_active), send(send_c, across)]
        keeps.append((keep_bd, keep_c))
    arrived += before

    diag_mine, diag_other = pl.pallas_call(
        diag_kernel,
        in_specs=[SMEM, VMEM, VMEM],
        out_specs=[VMEM, VMEM],
        out_shape=[jax.ShapeDtypeStruct((strip, width), F32)] * 2,
        name="diag_strips",
    )(pos, diag_keep, arrived[0])
    diag_got = send(diag_other, sibling)

    held = []
    for part, (keep_bd, keep_c) in enumerate(keeps):
        held += [keep_c, arrived[2 + 2 * part], keep_bd, arrived[1 + 2 * part]]
    two = jax.ShapeDtypeStruct((2, strip, width), F32)
    own, sib, to_y_same, to_y_cross, to_z_same, to_z_cross = pl.pallas_call(
        strips_kernel,
        in_specs=[SMEM] + [VMEM] * 8,
        out_specs=[VMEM] * 6,
        out_shape=[two] * 6,
        name="strips",
    )(pos, *held)

    got_z_cross = send(to_z_cross, z_cross)
    got_z_same = send(to_z_same, [(at(a, b), at(t, b)) for a, b, t in z_step if 0 <= t < n_var])
    got_y_same = send(to_y_same, [(at(a, b), at(a ^ 1, b)) for a, b in everyone if active_on(a, b)])
    got_y_cross = send(to_y_cross, y_cross)
    got_sib = send(sib, sibling)

    return pl.pallas_call(
        finish_kernel,
        in_specs=[SMEM, SMEM] + [VMEM] * 8,
        out_specs=[VMEM, VMEM],
        out_shape=[jax.ShapeDtypeStruct((1, SLOTS, strip, width), BF16),
                   jax.ShapeDtypeStruct((1, 2, strip, width), BF16)],
        name="finish",
    )(pos, pair_offsets, diag_mine, diag_got, own, got_sib, got_y_same, got_y_cross, got_z_same, got_z_cross)


def solution(mesh):
    in_specs = (P("samp", "var"), P("var", None), P("var"))
    out_specs = (P("var", None, "samp", None), P("var", None, "samp", None))
    return jax.shard_map(body, mesh=mesh, in_specs=in_specs, out_specs=out_specs, check_vma=False)
```

```python
import jax
import jax.numpy as jnp
from jax import lax
from jax.experimental import pallas as pl
from jax.experimental.pallas import tpu as pltpu
from jax.sharding import PartitionSpec as P

SLOTS = 3
AXES = ("var", "samp")
F32 = jnp.float32
BF16 = jnp.bfloat16
VMEM = pl.BlockSpec(memory_space=pltpu.VMEM)
SMEM = pl.BlockSpec(memory_space=pltpu.SMEM)
BIG = pltpu.CompilerParams(vmem_limit_bytes=56 << 20)
D_BLOCKS = {0: [(0, 0)], 1: [(0, 1), (1, 0), (1, 1)]}


def dot(a, b):
    return jnp.dot(a, b, preferred_element_type=F32)


def standardized(raw, stat_ref):
    return ((raw.astype(F32) - stat_ref[0:1, :]) * stat_ref[1:2, :]).astype(BF16)


def first_kernel(steps, x_ref, chunk_0, chunk_1, out_ref, center, total, square):
    step = pl.program_id(0)
    rows, width = x_ref.shape
    strip = chunk_0.shape[1] // 2
    group = min(64, rows)
    for part, out in enumerate((chunk_0, chunk_1)):
        for half in range(2):
            start = (2 * half + part) * strip
            out[:, half * strip:(half + 1) * strip] = x_ref[:, start:start + strip]

    @pl.when(step == 0)
    def _():
        center[...] = jnp.mean(x_ref[:group, :].astype(F32), axis=0, keepdims=True)
        total[...] = jnp.zeros_like(total)
        square[...] = jnp.zeros_like(square)

    middle = center[...]

    def add(i, sums):
        x = x_ref[pl.ds(pl.multiple_of(i * group, group), group), :].astype(F32) - middle
        x = x.reshape(group // 8, 8, width)
        return sums[0] + jnp.sum(x, axis=0), sums[1] + jnp.sum(x * x, axis=0)

    sums = lax.fori_loop(0, rows // group, add, (total[...], square[...]))
    total[...], square[...] = sums

    @pl.when(step == pl.num_programs(0) - 1)
    def _():
        count = float(rows * steps)
        shift = jnp.sum(total[...], axis=0, keepdims=True) * (1.0 / count)
        around = jnp.sum(square[...], axis=0, keepdims=True) - shift * shift * count
        out_ref[0:1, :] = middle + shift
        out_ref[1:2, :] = jnp.maximum(around, 0.0)


def stat_kernel(pos_ref, live_ref, offsets_ref, own_ref, sib_ref, far_ref, cross_ref, plain_ref, chunked_ref):
    width = own_ref.shape[1]
    strip = width // 4
    samples = pos_ref[4].astype(F32)

    def merged(values):
        return (values[0] + values[1]) + (values[2] + values[3])

    groups = (own_ref, sib_ref, far_ref, cross_ref)
    mean = merged([ref[0:1, :] for ref in groups]) * 0.25
    between = merged([jnp.square(ref[0:1, :] - mean) for ref in groups]) * (samples * 0.25)
    spread = (merged([ref[1:2, :] for ref in groups]) + between) / samples
    live = lax.broadcasted_iota(jnp.int32, (1, width), 1) < live_ref[0]
    plain_ref[0:1, :] = mean
    plain_ref[1:2, :] = jnp.where(live, lax.rsqrt(spread + 1e-05), 0.0)
    for step in (1, 2):
        listed = offsets_ref[0, 0] == step
        for slot in range(1, SLOTS):
            listed = jnp.logical_or(listed, offsets_ref[0, slot] == step)
        plain_ref[1 + step:2 + step, :] = jnp.full((1, width), jnp.where(listed, 1.0, 0.0), F32)
    for part in range(2):
        for half in range(2):
            start, to = (2 * half + part) * strip, (2 * part + half) * strip
            chunked_ref[:, to:to + strip] = plain_ref[:, start:start + strip]


def own_kernel(pos_ref, x_ref, stat_ref, turned_ref, keep_ref, send_ref, acc):
    step = pl.program_id(0)
    z = standardized(x_ref[...], stat_ref)
    zt = z.T
    turned_ref[...] = zt
    part = dot(zt, z)

    @pl.when(step == 0)
    def _():
        acc[...] = part

    @pl.when(step > 0)
    def _():
        acc[...] += part

    @pl.when(step == pl.num_programs(0) - 1)
    def _():
        half = keep_ref.shape[0]
        keep_ref[...] = acc[pl.ds(pl.multiple_of(pos_ref[0] * half, half), half), :]
        send_ref[...] = acc[pl.ds(pl.multiple_of((1 - pos_ref[0]) * half, half), half), :]


def put_blocks(x, source, base, out_keep, out_send, first, parts):
    size = out_keep.shape[-1]
    for out, near in ((out_keep, x), (out_send, 1 - x)):
        index = first
        for r, h in ((near, near), (near, 1 - near), (1 - near, near)):
            for part in range(parts):
                row = pl.multiple_of(r * parts * size + part * size, size)
                col = pl.multiple_of(base + h * size, size)
                out[index] = source[pl.ds(row, size), pl.ds(col, size)].astype(out.dtype)
                index += 1


def pair_kernel(chunk, *refs):
    (pos_ref, turned_ref, y_ref, w_ref, stat_ref, ystat_ref, wstat_ref), refs = refs[:7], refs[7:]
    if chunk == 0:
        keep_c, send_c, keep_bd, send_bd, yt_out, w_out, acc_b, acc_c, acc_d = refs
    else:
        yt_old, w_old, keep_c, send_c, keep_bd, send_bd, acc_b, acc_c, acc_d, acc_e = refs
    step = pl.program_id(0)
    last = pl.num_programs(0) - 1
    x = pos_ref[0]
    active = pos_ref[1] == 1
    size = keep_c.shape[-1]

    @pl.when(step == 0)
    def _():
        for acc in (acc_b, acc_c, acc_d) + (() if chunk == 0 else (acc_e,)):
            acc[...] = jnp.zeros_like(acc)

    zt = turned_ref[...]
    w = standardized(w_ref[...], wstat_ref)
    acc_c[...] += dot(zt, w)
    if chunk == 0:
        w_out[...] = w

    @pl.when(active)
    def _():
        y = standardized(y_ref[...], ystat_ref)
        yt = y.T
        acc_b[...] += dot(zt, y)
        if chunk == 0:
            yt_out[...] = yt
            acc_d[...] += dot(yt, w)
        else:
            acc_e[...] += dot(yt_old[...], w)
            acc_d[:, :2 * size] += dot(yt, w_old[...])
            acc_d[:, 2 * size:] += dot(yt, w)

    @pl.when(step == last)
    def _():
        first = pos_ref[2] == 0
        share = 1.0 / pos_ref[4].astype(F32)
        acc_c[...] *= jnp.where(first, stat_ref[3:4, :], wstat_ref[3:4, :]) * share
        put_blocks(x, acc_c, 0, keep_c, send_c, 0, 2)

        @pl.when(active)
        def _():
            acc_b[...] *= jnp.where(first, stat_ref[2:3, :], ystat_ref[2:3, :]) * share
            put_blocks(x, acc_b, 0, keep_bd, send_bd, 0, 2)
            scale = jnp.where(first, ystat_ref[2:3, :], wstat_ref[2:3, :]) * share
            acc_d[:, :2 * size] *= scale
            if chunk == 0:
                put_blocks(x, acc_d, 0, keep_bd, send_bd, 6, 1)
            else:
                acc_d[:, 2 * size:] *= scale
                acc_e[...] *= scale
                put_blocks(x, acc_e, 0, keep_bd, send_bd, 6, 1)
                put_blocks(x, acc_d, 0, keep_bd, send_bd, 9, 1)
                put_blocks(x, acc_d, 2 * size, keep_bd, send_bd, 12, 1)


def strips_kernel(chunk, pos_ref, keep_c, got_c, keep_bd, got_bd, held_b, held_c, to_y, to_z):
    size = keep_c.shape[-1]
    x = pos_ref[0]

    def at(half, part):
        return pl.ds(pl.multiple_of(half * 2 * size + part * size, size), size)

    def summed(keep, got, index):
        return keep[index] + got[index].astype(F32)

    def side(keep, got, held, out):
        for core in range(2):
            for first, half in ((0, x), (2, 1 - x)):
                held[core, :, pl.ds(pl.multiple_of(half * size, size), size)] = summed(keep, got, first + core)
            for first, half in ((0, x), (4, 1 - x)):
                out[:, at(half, core)] = summed(keep, got, first + core).T.astype(out.dtype)

    side(keep_c, got_c, held_c, to_z)

    @pl.when(pos_ref[1] == 1)
    def _():
        side(keep_bd, got_bd, held_b, to_y)
        for index in range(len(D_BLOCKS[chunk])):
            near, right, below = [summed(keep_bd, got_bd, 6 + 3 * index + which) for which in range(3)]
            start = (4 + 2 * index) * size
            to_y[:, start:start + size] = near.astype(to_y.dtype)
            to_y[:, start + size:start + 2 * size] = right.astype(to_y.dtype)
            to_z[:, start:start + size] = near.T.astype(to_z.dtype)
            to_z[:, start + size:start + 2 * size] = below.T.astype(to_z.dtype)


def combine_kernel(pos_ref, held_b0, held_c0, held_b1, held_c1, y_0, z_0, y_1, z_1, diag_keep, diag_got, mine, sib):
    size = held_b0.shape[1]
    x = pos_ref[0]
    active = pos_ref[1]

    def at(half, part):
        return pl.ds(pl.multiple_of(half * 2 * size + part * size, size), size)

    def fill(core, out):
        def total(index, helds, side):
            for part, held in enumerate(helds):
                for half in range(2):
                    cols = slice((2 * half + part) * size, (2 * half + part + 1) * size)
                    out[index, :, cols] = (held[core, :, half * size:(half + 1) * size] + side[:, cols].astype(F32))

        def far(pieces, sides):
            for part in range(2):
                block = pieces(part)
                chunk = max(block)
                start = (4 + 2 * D_BLOCKS[chunk].index(block)) * size
                out[2, :, at(x, part)] = sides[chunk][:, start:start + size].astype(F32)
                out[2, :, at(1 - x, part)] = sides[chunk][:, start + size:start + 2 * size].astype(F32)

        total(1, (held_c0, held_c1), (z_0, z_1)[core])

        @pl.when(active == 1)
        def _():
            total(0, (held_b0, held_b1), (y_0, y_1)[core])
            far(lambda part: (core, part), (y_0, y_1))

        @pl.when(active == 0)
        def _():
            far(lambda part: (part, core), (z_0, z_1))

        rows = slice(core * size, (core + 1) * size)
        out[3] = diag_keep[rows, :] + diag_got[rows, :]

    for core in range(2):
        @pl.when(pos_ref[2] == core)
        def _():
            fill(core, mine)
            fill(1 - core, sib)


def finish_kernel(pos_ref, offsets_ref, mine, sib, upper, mirror):
    active = pos_ref[1] == 1
    first_core = pos_ref[2] == 0
    even = pos_ref[3] == 0
    pick = jnp.where
    near = pick(active, mine[0], sib[0])
    far = mine[2] + sib[2]
    upper_1 = pick(even, near, far)
    upper_2 = pick(first_core, mine[1], sib[1])
    mirror[0, 0] = pick(even, far, near).astype(BF16)
    mirror[0, 1] = pick(first_core, sib[1], mine[1]).astype(BF16)
    self_tile = (mine[3] + sib[3]) * (1.0 / pos_ref[4].astype(F32))
    for slot in range(SLOTS):
        offset = offsets_ref[0, slot]
        tile = pick(offset == 0, self_tile, pick(offset == 1, upper_1, pick(offset == 2, upper_2, 0.0)))
        upper[0, slot] = tile.astype(BF16)


def body(dosage, pair_offsets, live_counts):
    n_var = lax.axis_size("var")
    n_samp = lax.axis_size("samp")
    depth, width = dosage.shape
    half = width // 2
    strip = width // n_samp
    samples_all = depth * n_samp
    v = lax.axis_index("var")
    s = lax.axis_index("samp")
    x, core, odd = s // 2, s % 2, v % 2
    active = (core == odd).astype(jnp.int32)

    def at(var, samp):
        return var * n_samp + samp

    def active_on(var, samp):
        return var % 2 == samp % 2

    everyone = [(var, samp) for var in range(n_var) for samp in range(n_samp)]
    z_main = [(at(a, b), at(a - 2 if b % 2 == 0 else a + 2, b)) for a, b in everyone
              if 0 <= (a - 2 if b % 2 == 0 else a + 2) < n_var]
    y_main = [(at(a, b), at(a ^ 1, b)) for a, b in everyone if not active_on(a, b)]
    across = [(at(a, b), at(a, b ^ 2)) for a, b in everyone]
    across_active = [(at(a, b), at(a, b ^ 2)) for a, b in everyone if active_on(a, b)]
    sibling = [(at(a, b), at(a, b ^ 1)) for a, b in everyone]

    def send(value, pairs):
        return lax.ppermute(value, AXES, pairs)

    pos = jnp.stack([x, active, core, odd, jnp.int32(samples_all), s]).astype(jnp.int32)
    step_rows = min(1024, depth)
    steps = depth // step_rows
    tall = pl.BlockSpec((step_rows, half), lambda k: (k, 0))
    wide = pl.BlockSpec((step_rows, width), lambda k: (k, 0))
    flat = lambda rows: pl.BlockSpec((rows, step_rows), lambda k: (0, k))
    whole = lambda *shape: pl.BlockSpec(shape, lambda k: (0,) * len(shape))

    chunk_0, chunk_1, local = pl.pallas_call(
        lambda *refs: first_kernel(steps, *refs),
        grid=(steps,),
        in_specs=[wide],
        out_specs=[tall, tall, whole(2, width)],
        out_shape=[jax.ShapeDtypeStruct((depth, half), BF16)] * 2 + [jax.ShapeDtypeStruct((2, width), F32)],
        scratch_shapes=[pltpu.VMEM((1, width), F32)] + [pltpu.VMEM((8, width), F32)] * 2,
        compiler_params=BIG,
        cost_estimate=pl.CostEstimate(flops=5 * depth * width, bytes_accessed=4 * depth * width, transcendentals=0),
        name="chunks_and_local_stats",
    )(dosage)
    w_raw, y_raw = [send(chunk_0, z_main)], [send(chunk_0, y_main)]
    others = [send(local, [(at(a, b), at(a, b ^ flip)) for a, b in everyone]) for flip in (1, 2, 3)]
    stat, stat_chunked = pl.pallas_call(
        stat_kernel,
        in_specs=[SMEM, SMEM, SMEM] + [VMEM] * 4,
        out_specs=[VMEM, VMEM],
        out_shape=[jax.ShapeDtypeStruct((4, width), F32)] * 2,
        name="stats",
    )(pos, live_counts, pair_offsets, local, *others)
    stat, chunk_1 = lax.optimization_barrier((stat, chunk_1))
    w_raw.append(send(chunk_1, z_main))
    y_raw.append(send(chunk_1, y_main))
    z_step = [(a, b, a + 2 if b % 2 == 0 else a - 2) for a, b in everyone]
    z_cross = [(at(a, b), at(t, b ^ 1)) for a, b, t in z_step if 0 <= t < n_var]
    y_cross = [(at(a, b), at(a ^ 1, b ^ 1)) for a, b in everyone if active_on(a, b)]
    w_stat, y_stat = send(stat_chunked, z_cross), send(stat_chunked, y_cross)

    turned, diag_keep, diag_send = pl.pallas_call(
        own_kernel,
        grid=(steps,),
        in_specs=[SMEM, wide, whole(4, width)],
        out_specs=[flat(width)] + [whole(half, width)] * 2,
        out_shape=[jax.ShapeDtypeStruct((width, depth), BF16)] + [jax.ShapeDtypeStruct((half, width), F32)] * 2,
        scratch_shapes=[pltpu.VMEM((width, width), F32)],
        compiler_params=BIG,
        cost_estimate=pl.CostEstimate(flops=2 * depth * width * width, bytes_accessed=4 * depth * width, transcendentals=0),
        name="own_tile",
    )(pos, dosage, stat)
    diag_across = send(diag_send, across)
    keeps, arrived, passed, before = [], [], [], [diag_across]
    sent_as = (F32, BF16)
    for part in range(2):
        n_bd = 6 + 3 * len(D_BLOCKS[part])
        in_specs = [SMEM, flat(width), tall, tall] + [pl.BlockSpec((4, half), lambda k, part=part: (0, part))] * 3
        out_specs = [whole(6, strip, strip)] * 2 + [whole(n_bd, strip, strip)] * 2
        out_shape = [jax.ShapeDtypeStruct((n, strip, strip), kind) for n in (6, n_bd) for kind in (F32, sent_as[part])]
        scratch = [pltpu.VMEM((width, half), F32)] * 2
        if part == 0:
            out_specs += [flat(half), tall]
            out_shape += [jax.ShapeDtypeStruct((half, depth), BF16), jax.ShapeDtypeStruct((depth, half), BF16)]
            scratch += [pltpu.VMEM((half, half), F32)]
        else:
            in_specs += [flat(half), tall]
            scratch += [pltpu.VMEM((half, width), F32), pltpu.VMEM((half, half), F32)]
        keep_c, send_c, keep_bd, send_bd, *passed = pl.pallas_call(
            lambda *refs, part=part: pair_kernel(part, *refs),
            grid=(steps,),
            in_specs=in_specs,
            out_specs=out_specs,
            out_shape=out_shape,
            scratch_shapes=scratch,
            compiler_params=BIG,
            cost_estimate=pl.CostEstimate(flops=3 * depth * width * width, bytes_accessed=4 * depth * width, transcendentals=0),
            name=f"pair_tiles_{part}",
        )(pos, turned, y_raw[part], w_raw[part], stat_chunked, y_stat, w_stat, *passed)
        send_bd, send_c, *before = lax.optimization_barrier((send_bd, send_c, *before))
        arrived += before
        before = [send(send_bd, across_active), send(send_c, across)]
        keeps.append((keep_bd, keep_c))
    arrived += before

    held, sides = [], []
    for part, (keep_bd, keep_c) in enumerate(keeps):
        sent = jax.ShapeDtypeStruct((strip, width + half * len(D_BLOCKS[part])), sent_as[part])
        held_b, held_c, to_y, to_z = pl.pallas_call(
            lambda *refs, part=part: strips_kernel(part, *refs),
            in_specs=[SMEM] + [VMEM] * 4,
            out_specs=[VMEM] * 4,
            out_shape=[jax.ShapeDtypeStruct((2, strip, half), F32)] * 2 + [sent] * 2,
            name=f"strips_{part}",
        )(pos, keep_c, arrived[2 + 2 * part], keep_bd, arrived[1 + 2 * part])
        held += [held_b, held_c]
        sides += [send(to_y, y_cross), send(to_z, z_cross)]

    four = jax.ShapeDtypeStruct((4, strip, width), F32)
    mine, sib = pl.pallas_call(
        combine_kernel,
        in_specs=[SMEM] + [VMEM] * 10,
        out_specs=[VMEM] * 2,
        out_shape=[four] * 2,
        name="combine",
    )(pos, *held, *sides, diag_keep, arrived[0])

    return pl.pallas_call(
        finish_kernel,
        in_specs=[SMEM, SMEM, VMEM, VMEM],
        out_specs=[VMEM, VMEM],
        out_shape=[jax.ShapeDtypeStruct((1, SLOTS, strip, width), BF16),
                   jax.ShapeDtypeStruct((1, 2, strip, width), BF16)],
        name="finish",
    )(pos, pair_offsets, mine, send(sib, sibling))


def solution(mesh):
    in_specs = (P("samp", "var"), P("var", None), P("var"))
    out_specs = (P("var", None, "samp", None), P("var", None, "samp", None))
    return jax.shard_map(body, mesh=mesh, in_specs=in_specs, out_specs=out_specs, check_vma=False)
```

```python
import jax
import jax.numpy as jnp
from jax import lax
from jax.experimental import pallas as pl
from jax.experimental.pallas import tpu as pltpu
from jax.sharding import PartitionSpec as P

SLOTS = 3
AXES = ("var", "samp")
F32 = jnp.float32
BF16 = jnp.bfloat16
VMEM = pl.BlockSpec(memory_space=pltpu.VMEM)
SMEM = pl.BlockSpec(memory_space=pltpu.SMEM)
SOME = pltpu.CompilerParams(vmem_limit_bytes=24 << 20)
MOST = pltpu.CompilerParams(vmem_limit_bytes=58 << 20)
D_BLOCKS = {0: [(0, 0)], 1: [(0, 1), (1, 0), (1, 1)]}


def dot(a, b):
    return jnp.dot(a, b, preferred_element_type=F32)


def standardized(raw, stat_ref):
    return ((raw.astype(F32) - stat_ref[0:1, :]) * stat_ref[1:2, :]).astype(BF16)


def cut_kernel(x_ref, out_ref, sems):
    strip = out_ref.shape[1] // 2
    copies = [pltpu.make_async_copy(x_ref.at[:, pl.ds(2 * half * strip, strip)],
                                    out_ref.at[:, pl.ds(half * strip, strip)], sems.at[half]) for half in range(2)]
    for copy in copies:
        copy.start()
    for copy in copies:
        copy.wait()


def first_kernel(steps, x_ref, upper_ref, lower_ref, out_ref, center, total, square):
    step = pl.program_id(0)
    rows, width = x_ref.shape
    strip = upper_ref.shape[1] // 2
    group = min(64, rows)
    for first, out in ((True, upper_ref), (False, lower_ref)):
        @pl.when((step < steps // 2) == first)
        def _():
            for half in range(2):
                start = (2 * half + 1) * strip
                out[:, half * strip:(half + 1) * strip] = x_ref[:, start:start + strip]

    @pl.when(step == 0)
    def _():
        center[...] = jnp.mean(x_ref[:group, :].astype(F32), axis=0, keepdims=True)
        total[...] = jnp.zeros_like(total)
        square[...] = jnp.zeros_like(square)

    middle = center[...]

    def add(i, sums):
        x = x_ref[pl.ds(pl.multiple_of(i * group, group), group), :].astype(F32) - middle
        x = x.reshape(group // 8, 8, width)
        return sums[0] + jnp.sum(x, axis=0), sums[1] + jnp.sum(x * x, axis=0)

    sums = lax.fori_loop(0, rows // group, add, (total[...], square[...]))
    total[...], square[...] = sums

    @pl.when(step == pl.num_programs(0) - 1)
    def _():
        count = float(rows * steps)
        shift = jnp.sum(total[...], axis=0, keepdims=True) * (1.0 / count)
        around = jnp.sum(square[...], axis=0, keepdims=True) - shift * shift * count
        out_ref[0:1, :] = middle + shift
        out_ref[1:2, :] = jnp.maximum(around, 0.0)


def stat_kernel(pos_ref, live_ref, offsets_ref, own_ref, sib_ref, far_ref, cross_ref, plain_ref, chunked_ref):
    width = own_ref.shape[1]
    strip = width // 4
    samples = pos_ref[4].astype(F32)

    def merged(values):
        return (values[0] + values[1]) + (values[2] + values[3])

    groups = (own_ref, sib_ref, far_ref, cross_ref)
    mean = merged([ref[0:1, :] for ref in groups]) * 0.25
    between = merged([jnp.square(ref[0:1, :] - mean) for ref in groups]) * (samples * 0.25)
    spread = (merged([ref[1:2, :] for ref in groups]) + between) / samples
    live = lax.broadcasted_iota(jnp.int32, (1, width), 1) < live_ref[0]
    plain_ref[0:1, :] = mean
    plain_ref[1:2, :] = jnp.where(live, lax.rsqrt(spread + 1e-05), 0.0)
    for step in (1, 2):
        listed = offsets_ref[0, 0] == step
        for slot in range(1, SLOTS):
            listed = jnp.logical_or(listed, offsets_ref[0, slot] == step)
        plain_ref[1 + step:2 + step, :] = jnp.full((1, width), jnp.where(listed, 1.0, 0.0), F32)
    for part in range(2):
        for half in range(2):
            start, to = (2 * half + part) * strip, (2 * part + half) * strip
            chunked_ref[:, to:to + strip] = plain_ref[:, start:start + strip]


def own_kernel(pos_ref, x_ref, stat_ref, turned_ref, keep_ref, send_ref, acc):
    step = pl.program_id(0)
    z = standardized(x_ref[...], stat_ref)
    zt = z.T
    turned_ref[...] = zt
    part = dot(zt, z)

    @pl.when(step == 0)
    def _():
        acc[...] = part

    @pl.when(step > 0)
    def _():
        acc[...] += part

    @pl.when(step == pl.num_programs(0) - 1)
    def _():
        half = keep_ref.shape[0]
        keep_ref[...] = acc[pl.ds(pl.multiple_of(pos_ref[0] * half, half), half), :]
        send_ref[...] = acc[pl.ds(pl.multiple_of((1 - pos_ref[0]) * half, half), half), :]


def put_blocks(x, source, base, out_keep, out_send, first, parts):
    size = out_keep.shape[-1]
    for out, near in ((out_keep, x), (out_send, 1 - x)):
        index = first
        for r, h in ((near, near), (near, 1 - near), (1 - near, near)):
            for part in range(parts):
                row = pl.multiple_of(r * parts * size + part * size, size)
                col = pl.multiple_of(base + h * size, size)
                out[index] = source[pl.ds(row, size), pl.ds(col, size)].astype(out.dtype)
                index += 1


def pair_kernel(stage, *refs):
    (pos_ref, turned_ref, y_ref, w_ref, stat_ref, ystat_ref, wstat_ref), refs = refs[:7], refs[7:]
    if stage == 0:
        (keep_c, send_c, keep_bd, send_bd, yt_out, w_out), accs = refs[:6], refs[6:]
    elif stage == 1:
        (yt_old, w_old), accs = refs[:2], refs[2:]
    else:
        (yt_old, w_old), olds, (keep_c, send_c, keep_bd, send_bd), accs = refs[:2], refs[2:6], refs[6:10], refs[10:]
    acc_b, acc_c, acc_d = accs[:3]
    step = pl.program_id(0)
    last = pl.num_programs(0) - 1
    x = pos_ref[0]
    active = pos_ref[1] == 1
    size = y_ref.shape[1] // 2

    @pl.when(step == 0)
    def _():
        for index, acc in enumerate(accs):
            acc[...] = olds[index][...] if stage == 2 else jnp.zeros_like(acc)

    zt = turned_ref[...]
    w = standardized(w_ref[...], wstat_ref)
    acc_c[...] += dot(zt, w)
    if stage == 0:
        w_out[...] = w

    @pl.when(active)
    def _():
        y = standardized(y_ref[...], ystat_ref)
        yt = y.T
        acc_b[...] += dot(zt, y)
        if stage == 0:
            yt_out[...] = yt
            acc_d[...] += dot(yt, w)
        else:
            accs[3][...] += dot(yt_old[...], w)
            acc_d[:, :2 * size] += dot(yt, w_old[...])
            acc_d[:, 2 * size:] += dot(yt, w)

    if stage == 1:
        return

    @pl.when(step == last)
    def _():
        first = pos_ref[2] == 0
        share = 1.0 / pos_ref[4].astype(F32)
        acc_c[...] *= jnp.where(first, stat_ref[3:4, :], wstat_ref[3:4, :]) * share
        put_blocks(x, acc_c, 0, keep_c, send_c, 0, 2)

        @pl.when(active)
        def _():
            acc_b[...] *= jnp.where(first, stat_ref[2:3, :], ystat_ref[2:3, :]) * share
            put_blocks(x, acc_b, 0, keep_bd, send_bd, 0, 2)
            scale = jnp.where(first, ystat_ref[2:3, :], wstat_ref[2:3, :]) * share
            acc_d[:, :2 * size] *= scale
            if stage == 0:
                put_blocks(x, acc_d, 0, keep_bd, send_bd, 6, 1)
            else:
                acc_e = accs[3]
                acc_d[:, 2 * size:] *= scale
                acc_e[...] *= scale
                put_blocks(x, acc_e, 0, keep_bd, send_bd, 6, 1)
                put_blocks(x, acc_d, 0, keep_bd, send_bd, 9, 1)
                put_blocks(x, acc_d, 2 * size, keep_bd, send_bd, 12, 1)


def strips_kernel(chunk, pos_ref, keep_c, got_c, keep_bd, got_bd, held_b, held_c, to_y, to_z):
    size = keep_c.shape[-1]
    x = pos_ref[0]

    def at(half, part):
        return pl.ds(pl.multiple_of(half * 2 * size + part * size, size), size)

    def summed(keep, got, index):
        return keep[index] + got[index].astype(F32)

    def side(keep, got, held, out):
        for core in range(2):
            for first, half in ((0, x), (2, 1 - x)):
                held[core, :, pl.ds(pl.multiple_of(half * size, size), size)] = summed(keep, got, first + core)
            for first, half in ((0, x), (4, 1 - x)):
                out[:, at(half, core)] = summed(keep, got, first + core).T.astype(out.dtype)

    side(keep_c, got_c, held_c, to_z)

    @pl.when(pos_ref[1] == 1)
    def _():
        side(keep_bd, got_bd, held_b, to_y)
        for index in range(len(D_BLOCKS[chunk])):
            near, right, below = [summed(keep_bd, got_bd, 6 + 3 * index + which) for which in range(3)]
            start = (4 + 2 * index) * size
            to_y[:, start:start + size] = near.astype(to_y.dtype)
            to_y[:, start + size:start + 2 * size] = right.astype(to_y.dtype)
            to_z[:, start:start + size] = near.T.astype(to_z.dtype)
            to_z[:, start + size:start + 2 * size] = below.T.astype(to_z.dtype)


def combine_kernel(pos_ref, held_b0, held_c0, held_b1, held_c1, y_0, z_0, y_1, z_1, diag_keep, diag_got, mine, sib):
    size = held_b0.shape[1]
    x = pos_ref[0]
    active = pos_ref[1]

    def at(half, part):
        return pl.ds(pl.multiple_of(half * 2 * size + part * size, size), size)

    def fill(core, out):
        def total(index, helds, side):
            for part, held in enumerate(helds):
                for half in range(2):
                    cols = slice((2 * half + part) * size, (2 * half + part + 1) * size)
                    out[index, :, cols] = (held[core, :, half * size:(half + 1) * size] + side[:, cols].astype(F32))

        def far(pieces, sides):
            for part in range(2):
                block = pieces(part)
                chunk = max(block)
                start = (4 + 2 * D_BLOCKS[chunk].index(block)) * size
                out[2, :, at(x, part)] = sides[chunk][:, start:start + size].astype(F32)
                out[2, :, at(1 - x, part)] = sides[chunk][:, start + size:start + 2 * size].astype(F32)

        total(1, (held_c0, held_c1), (z_0, z_1)[core])

        @pl.when(active == 1)
        def _():
            total(0, (held_b0, held_b1), (y_0, y_1)[core])
            far(lambda part: (core, part), (y_0, y_1))

        @pl.when(active == 0)
        def _():
            far(lambda part: (part, core), (z_0, z_1))

        rows = slice(core * size, (core + 1) * size)
        out[3] = diag_keep[rows, :] + diag_got[rows, :]

    for core in range(2):
        @pl.when(pos_ref[2] == core)
        def _():
            fill(core, mine)
            fill(1 - core, sib)


def finish_kernel(pos_ref, offsets_ref, mine, sib, upper, mirror):
    active = pos_ref[1] == 1
    first_core = pos_ref[2] == 0
    even = pos_ref[3] == 0
    pick = jnp.where
    near = pick(active, mine[0], sib[0])
    far = mine[2] + sib[2]
    upper_1 = pick(even, near, far)
    upper_2 = pick(first_core, mine[1], sib[1])
    mirror[0, 0] = pick(even, far, near).astype(BF16)
    mirror[0, 1] = pick(first_core, sib[1], mine[1]).astype(BF16)
    self_tile = (mine[3] + sib[3]) * (1.0 / pos_ref[4].astype(F32))
    for slot in range(SLOTS):
        offset = offsets_ref[0, slot]
        tile = pick(offset == 0, self_tile, pick(offset == 1, upper_1, pick(offset == 2, upper_2, 0.0)))
        upper[0, slot] = tile.astype(BF16)


def body(dosage, pair_offsets, live_counts):
    n_var = lax.axis_size("var")
    n_samp = lax.axis_size("samp")
    depth, width = dosage.shape
    half = width // 2
    strip = width // n_samp
    samples_all = depth * n_samp
    v = lax.axis_index("var")
    s = lax.axis_index("samp")
    x, core, odd = s // 2, s % 2, v % 2
    active = (core == odd).astype(jnp.int32)

    def at(var, samp):
        return var * n_samp + samp

    def active_on(var, samp):
        return var % 2 == samp % 2

    everyone = [(var, samp) for var in range(n_var) for samp in range(n_samp)]
    z_main = [(at(a, b), at(a - 2 if b % 2 == 0 else a + 2, b)) for a, b in everyone
              if 0 <= (a - 2 if b % 2 == 0 else a + 2) < n_var]
    y_main = [(at(a, b), at(a ^ 1, b)) for a, b in everyone if not active_on(a, b)]
    across = [(at(a, b), at(a, b ^ 2)) for a, b in everyone]
    across_active = [(at(a, b), at(a, b ^ 2)) for a, b in everyone if active_on(a, b)]
    sibling = [(at(a, b), at(a, b ^ 1)) for a, b in everyone]

    def send(value, pairs):
        return lax.ppermute(value, AXES, pairs)

    pos = jnp.stack([x, active, core, odd, jnp.int32(samples_all), s]).astype(jnp.int32)
    step_rows = min(1024, depth)
    steps = depth // step_rows
    tall = pl.BlockSpec((step_rows, half), lambda k: (k, 0))
    wide = pl.BlockSpec((step_rows, width), lambda k: (k, 0))
    flat = lambda rows: pl.BlockSpec((rows, step_rows), lambda k: (0, k))
    whole = lambda *shape: pl.BlockSpec(shape, lambda k: (0,) * len(shape))

    chunk_0 = pl.pallas_call(
        cut_kernel,
        in_specs=[pl.BlockSpec(memory_space=pl.ANY)],
        out_specs=pl.BlockSpec(memory_space=pl.ANY),
        out_shape=jax.ShapeDtypeStruct((depth, half), BF16),
        scratch_shapes=[pltpu.SemaphoreType.DMA((2,))],
        compiler_params=MOST,
        name="first_chunk",
    )(dosage)
    w_raw, y_raw = [send(chunk_0, z_main)], [send(chunk_0, y_main)]
    dosage, chunk_0 = lax.optimization_barrier((dosage, chunk_0))
    *pieces, local = pl.pallas_call(
        lambda *refs: first_kernel(steps, *refs),
        grid=(steps,),
        in_specs=[wide],
        out_specs=[pl.BlockSpec((step_rows, half), lambda k: (jnp.minimum(k, steps // 2 - 1), 0)),
                   pl.BlockSpec((step_rows, half), lambda k: (jnp.maximum(k - steps // 2, 0), 0)), whole(2, width)],
        out_shape=[jax.ShapeDtypeStruct((depth // 2, half), BF16)] * 2 + [jax.ShapeDtypeStruct((2, width), F32)],
        scratch_shapes=[pltpu.VMEM((1, width), F32)] + [pltpu.VMEM((8, width), F32)] * 2,
        compiler_params=SOME,
        cost_estimate=pl.CostEstimate(flops=5 * depth * width, bytes_accessed=3 * depth * width, transcendentals=0),
        name="second_chunk_and_local_stats",
    )(dosage)
    others = [send(local, [(at(a, b), at(a, b ^ flip)) for a, b in everyone]) for flip in (1, 2, 3)]
    stat, stat_chunked = pl.pallas_call(
        stat_kernel,
        in_specs=[SMEM, SMEM, SMEM] + [VMEM] * 4,
        out_specs=[VMEM, VMEM],
        out_shape=[jax.ShapeDtypeStruct((4, width), F32)] * 2,
        name="stats",
    )(pos, live_counts, pair_offsets, local, *others)
    z_step = [(a, b, a + 2 if b % 2 == 0 else a - 2) for a, b in everyone]
    z_cross = [(at(a, b), at(t, b ^ 1)) for a, b, t in z_step if 0 <= t < n_var]
    y_cross = [(at(a, b), at(a ^ 1, b ^ 1)) for a, b in everyone if active_on(a, b)]
    w_stat, y_stat = send(stat_chunked, z_cross), send(stat_chunked, y_cross)

    turned, diag_keep, diag_send = pl.pallas_call(
        own_kernel,
        grid=(steps,),
        in_specs=[SMEM, wide, whole(4, width)],
        out_specs=[flat(width)] + [whole(half, width)] * 2,
        out_shape=[jax.ShapeDtypeStruct((width, depth), BF16)] + [jax.ShapeDtypeStruct((half, width), F32)] * 2,
        scratch_shapes=[pltpu.VMEM((width, width), F32)],
        compiler_params=SOME,
        cost_estimate=pl.CostEstimate(flops=2 * depth * width * width, bytes_accessed=4 * depth * width, transcendentals=0),
        name="own_tile",
    )(pos, dosage, stat)
    turned, w_stat, y_stat, *pieces = lax.optimization_barrier((turned, w_stat, y_stat, *pieces))
    for piece in pieces:
        w_raw.append(send(piece, z_main))
        y_raw.append(send(piece, y_main))
    diag_across = send(diag_send, across)
    keeps, arrived, passed, before = [], [], [], [diag_across]
    sent_as = (F32, BF16)
    for stage in range(3):
        part = min(stage, 1)
        here = steps if stage == 0 else steps // 2
        skip = steps // 2 if stage == 2 else 0
        lower = lambda rows, skip=skip: pl.BlockSpec((rows, step_rows), lambda k: (0, k + skip))
        n_bd = 6 + 3 * len(D_BLOCKS[part])
        in_specs = [SMEM, lower(width), tall, tall] + [pl.BlockSpec((4, half), lambda k, part=part: (0, part))] * 3
        sums = [(width, half), (width, half), (half, half if stage == 0 else width)] + [(half, half)] * part
        out_specs, out_shape, scratch = [], [], []
        if stage > 0:
            in_specs += [lower(half), pl.BlockSpec((step_rows, half), lambda k, skip=skip: (k + skip, 0))]
        if stage == 2:
            in_specs += [whole(*shape) for shape in sums]
        if stage != 1:
            out_specs += [whole(n, strip, strip) for n in (6, 6, n_bd, n_bd)]
            out_shape += [jax.ShapeDtypeStruct((n, strip, strip), kind) for n in (6, n_bd) for kind in (F32, sent_as[part])]
            scratch += [pltpu.VMEM(shape, F32) for shape in sums]
        else:
            out_specs += [whole(*shape) for shape in sums]
            out_shape += [jax.ShapeDtypeStruct(shape, F32) for shape in sums]
        if stage == 0:
            out_specs += [flat(half), tall]
            out_shape += [jax.ShapeDtypeStruct((half, depth), BF16), jax.ShapeDtypeStruct((depth, half), BF16)]
        results = pl.pallas_call(
            lambda *refs, stage=stage: pair_kernel(stage, *refs),
            grid=(here,),
            in_specs=in_specs,
            out_specs=out_specs,
            out_shape=out_shape,
            scratch_shapes=scratch,
            compiler_params=SOME,
            cost_estimate=pl.CostEstimate(flops=3 * depth * width * width * here // steps, bytes_accessed=4 * depth * width * here // steps, transcendentals=0),
            name=f"pair_tiles_{stage}",
        )(pos, turned, y_raw[stage], w_raw[stage], stat_chunked, y_stat, w_stat, *passed)
        if stage == 1:
            passed = [*passed, *results]
            continue
        keep_c, send_c, keep_bd, send_bd, *passed = results
        send_bd, send_c, *before = lax.optimization_barrier((send_bd, send_c, *before))
        arrived += before
        before = [send(send_bd, across_active), send(send_c, across)]
        keeps.append((keep_bd, keep_c))
    arrived += before

    held, sides = [], []
    for part, (keep_bd, keep_c) in enumerate(keeps):
        sent = jax.ShapeDtypeStruct((strip, width + half * len(D_BLOCKS[part])), sent_as[part])
        held_b, held_c, to_y, to_z = pl.pallas_call(
            lambda *refs, part=part: strips_kernel(part, *refs),
            in_specs=[SMEM] + [VMEM] * 4,
            out_specs=[VMEM] * 4,
            out_shape=[jax.ShapeDtypeStruct((2, strip, half), F32)] * 2 + [sent] * 2,
            name=f"strips_{part}",
        )(pos, keep_c, arrived[2 + 2 * part], keep_bd, arrived[1 + 2 * part])
        held += [held_b, held_c]
        sides += [send(to_y, y_cross), send(to_z, z_cross)]

    four = jax.ShapeDtypeStruct((4, strip, width), F32)
    mine, sib = pl.pallas_call(
        combine_kernel,
        in_specs=[SMEM] + [VMEM] * 10,
        out_specs=[VMEM] * 2,
        out_shape=[four] * 2,
        name="combine",
    )(pos, *held, *sides, diag_keep, arrived[0])

    return pl.pallas_call(
        finish_kernel,
        in_specs=[SMEM, SMEM, VMEM, VMEM],
        out_specs=[VMEM, VMEM],
        out_shape=[jax.ShapeDtypeStruct((1, SLOTS, strip, width), BF16),
                   jax.ShapeDtypeStruct((1, 2, strip, width), BF16)],
        name="finish",
    )(pos, pair_offsets, mine, send(sib, sibling))


def solution(mesh):
    in_specs = (P("samp", "var"), P("var", None), P("var"))
    out_specs = (P("var", None, "samp", None), P("var", None, "samp", None))
    return jax.shard_map(body, mesh=mesh, in_specs=in_specs, out_specs=out_specs, check_vma=False)
```

```python
import jax
import jax.numpy as jnp
from jax import lax
from jax.experimental import pallas as pl
from jax.experimental.pallas import tpu as pltpu
from jax.sharding import PartitionSpec as P

SLOTS = 3
AXES = ("var", "samp")
F32 = jnp.float32
BF16 = jnp.bfloat16
VMEM = pl.BlockSpec(memory_space=pltpu.VMEM)
SMEM = pl.BlockSpec(memory_space=pltpu.SMEM)
SOME = pltpu.CompilerParams(vmem_limit_bytes=24 << 20)
MOST = pltpu.CompilerParams(vmem_limit_bytes=58 << 20)
D_BLOCKS = {0: [(0, 0)], 1: [(0, 1), (1, 0), (1, 1)]}


def dot(a, b):
    return jnp.dot(a, b, preferred_element_type=F32)


def standardized(raw, stat_ref):
    return ((raw.astype(F32) - stat_ref[0:1, :]) * stat_ref[1:2, :]).astype(BF16)


def cut_kernel(left_ref, right_ref, out_ref):
    strip = left_ref.shape[1]
    out_ref[:, :strip] = left_ref[...]
    out_ref[:, strip:] = right_ref[...]


def first_kernel(steps, x_ref, copy_ref, chunk_ref, out_ref, center, total, square):
    step = pl.program_id(0)
    rows, width = x_ref.shape
    strip = chunk_ref.shape[1] // 2
    group = min(64, rows)
    copy_ref[...] = x_ref[...]
    for half in range(2):
        start = (2 * half + 1) * strip
        chunk_ref[:, half * strip:(half + 1) * strip] = x_ref[:, start:start + strip]

    @pl.when(step == 0)
    def _():
        center[...] = jnp.mean(x_ref[:group, :].astype(F32), axis=0, keepdims=True)
        total[...] = jnp.zeros_like(total)
        square[...] = jnp.zeros_like(square)

    middle = center[...]

    def add(i, sums):
        x = x_ref[pl.ds(pl.multiple_of(i * group, group), group), :].astype(F32) - middle
        x = x.reshape(group // 8, 8, width)
        return sums[0] + jnp.sum(x, axis=0), sums[1] + jnp.sum(x * x, axis=0)

    sums = lax.fori_loop(0, rows // group, add, (total[...], square[...]))
    total[...], square[...] = sums

    @pl.when(step == pl.num_programs(0) - 1)
    def _():
        count = float(rows * steps)
        shift = jnp.sum(total[...], axis=0, keepdims=True) * (1.0 / count)
        around = jnp.sum(square[...], axis=0, keepdims=True) - shift * shift * count
        out_ref[0:1, :] = middle + shift
        out_ref[1:2, :] = jnp.maximum(around, 0.0)


def stat_kernel(pos_ref, live_ref, offsets_ref, own_ref, sib_ref, far_ref, cross_ref, plain_ref, chunked_ref):
    width = own_ref.shape[1]
    strip = width // 4
    samples = pos_ref[4].astype(F32)

    def merged(values):
        return (values[0] + values[1]) + (values[2] + values[3])

    groups = (own_ref, sib_ref, far_ref, cross_ref)
    mean = merged([ref[0:1, :] for ref in groups]) * 0.25
    between = merged([jnp.square(ref[0:1, :] - mean) for ref in groups]) * (samples * 0.25)
    spread = (merged([ref[1:2, :] for ref in groups]) + between) / samples
    live = lax.broadcasted_iota(jnp.int32, (1, width), 1) < live_ref[0]
    plain_ref[0:1, :] = mean
    plain_ref[1:2, :] = jnp.where(live, lax.rsqrt(spread + 1e-05), 0.0)
    for step in (1, 2):
        listed = offsets_ref[0, 0] == step
        for slot in range(1, SLOTS):
            listed = jnp.logical_or(listed, offsets_ref[0, slot] == step)
        plain_ref[1 + step:2 + step, :] = jnp.full((1, width), jnp.where(listed, 1.0, 0.0), F32)
    for part in range(2):
        for half in range(2):
            start, to = (2 * half + part) * strip, (2 * part + half) * strip
            chunked_ref[:, to:to + strip] = plain_ref[:, start:start + strip]


def own_kernel(pos_ref, x_ref, stat_ref, turned_ref, keep_ref, send_ref, acc):
    step = pl.program_id(0)
    z = standardized(x_ref[...], stat_ref)
    zt = z.T
    turned_ref[...] = zt
    part = dot(zt, z)

    @pl.when(step == 0)
    def _():
        acc[...] = part

    @pl.when(step > 0)
    def _():
        acc[...] += part

    @pl.when(step == pl.num_programs(0) - 1)
    def _():
        half = keep_ref.shape[0]
        keep_ref[...] = acc[pl.ds(pl.multiple_of(pos_ref[0] * half, half), half), :]
        send_ref[...] = acc[pl.ds(pl.multiple_of((1 - pos_ref[0]) * half, half), half), :]


def put_blocks(x, source, base, out_keep, out_send, first, parts):
    size = out_keep.shape[-1]
    for out, near in ((out_keep, x), (out_send, 1 - x)):
        index = first
        for r, h in ((near, near), (near, 1 - near), (1 - near, near)):
            for part in range(parts):
                row = pl.multiple_of(r * parts * size + part * size, size)
                col = pl.multiple_of(base + h * size, size)
                out[index] = source[pl.ds(row, size), pl.ds(col, size)].astype(out.dtype)
                index += 1


def pair_kernel(chunk, *refs):
    (pos_ref, turned_ref, y_ref, w_ref, stat_ref, ystat_ref, wstat_ref), refs = refs[:7], refs[7:]
    if chunk == 0:
        (keep_c, send_c, keep_bd, send_bd, yt_out, w_out), accs = refs[:6], refs[6:]
    else:
        (yt_old, w_old, keep_c, send_c, keep_bd, send_bd), accs = refs[:6], refs[6:]
    acc_b, acc_c, acc_d = accs[:3]
    step = pl.program_id(0)
    last = pl.num_programs(0) - 1
    x = pos_ref[0]
    active = pos_ref[1] == 1
    size = keep_c.shape[-1]

    @pl.when(step == 0)
    def _():
        for acc in accs:
            acc[...] = jnp.zeros_like(acc)

    zt = turned_ref[...]
    w = standardized(w_ref[...], wstat_ref)
    acc_c[...] += dot(zt, w)
    if chunk == 0:
        w_out[...] = w

    @pl.when(active)
    def _():
        y = standardized(y_ref[...], ystat_ref)
        yt = y.T
        acc_b[...] += dot(zt, y)
        if chunk == 0:
            yt_out[...] = yt
            acc_d[...] += dot(yt, w)
        else:
            accs[3][...] += dot(yt_old[...], w)
            acc_d[:, :2 * size] += dot(yt, w_old[...])
            acc_d[:, 2 * size:] += dot(yt, w)

    @pl.when(step == last)
    def _():
        first = pos_ref[2] == 0
        share = 1.0 / pos_ref[4].astype(F32)
        acc_c[...] *= jnp.where(first, stat_ref[3:4, :], wstat_ref[3:4, :]) * share
        put_blocks(x, acc_c, 0, keep_c, send_c, 0, 2)

        @pl.when(active)
        def _():
            acc_b[...] *= jnp.where(first, stat_ref[2:3, :], ystat_ref[2:3, :]) * share
            put_blocks(x, acc_b, 0, keep_bd, send_bd, 0, 2)
            scale = jnp.where(first, ystat_ref[2:3, :], wstat_ref[2:3, :]) * share
            acc_d[:, :2 * size] *= scale
            if chunk == 0:
                put_blocks(x, acc_d, 0, keep_bd, send_bd, 6, 1)
            else:
                acc_e = accs[3]
                acc_d[:, 2 * size:] *= scale
                acc_e[...] *= scale
                put_blocks(x, acc_e, 0, keep_bd, send_bd, 6, 1)
                put_blocks(x, acc_d, 0, keep_bd, send_bd, 9, 1)
                put_blocks(x, acc_d, 2 * size, keep_bd, send_bd, 12, 1)


def strips_kernel(chunk, pos_ref, keep_c, got_c, keep_bd, got_bd, held_b, held_c, to_y, to_z):
    size = keep_c.shape[-1]
    x = pos_ref[0]

    def at(half, part):
        return pl.ds(pl.multiple_of(half * 2 * size + part * size, size), size)

    def summed(keep, got, index):
        return keep[index] + got[index].astype(F32)

    def side(keep, got, held, out):
        for core in range(2):
            for first, half in ((0, x), (2, 1 - x)):
                held[core, :, pl.ds(pl.multiple_of(half * size, size), size)] = summed(keep, got, first + core)
            for first, half in ((0, x), (4, 1 - x)):
                out[:, at(half, core)] = summed(keep, got, first + core).T.astype(out.dtype)

    side(keep_c, got_c, held_c, to_z)

    @pl.when(pos_ref[1] == 1)
    def _():
        side(keep_bd, got_bd, held_b, to_y)
        for index in range(len(D_BLOCKS[chunk])):
            near, right, below = [summed(keep_bd, got_bd, 6 + 3 * index + which) for which in range(3)]
            start = (4 + 2 * index) * size
            to_y[:, start:start + size] = near.astype(to_y.dtype)
            to_y[:, start + size:start + 2 * size] = right.astype(to_y.dtype)
            to_z[:, start:start + size] = near.T.astype(to_z.dtype)
            to_z[:, start + size:start + 2 * size] = below.T.astype(to_z.dtype)


def combine_kernel(pos_ref, held_b0, held_c0, held_b1, held_c1, y_0, z_0, y_1, z_1, diag_keep, diag_got, mine, sib):
    size = held_b0.shape[1]
    x = pos_ref[0]
    active = pos_ref[1]

    def at(half, part):
        return pl.ds(pl.multiple_of(half * 2 * size + part * size, size), size)

    def fill(core, out):
        def total(index, helds, side):
            for part, held in enumerate(helds):
                for half in range(2):
                    cols = slice((2 * half + part) * size, (2 * half + part + 1) * size)
                    out[index, :, cols] = (held[core, :, half * size:(half + 1) * size] + side[:, cols].astype(F32))

        def far(pieces, sides):
            for part in range(2):
                block = pieces(part)
                chunk = max(block)
                start = (4 + 2 * D_BLOCKS[chunk].index(block)) * size
                out[2, :, at(x, part)] = sides[chunk][:, start:start + size].astype(F32)
                out[2, :, at(1 - x, part)] = sides[chunk][:, start + size:start + 2 * size].astype(F32)

        total(1, (held_c0, held_c1), (z_0, z_1)[core])

        @pl.when(active == 1)
        def _():
            total(0, (held_b0, held_b1), (y_0, y_1)[core])
            far(lambda part: (core, part), (y_0, y_1))

        @pl.when(active == 0)
        def _():
            far(lambda part: (part, core), (z_0, z_1))

        rows = slice(core * size, (core + 1) * size)
        out[3] = diag_keep[rows, :] + diag_got[rows, :]

    for core in range(2):
        @pl.when(pos_ref[2] == core)
        def _():
            fill(core, mine)
            fill(1 - core, sib)


def finish_kernel(pos_ref, offsets_ref, mine, sib, upper, mirror):
    active = pos_ref[1] == 1
    first_core = pos_ref[2] == 0
    even = pos_ref[3] == 0
    pick = jnp.where
    near = pick(active, mine[0], sib[0])
    far = mine[2] + sib[2]
    upper_1 = pick(even, near, far)
    upper_2 = pick(first_core, mine[1], sib[1])
    mirror[0, 0] = pick(even, far, near).astype(BF16)
    mirror[0, 1] = pick(first_core, sib[1], mine[1]).astype(BF16)
    self_tile = (mine[3] + sib[3]) * (1.0 / pos_ref[4].astype(F32))
    for slot in range(SLOTS):
        offset = offsets_ref[0, slot]
        tile = pick(offset == 0, self_tile, pick(offset == 1, upper_1, pick(offset == 2, upper_2, 0.0)))
        upper[0, slot] = tile.astype(BF16)


def body(dosage, pair_offsets, live_counts):
    n_var = lax.axis_size("var")
    n_samp = lax.axis_size("samp")
    depth, width = dosage.shape
    half = width // 2
    strip = width // n_samp
    samples_all = depth * n_samp
    v = lax.axis_index("var")
    s = lax.axis_index("samp")
    x, core, odd = s // 2, s % 2, v % 2
    active = (core == odd).astype(jnp.int32)

    def at(var, samp):
        return var * n_samp + samp

    def active_on(var, samp):
        return var % 2 == samp % 2

    everyone = [(var, samp) for var in range(n_var) for samp in range(n_samp)]
    z_main = [(at(a, b), at(a - 2 if b % 2 == 0 else a + 2, b)) for a, b in everyone
              if 0 <= (a - 2 if b % 2 == 0 else a + 2) < n_var]
    y_main = [(at(a, b), at(a ^ 1, b)) for a, b in everyone if not active_on(a, b)]
    across = [(at(a, b), at(a, b ^ 2)) for a, b in everyone]
    across_active = [(at(a, b), at(a, b ^ 2)) for a, b in everyone if active_on(a, b)]
    sibling = [(at(a, b), at(a, b ^ 1)) for a, b in everyone]

    def send(value, pairs):
        return lax.ppermute(value, AXES, pairs)

    pos = jnp.stack([x, active, core, odd, jnp.int32(samples_all), s]).astype(jnp.int32)
    step_rows = min(1024, depth)
    steps = depth // step_rows
    tall = pl.BlockSpec((step_rows, half), lambda k: (k, 0))
    wide = pl.BlockSpec((step_rows, width), lambda k: (k, 0))
    flat = lambda rows: pl.BlockSpec((rows, step_rows), lambda k: (0, k))
    whole = lambda *shape: pl.BlockSpec(shape, lambda k: (0,) * len(shape))

    chunk_0 = pl.pallas_call(
        cut_kernel,
        grid=(steps,),
        in_specs=[pl.BlockSpec((step_rows, strip), lambda k, half=half: (k, 2 * half)) for half in range(2)],
        out_specs=tall,
        out_shape=jax.ShapeDtypeStruct((depth, half), BF16),
        compiler_params=MOST,
        cost_estimate=pl.CostEstimate(flops=0, bytes_accessed=2 * depth * width, transcendentals=0),
        name="first_chunk",
    )(dosage, dosage)
    w_raw, y_raw = [send(chunk_0, z_main)], [send(chunk_0, y_main)]
    dosage, chunk_0 = lax.optimization_barrier((dosage, chunk_0))
    block, chunk_1, local = pl.pallas_call(
        lambda *refs: first_kernel(steps, *refs),
        grid=(steps,),
        in_specs=[wide],
        out_specs=[wide, tall, whole(2, width)],
        out_shape=[jax.ShapeDtypeStruct((depth, width), BF16), jax.ShapeDtypeStruct((depth, half), BF16),
                   jax.ShapeDtypeStruct((2, width), F32)],
        scratch_shapes=[pltpu.VMEM((1, width), F32)] + [pltpu.VMEM((8, width), F32)] * 2,
        compiler_params=SOME,
        cost_estimate=pl.CostEstimate(flops=5 * depth * width, bytes_accessed=5 * depth * width, transcendentals=0),
        name="second_chunk_and_local_stats",
    )(dosage)
    others = [send(local, [(at(a, b), at(a, b ^ flip)) for a, b in everyone]) for flip in (1, 2, 3)]
    stat, stat_chunked = pl.pallas_call(
        stat_kernel,
        in_specs=[SMEM, SMEM, SMEM] + [VMEM] * 4,
        out_specs=[VMEM, VMEM],
        out_shape=[jax.ShapeDtypeStruct((4, width), F32)] * 2,
        compiler_params=SOME,
        name="stats",
    )(pos, live_counts, pair_offsets, local, *others)
    z_step = [(a, b, a + 2 if b % 2 == 0 else a - 2) for a, b in everyone]
    z_cross = [(at(a, b), at(t, b ^ 1)) for a, b, t in z_step if 0 <= t < n_var]
    y_cross = [(at(a, b), at(a ^ 1, b ^ 1)) for a, b in everyone if active_on(a, b)]
    w_stat, y_stat = send(stat_chunked, z_cross), send(stat_chunked, y_cross)

    turned, diag_keep, diag_send = pl.pallas_call(
        own_kernel,
        grid=(steps,),
        in_specs=[SMEM, wide, whole(4, width)],
        out_specs=[flat(width)] + [whole(half, width)] * 2,
        out_shape=[jax.ShapeDtypeStruct((width, depth), BF16)] + [jax.ShapeDtypeStruct((half, width), F32)] * 2,
        scratch_shapes=[pltpu.VMEM((width, width), F32)],
        compiler_params=SOME,
        cost_estimate=pl.CostEstimate(flops=2 * depth * width * width, bytes_accessed=4 * depth * width, transcendentals=0),
        name="own_tile",
    )(pos, block, stat)
    turned, w_stat, y_stat, chunk_1 = lax.optimization_barrier((turned, w_stat, y_stat, chunk_1))
    w_raw.append(send(chunk_1, z_main))
    y_raw.append(send(chunk_1, y_main))
    diag_across = send(diag_send, across)
    keeps, arrived, passed, before = [], [], [], [diag_across]
    sent_as = (F32, BF16)
    for part in range(2):
        n_bd = 6 + 3 * len(D_BLOCKS[part])
        in_specs = [SMEM, flat(width), tall, tall] + [pl.BlockSpec((4, half), lambda k, part=part: (0, part))] * 3
        sums = [(width, half), (width, half), (half, half if part == 0 else width)] + [(half, half)] * part
        out_specs = [whole(n, strip, strip) for n in (6, 6, n_bd, n_bd)]
        out_shape = [jax.ShapeDtypeStruct((n, strip, strip), kind) for n in (6, n_bd) for kind in (F32, sent_as[part])]
        if part == 0:
            out_specs += [flat(half), tall]
            out_shape += [jax.ShapeDtypeStruct((half, depth), BF16), jax.ShapeDtypeStruct((depth, half), BF16)]
        else:
            in_specs += [flat(half), tall]
        keep_c, send_c, keep_bd, send_bd, *passed = pl.pallas_call(
            lambda *refs, part=part: pair_kernel(part, *refs),
            grid=(steps,),
            in_specs=in_specs,
            out_specs=out_specs,
            out_shape=out_shape,
            scratch_shapes=[pltpu.VMEM(shape, F32) for shape in sums],
            compiler_params=SOME,
            cost_estimate=pl.CostEstimate(flops=3 * depth * width * width, bytes_accessed=4 * depth * width, transcendentals=0),
            name=f"pair_tiles_{part}",
        )(pos, turned, y_raw[part], w_raw[part], stat_chunked, y_stat, w_stat, *passed)
        send_bd, send_c, *before = lax.optimization_barrier((send_bd, send_c, *before))
        arrived += before
        before = [send(send_bd, across_active), send(send_c, across)]
        keeps.append((keep_bd, keep_c))
    arrived += before

    held, sides = [], []
    for part, (keep_bd, keep_c) in enumerate(keeps):
        sent = jax.ShapeDtypeStruct((strip, width + half * len(D_BLOCKS[part])), sent_as[part])
        held_b, held_c, to_y, to_z = pl.pallas_call(
            lambda *refs, part=part: strips_kernel(part, *refs),
            in_specs=[SMEM] + [VMEM] * 4,
            out_specs=[VMEM] * 4,
            out_shape=[jax.ShapeDtypeStruct((2, strip, half), F32)] * 2 + [sent] * 2,
            compiler_params=SOME,
            name=f"strips_{part}",
        )(pos, keep_c, arrived[2 + 2 * part], keep_bd, arrived[1 + 2 * part])
        held += [held_b, held_c]
        sides += [send(to_y, y_cross), send(to_z, z_cross)]

    four = jax.ShapeDtypeStruct((4, strip, width), F32)
    mine, sib = pl.pallas_call(
        combine_kernel,
        in_specs=[SMEM] + [VMEM] * 10,
        out_specs=[VMEM] * 2,
        out_shape=[four] * 2,
        compiler_params=SOME,
        name="combine",
    )(pos, *held, *sides, diag_keep, arrived[0])

    return pl.pallas_call(
        finish_kernel,
        in_specs=[SMEM, SMEM, VMEM, VMEM],
        out_specs=[VMEM, VMEM],
        out_shape=[jax.ShapeDtypeStruct((1, SLOTS, strip, width), BF16),
                   jax.ShapeDtypeStruct((1, 2, strip, width), BF16)],
        compiler_params=SOME,
        name="finish",
    )(pos, pair_offsets, mine, send(sib, sibling))


def solution(mesh):
    in_specs = (P("samp", "var"), P("var", None), P("var"))
    out_specs = (P("var", None, "samp", None), P("var", None, "samp", None))
    return jax.shard_map(body, mesh=mesh, in_specs=in_specs, out_specs=out_specs, check_vma=False)
```

```python
import jax
import jax.numpy as jnp
from jax import lax
from jax.experimental import pallas as pl
from jax.experimental.pallas import tpu as pltpu
from jax.sharding import PartitionSpec as P

SLOTS = 3
AXES = ("var", "samp")
F32 = jnp.float32
BF16 = jnp.bfloat16
VMEM = pl.BlockSpec(memory_space=pltpu.VMEM)
SMEM = pl.BlockSpec(memory_space=pltpu.SMEM)
SOME = pltpu.CompilerParams(vmem_limit_bytes=24 << 20)
C_TYPE, BD_TYPE = F32, BF16


def dot(a, b):
    return jnp.dot(a, b, preferred_element_type=F32)


def standardized(raw, stat_ref):
    return ((raw.astype(F32) - stat_ref[0:1, :]) * stat_ref[1:2, :]).astype(BF16)


def local_kernel(steps, x_ref, out_ref, center, total, square):
    step = pl.program_id(0)
    rows, width = x_ref.shape
    group = min(64, rows)

    @pl.when(step == 0)
    def _():
        center[...] = jnp.mean(x_ref[:group, :].astype(F32), axis=0, keepdims=True)
        total[...] = jnp.zeros_like(total)
        square[...] = jnp.zeros_like(square)

    middle = center[...]

    def add(i, sums):
        x = x_ref[pl.ds(pl.multiple_of(i * group, group), group), :].astype(F32) - middle
        x = x.reshape(group // 8, 8, width)
        return sums[0] + jnp.sum(x, axis=0), sums[1] + jnp.sum(x * x, axis=0)

    sums = lax.fori_loop(0, rows // group, add, (total[...], square[...]))
    total[...], square[...] = sums

    @pl.when(step == steps - 1)
    def _():
        count = float(rows * steps)
        shift = jnp.sum(total[...], axis=0, keepdims=True) * (1.0 / count)
        around = jnp.sum(square[...], axis=0, keepdims=True) - shift * shift * count
        out_ref[0:1, :] = middle + shift
        out_ref[1:2, :] = jnp.maximum(around, 0.0)


def stat_kernel(pos_ref, live_ref, offsets_ref, own_ref, sib_ref, far_ref, cross_ref, stat_ref):
    width = own_ref.shape[1]
    samples = pos_ref[4].astype(F32)

    def merged(values):
        return (values[0] + values[1]) + (values[2] + values[3])

    groups = (own_ref, sib_ref, far_ref, cross_ref)
    mean = merged([ref[0:1, :] for ref in groups]) * 0.25
    between = merged([jnp.square(ref[0:1, :] - mean) for ref in groups]) * (samples * 0.25)
    spread = (merged([ref[1:2, :] for ref in groups]) + between) / samples
    live = lax.broadcasted_iota(jnp.int32, (1, width), 1) < live_ref[0]
    stat_ref[0:1, :] = mean
    stat_ref[1:2, :] = jnp.where(live, lax.rsqrt(spread + 1e-05), 0.0)
    for step in (1, 2):
        listed = offsets_ref[0, 0] == step
        for slot in range(1, SLOTS):
            listed = jnp.logical_or(listed, offsets_ref[0, slot] == step)
        stat_ref[1 + step:2 + step, :] = jnp.full((1, width), jnp.where(listed, 1.0, 0.0), F32)


def own_kernel(pos_ref, x_ref, stat_ref, turned_ref, keep_ref, send_ref, acc):
    step = pl.program_id(0)
    z = standardized(x_ref[...], stat_ref)
    zt = z.T
    turned_ref[...] = zt
    part = dot(zt, z)

    @pl.when(step == 0)
    def _():
        acc[...] = part

    @pl.when(step > 0)
    def _():
        acc[...] += part

    @pl.when(step == pl.num_programs(0) - 1)
    def _():
        rows = keep_ref.shape[1]
        for far in range(2):
            for core, out in ((pos_ref[2], keep_ref), (1 - pos_ref[2], send_ref)):
                out[far] = acc[pl.ds(pl.multiple_of((2 * far + core) * rows, rows), rows), :]


def diag_kernel(pos_ref, keep_ref, got_ref, mine_ref, send_ref):
    mine_ref[...] = keep_ref[pos_ref[0]] + got_ref[pos_ref[0]]
    send_ref[...] = keep_ref[1 - pos_ref[0]] + got_ref[1 - pos_ref[0]]


def put_quarters(x, source, keep, send):
    half = keep.shape[-1]
    for out, near in ((keep, x), (send, 1 - x)):
        for index, (row, col) in enumerate(((near, near), (near, 1 - near), (1 - near, near))):
            rows = pl.ds(pl.multiple_of(row * half, half), half)
            cols = pl.ds(pl.multiple_of(col * half, half), half)
            out[index] = source[rows, cols].astype(out.dtype)


def far_kernel(pos_ref, turned_ref, w_ref, stat_ref, wstat_ref, keep_ref, send_ref, w_out, acc):
    step = pl.program_id(0)

    @pl.when(step == 0)
    def _():
        acc[...] = jnp.zeros_like(acc)

    w = standardized(w_ref[...], wstat_ref)
    w_out[...] = w
    acc[...] += dot(turned_ref[...], w)

    @pl.when(step == pl.num_programs(0) - 1)
    def _():
        listed = jnp.where(pos_ref[2] == 0, stat_ref[3:4, :], wstat_ref[3:4, :])
        acc[...] *= listed * (1.0 / pos_ref[4].astype(F32))
        put_quarters(pos_ref[0], acc, keep_ref, send_ref)


def near_kernel(pos_ref, turned_ref, y_ref, w_ref, stat_ref, ystat_ref, wstat_ref, keep_ref, send_ref, acc_b, acc_d):
    step = pl.program_id(0)

    @pl.when(pos_ref[1] == 1)
    def _():
        @pl.when(step == 0)
        def _():
            acc_b[...] = jnp.zeros_like(acc_b)
            acc_d[...] = jnp.zeros_like(acc_d)

        y = standardized(y_ref[...], ystat_ref)
        acc_b[...] += dot(turned_ref[...], y)
        acc_d[...] += dot(y.T, w_ref[...])

        @pl.when(step == pl.num_programs(0) - 1)
        def _():
            first = pos_ref[2] == 0
            share = 1.0 / pos_ref[4].astype(F32)
            acc_b[...] *= jnp.where(first, stat_ref[2:3, :], ystat_ref[2:3, :]) * share
            acc_d[...] *= jnp.where(first, ystat_ref[2:3, :], wstat_ref[2:3, :]) * share
            put_quarters(pos_ref[0], acc_b, keep_ref.at[0], send_ref.at[0])
            put_quarters(pos_ref[0], acc_d, keep_ref.at[1], send_ref.at[1])


def add_halves(x, keep, got, rows_out, cols_out):
    half = keep.shape[-1]
    here = pl.ds(pl.multiple_of(x * half, half), half)
    there = pl.ds(pl.multiple_of((1 - x) * half, half), half)
    corner = keep[0] + got[0].astype(F32)
    rows_out[:, here] = corner.astype(rows_out.dtype)
    rows_out[:, there] = (keep[1] + got[1].astype(F32)).astype(rows_out.dtype)
    cols_out[:, here] = corner.T.astype(cols_out.dtype)
    cols_out[:, there] = (keep[2] + got[2].astype(F32)).T.astype(cols_out.dtype)


def far_strips_kernel(pos_ref, keep, got, held, to_z):
    add_halves(pos_ref[0], keep, got, held, to_z)


def near_strips_kernel(pos_ref, keep, got, held, to_y, to_z):
    @pl.when(pos_ref[1] == 1)
    def _():
        add_halves(pos_ref[0], keep.at[0], got.at[0], held, to_y.at[0])
        add_halves(pos_ref[0], keep.at[1], got.at[1], to_y.at[1], to_z)


def combine_kernel(pos_ref, held_b, held_c, from_y, from_z_c, from_z_d, mine, sib):
    rows = mine.shape[1]
    for core, out in ((pos_ref[2], mine), (1 - pos_ref[2], sib)):
        at = pl.ds(pl.multiple_of(core * rows, rows), rows)
        out[1] = held_c[at, :] + from_z_c[at, :].astype(F32)

        @pl.when(pos_ref[1] == 1)
        def _():
            out[0] = held_b[at, :] + from_y[0, at, :].astype(F32)
            out[2] = from_y[1, at, :].astype(F32)

        @pl.when(pos_ref[1] == 0)
        def _():
            out[2] = from_z_d[at, :].astype(F32)


def finish_kernel(pos_ref, offsets_ref, diag_mine, diag_got, mine, sib, upper, mirror):
    active = pos_ref[1] == 1
    first_core = pos_ref[2] == 0
    even = pos_ref[3] == 0
    pick = jnp.where
    near = pick(active, mine[0], sib[0])
    far = mine[2] + sib[2]
    upper_1 = pick(even, near, far)
    upper_2 = pick(first_core, mine[1], sib[1])
    mirror[0, 0] = pick(even, far, near).astype(BF16)
    mirror[0, 1] = pick(first_core, sib[1], mine[1]).astype(BF16)
    self_tile = (diag_mine[...] + diag_got[...]) * (1.0 / pos_ref[4].astype(F32))
    for slot in range(SLOTS):
        offset = offsets_ref[0, slot]
        tile = pick(offset == 0, self_tile, pick(offset == 1, upper_1, pick(offset == 2, upper_2, 0.0)))
        upper[0, slot] = tile.astype(BF16)


def body(dosage, pair_offsets, live_counts):
    n_var = lax.axis_size("var")
    n_samp = lax.axis_size("samp")
    depth, width = dosage.shape
    half = width // 2
    strip = width // n_samp
    samples_all = depth * n_samp
    v = lax.axis_index("var")
    s = lax.axis_index("samp")
    x, core, odd = s // 2, s % 2, v % 2
    active = (core == odd).astype(jnp.int32)

    def at(var, samp):
        return var * n_samp + samp

    def active_on(var, samp):
        return var % 2 == samp % 2

    def send(value, pairs):
        return lax.ppermute(value, AXES, pairs)

    def shape(*dims, dtype=F32):
        return jax.ShapeDtypeStruct(dims, dtype)

    everyone = [(var, samp) for var in range(n_var) for samp in range(n_samp)]
    z_main = [(at(a, b), at(a - 2 if b % 2 == 0 else a + 2, b)) for a, b in everyone
              if 0 <= (a - 2 if b % 2 == 0 else a + 2) < n_var]
    y_main = [(at(a, b), at(a ^ 1, b)) for a, b in everyone if not active_on(a, b)]
    z_step = [(a, b, a + 2 if b % 2 == 0 else a - 2) for a, b in everyone]
    z_cross = [(at(a, b), at(t, b ^ 1)) for a, b, t in z_step if 0 <= t < n_var]
    z_cross_active = [(at(a, b), at(t, b ^ 1)) for a, b, t in z_step if 0 <= t < n_var and active_on(a, b)]
    y_cross = [(at(a, b), at(a ^ 1, b ^ 1)) for a, b in everyone if active_on(a, b)]
    across = [(at(a, b), at(a, b ^ 2)) for a, b in everyone]
    across_active = [(at(a, b), at(a, b ^ 2)) for a, b in everyone if active_on(a, b)]
    sibling = [(at(a, b), at(a, b ^ 1)) for a, b in everyone]

    w_raw, y_raw = send(dosage, z_main), send(dosage, y_main)

    pos = jnp.stack([x, active, core, odd, jnp.int32(samples_all)]).astype(jnp.int32)
    step_rows = min(1024, depth)
    steps = depth // step_rows
    wide = pl.BlockSpec((step_rows, width), lambda k: (k, 0))
    flat = pl.BlockSpec((width, step_rows), lambda k: (0, k))
    whole = lambda *dims: pl.BlockSpec(dims, lambda k: (0,) * len(dims))

    def call(kernel, name, grid, in_specs, out_specs, out_shape, scratch=(), flops=0, moved=0):
        return pl.pallas_call(
            kernel, grid=grid, in_specs=in_specs, out_specs=out_specs, out_shape=out_shape, scratch_shapes=scratch,
            compiler_params=SOME, name=name,
            cost_estimate=pl.CostEstimate(flops=flops, bytes_accessed=moved, transcendentals=0))

    bytes_block, tile_flops = 2 * depth * width, 2 * depth * width * width
    local = call(lambda *refs: local_kernel(steps, *refs), "local_stats", (steps,), [wide], whole(2, width), shape(2, width),
                 [pltpu.VMEM((1, width), F32)] + [pltpu.VMEM((8, width), F32)] * 2, 5 * depth * width, bytes_block)(dosage)
    others = [send(local, [(at(a, b), at(a, b ^ flip)) for a, b in everyone]) for flip in (1, 2, 3)]
    stat = call(stat_kernel, "stats", (), [SMEM] * 3 + [VMEM] * 4, VMEM, shape(4, width))(
        pos, live_counts, pair_offsets, local, *others)
    w_stat, y_stat = send(stat, z_cross), send(stat, y_cross)

    turned, diag_keep, diag_send = call(
        own_kernel, "own_tile", (steps,), [SMEM, wide, whole(4, width)],
        [flat, whole(2, strip, width), whole(2, strip, width)],
        [shape(width, depth, dtype=BF16), shape(2, strip, width), shape(2, strip, width)],
        [pltpu.VMEM((width, width), F32)], tile_flops, 2 * bytes_block)(pos, dosage, stat)
    diag_mine, diag_other = call(diag_kernel, "own_tile_strips", (), [SMEM, VMEM, VMEM], [VMEM] * 2, [shape(strip, width)] * 2)(
        pos, diag_keep, send(diag_send, sibling))
    diag_got = send(diag_other, across)

    keep_c, send_c, w = call(
        far_kernel, "far_tile", (steps,), [SMEM, flat, wide, whole(4, width), whole(4, width)],
        [whole(3, half, half)] * 2 + [wide],
        [shape(3, half, half), shape(3, half, half, dtype=C_TYPE), shape(depth, width, dtype=BF16)],
        [pltpu.VMEM((width, width), F32)], tile_flops, 3 * bytes_block)(pos, turned, w_raw, stat, w_stat)
    send_c, diag_got = lax.optimization_barrier((send_c, diag_got))
    got_c = send(send_c, across)

    keep_bd, send_bd = call(
        near_kernel, "near_tiles", (steps,), [SMEM, flat, wide, wide] + [whole(4, width)] * 3,
        [whole(2, 3, half, half)] * 2,
        [shape(2, 3, half, half), shape(2, 3, half, half, dtype=BD_TYPE)],
        [pltpu.VMEM((width, width), F32)] * 2, 2 * tile_flops, 3 * bytes_block)(pos, turned, y_raw, w, stat, y_stat, w_stat)
    got_bd = send(send_bd, across_active)

    held_c, to_z_c = call(far_strips_kernel, "far_strips", (), [SMEM] + [VMEM] * 2, [VMEM] * 2,
                          [shape(half, width), shape(half, width, dtype=C_TYPE)])(pos, keep_c, got_c)
    from_z_c = send(to_z_c, z_cross)
    held_b, to_y, to_z_d = call(
        near_strips_kernel, "near_strips", (), [SMEM] + [VMEM] * 2, [VMEM] * 3,
        [shape(half, width), shape(2, half, width, dtype=BD_TYPE), shape(half, width, dtype=BD_TYPE)])(pos, keep_bd, got_bd)
    from_y, from_z_d = send(to_y, y_cross), send(to_z_d, z_cross_active)

    mine, sib = call(combine_kernel, "combine", (), [SMEM] + [VMEM] * 5, [VMEM] * 2, [shape(3, strip, width)] * 2)(
        pos, held_b, held_c, from_y, from_z_c, from_z_d)
    return call(finish_kernel, "finish", (), [SMEM] * 2 + [VMEM] * 4, [VMEM] * 2,
                [shape(1, SLOTS, strip, width, dtype=BF16), shape(1, 2, strip, width, dtype=BF16)])(
        pos, pair_offsets, diag_mine, diag_got, mine, send(sib, sibling))


def solution(mesh):
    in_specs = (P("samp", "var"), P("var", None), P("var"))
    out_specs = (P("var", None, "samp", None), P("var", None, "samp", None))
    return jax.shard_map(body, mesh=mesh, in_specs=in_specs, out_specs=out_specs, check_vma=False)
```

```python
import jax
import jax.numpy as jnp
from jax import lax
from jax.experimental import pallas as pl
from jax.experimental.pallas import tpu as pltpu
from jax.sharding import PartitionSpec as P

SLOTS = 3
AXES = ("var", "samp")
F32 = jnp.float32
BF16 = jnp.bfloat16
VMEM = pl.BlockSpec(memory_space=pltpu.VMEM)
SMEM = pl.BlockSpec(memory_space=pltpu.SMEM)
SOME = pltpu.CompilerParams(vmem_limit_bytes=24 << 20)


def dot(a, b):
    return jnp.dot(a, b, preferred_element_type=F32)


def standardized(raw, stat_ref):
    return ((raw.astype(F32) - stat_ref[0:1, :]) * stat_ref[1:2, :]).astype(BF16)


def cut_kernel(part, x_ref, out_ref):
    size = out_ref.shape[1] // 2
    for half in range(2):
        start = (2 * half + part) * size
        out_ref[:, half * size:(half + 1) * size] = x_ref[:, start:start + size]


def local_kernel(steps, x_ref, chunk_ref, out_ref, center, total, square):
    step = pl.program_id(0)
    rows, width = x_ref.shape
    group = min(64, rows)
    cut_kernel(1, x_ref, chunk_ref)

    @pl.when(step == 0)
    def _():
        center[...] = jnp.mean(x_ref[:group, :].astype(F32), axis=0, keepdims=True)
        total[...] = jnp.zeros_like(total)
        square[...] = jnp.zeros_like(square)

    middle = center[...]

    def add(i, sums):
        x = x_ref[pl.ds(pl.multiple_of(i * group, group), group), :].astype(F32) - middle
        x = x.reshape(group // 8, 8, width)
        return sums[0] + jnp.sum(x, axis=0), sums[1] + jnp.sum(x * x, axis=0)

    sums = lax.fori_loop(0, rows // group, add, (total[...], square[...]))
    total[...], square[...] = sums

    @pl.when(step == steps - 1)
    def _():
        count = float(rows * steps)
        shift = jnp.sum(total[...], axis=0, keepdims=True) * (1.0 / count)
        around = jnp.sum(square[...], axis=0, keepdims=True) - shift * shift * count
        out_ref[0:1, :] = middle + shift
        out_ref[1:2, :] = jnp.maximum(around, 0.0)


def stat_kernel(pos_ref, live_ref, offsets_ref, own_ref, sib_ref, far_ref, cross_ref, stat_ref, chunked_ref):
    width = own_ref.shape[1]
    samples = pos_ref[4].astype(F32)

    def merged(values):
        return (values[0] + values[1]) + (values[2] + values[3])

    groups = (own_ref, sib_ref, far_ref, cross_ref)
    mean = merged([ref[0:1, :] for ref in groups]) * 0.25
    between = merged([jnp.square(ref[0:1, :] - mean) for ref in groups]) * (samples * 0.25)
    spread = (merged([ref[1:2, :] for ref in groups]) + between) / samples
    live = lax.broadcasted_iota(jnp.int32, (1, width), 1) < live_ref[0]
    stat_ref[0:1, :] = mean
    stat_ref[1:2, :] = jnp.where(live, lax.rsqrt(spread + 1e-05), 0.0)
    for step in (1, 2):
        listed = offsets_ref[0, 0] == step
        for slot in range(1, SLOTS):
            listed = jnp.logical_or(listed, offsets_ref[0, slot] == step)
        stat_ref[1 + step:2 + step, :] = jnp.full((1, width), jnp.where(listed, 1.0, 0.0), F32)
    for part in range(2):
        cut_kernel(part, stat_ref, chunked_ref.at[:, part * (width // 2):(part + 1) * (width // 2)])


def own_kernel(pos_ref, x_ref, stat_ref, turned_ref, keep_ref, send_ref, acc):
    step = pl.program_id(0)
    z = standardized(x_ref[...], stat_ref)
    zt = z.T
    turned_ref[...] = zt
    part = dot(zt, z)

    @pl.when(step == 0)
    def _():
        acc[...] = part

    @pl.when(step > 0)
    def _():
        acc[...] += part

    @pl.when(step == pl.num_programs(0) - 1)
    def _():
        rows = keep_ref.shape[1]
        for far in range(2):
            for core, out in ((pos_ref[2], keep_ref), (1 - pos_ref[2], send_ref)):
                out[far] = acc[pl.ds(pl.multiple_of((2 * far + core) * rows, rows), rows), :]


def diag_kernel(pos_ref, keep_ref, got_ref, mine_ref, send_ref):
    mine_ref[...] = keep_ref[pos_ref[0]] + got_ref[pos_ref[0]]
    send_ref[...] = keep_ref[1 - pos_ref[0]] + got_ref[1 - pos_ref[0]]


def put_quarters(x, source, keep, send):
    high, wide = keep.shape[1:]
    for out, near in ((keep, x), (send, 1 - x)):
        for index, (row, col) in enumerate(((near, near), (near, 1 - near), (1 - near, near))):
            rows = pl.ds(pl.multiple_of(row * high, high), high)
            cols = pl.ds(pl.multiple_of(col * wide, wide), wide)
            out[index] = source[rows, cols]


def far_kernel(pos_ref, turned_ref, w_ref, stat_ref, wstat_ref, keep_ref, send_ref, w_out, acc):
    step = pl.program_id(0)

    @pl.when(step == 0)
    def _():
        acc[...] = jnp.zeros_like(acc)

    w = standardized(w_ref[...], wstat_ref)
    w_out[...] = w
    acc[...] += dot(turned_ref[...], w)

    @pl.when(step == pl.num_programs(0) - 1)
    def _():
        listed = jnp.where(pos_ref[2] == 0, stat_ref[3:4, :], wstat_ref[3:4, :])
        acc[...] *= listed * (1.0 / pos_ref[4].astype(F32))
        put_quarters(pos_ref[0], acc, keep_ref, send_ref)


def near_kernel(pos_ref, turned_ref, y_ref, stat_ref, ystat_ref, keep_ref, send_ref, y_out, acc):
    step = pl.program_id(0)

    @pl.when(pos_ref[1] == 1)
    def _():
        @pl.when(step == 0)
        def _():
            acc[...] = jnp.zeros_like(acc)

        y = standardized(y_ref[...], ystat_ref)
        acc[...] += dot(turned_ref[...], y)
        y_out[...] = y.T

        @pl.when(step == pl.num_programs(0) - 1)
        def _():
            listed = jnp.where(pos_ref[2] == 0, stat_ref[2:3, :], ystat_ref[2:3, :])
            acc[...] *= listed * (1.0 / pos_ref[4].astype(F32))
            put_quarters(pos_ref[0], acc, keep_ref, send_ref)


def cross_kernel(pos_ref, y_ref, w0_ref, w1_ref, ystat_ref, wstat_ref, keep_ref, send_ref, acc_0, acc_1, acc):
    step = pl.program_id(0)

    @pl.when(pos_ref[1] == 1)
    def _():
        @pl.when(step == 0)
        def _():
            acc_0[...] = jnp.zeros_like(acc_0)
            acc_1[...] = jnp.zeros_like(acc_1)

        acc_0[...] += dot(y_ref[...], w0_ref[...])
        acc_1[...] += dot(y_ref[...], w1_ref[...])

        @pl.when(step == pl.num_programs(0) - 1)
        def _():
            listed = jnp.where(pos_ref[2] == 0, ystat_ref[2:3, :], wstat_ref[2:3, :]) * (1.0 / pos_ref[4].astype(F32))
            size = acc_0.shape[1] // 2
            for half in range(2):
                for part, piece in enumerate((acc_0, acc_1)):
                    start = (2 * half + part) * size
                    acc[:, start:start + size] = piece[:, half * size:(half + 1) * size] * listed[:, start:start + size]
            put_quarters(pos_ref[0], acc, keep_ref, send_ref)


def add_halves(x, keep, got, rows_out, cols_out):
    half = keep.shape[-1]
    here = pl.ds(pl.multiple_of(x * half, half), half)
    there = pl.ds(pl.multiple_of((1 - x) * half, half), half)
    corner = keep[0] + got[0]
    rows_out[:, here] = corner
    rows_out[:, there] = keep[1] + got[1]
    cols_out[:, here] = corner.T
    cols_out[:, there] = (keep[2] + got[2]).T


def far_strips_kernel(part, pos_ref, keep, got, rows_out, cols_out):
    high, wide = keep.shape[1:]
    x = pos_ref[0]
    here = pl.ds(pl.multiple_of(x * high, high), high)
    there = pl.ds(pl.multiple_of((1 - x) * high, high), high)
    corner = keep[0] + got[0]
    rows_out[:, pl.ds(pl.multiple_of(x * wide, wide), wide)] = corner
    rows_out[:, pl.ds(pl.multiple_of((1 - x) * wide, wide), wide)] = keep[1] + got[1]
    cols_out[:, here] = corner.T
    cols_out[:, there] = (keep[2] + got[2]).T


def near_strips_kernel(pos_ref, keep, got, rows_out, cols_out):
    @pl.when(pos_ref[1] == 1)
    def _():
        add_halves(pos_ref[0], keep, got, rows_out, cols_out)


def combine_kernel(pos_ref, held_b, held_c0, held_c1, from_y_b, from_y_d, from_z_c0, from_z_c1, from_z_d, mine, sib):
    rows = mine.shape[1]
    for core, out in ((pos_ref[2], mine), (1 - pos_ref[2], sib)):
        at = pl.ds(pl.multiple_of(core * rows, rows), rows)
        for part, held in enumerate((held_c0, held_c1)):
            for half in range(2):
                start = (2 * half + part) * rows
                side = jnp.where(core == 0, from_z_c0[:, start:start + rows], from_z_c1[:, start:start + rows])
                out[1, :, start:start + rows] = held[at, half * rows:(half + 1) * rows] + side

        @pl.when(pos_ref[1] == 1)
        def _():
            out[0] = held_b[at, :] + from_y_b[at, :]
            out[2] = from_y_d[at, :]

        @pl.when(pos_ref[1] == 0)
        def _():
            out[2] = from_z_d[at, :]


def finish_kernel(pos_ref, offsets_ref, diag_mine, diag_got, mine, sib, upper, mirror):
    active = pos_ref[1] == 1
    first_core = pos_ref[2] == 0
    even = pos_ref[3] == 0
    pick = jnp.where
    near = pick(active, mine[0], sib[0])
    far = mine[2] + sib[2]
    upper_1 = pick(even, near, far)
    upper_2 = pick(first_core, mine[1], sib[1])
    mirror[0, 0] = pick(even, far, near).astype(BF16)
    mirror[0, 1] = pick(first_core, sib[1], mine[1]).astype(BF16)
    self_tile = (diag_mine[...] + diag_got[...]) * (1.0 / pos_ref[4].astype(F32))
    for slot in range(SLOTS):
        offset = offsets_ref[0, slot]
        tile = pick(offset == 0, self_tile, pick(offset == 1, upper_1, pick(offset == 2, upper_2, 0.0)))
        upper[0, slot] = tile.astype(BF16)


def body(dosage, pair_offsets, live_counts):
    n_var = lax.axis_size("var")
    n_samp = lax.axis_size("samp")
    depth, width = dosage.shape
    half = width // 2
    strip = width // n_samp
    samples_all = depth * n_samp
    v = lax.axis_index("var")
    s = lax.axis_index("samp")
    x, core, odd = s // 2, s % 2, v % 2
    active = (core == odd).astype(jnp.int32)

    def at(var, samp):
        return var * n_samp + samp

    def active_on(var, samp):
        return var % 2 == samp % 2

    def send(value, pairs):
        return lax.ppermute(value, AXES, pairs)

    def shape(*dims, dtype=F32):
        return jax.ShapeDtypeStruct(dims, dtype)

    everyone = [(var, samp) for var in range(n_var) for samp in range(n_samp)]
    z_main = [(at(a, b), at(a - 2 if b % 2 == 0 else a + 2, b)) for a, b in everyone
              if 0 <= (a - 2 if b % 2 == 0 else a + 2) < n_var]
    y_main = [(at(a, b), at(a ^ 1, b)) for a, b in everyone if not active_on(a, b)]
    z_step = [(a, b, a + 2 if b % 2 == 0 else a - 2) for a, b in everyone]
    z_cross = [(at(a, b), at(t, b ^ 1)) for a, b, t in z_step if 0 <= t < n_var]
    z_cross_active = [(at(a, b), at(t, b ^ 1)) for a, b, t in z_step if 0 <= t < n_var and active_on(a, b)]
    y_cross = [(at(a, b), at(a ^ 1, b ^ 1)) for a, b in everyone if active_on(a, b)]
    across = [(at(a, b), at(a, b ^ 2)) for a, b in everyone]
    across_active = [(at(a, b), at(a, b ^ 2)) for a, b in everyone if active_on(a, b)]
    sibling = [(at(a, b), at(a, b ^ 1)) for a, b in everyone]

    y_raw = send(dosage, y_main)

    pos = jnp.stack([x, active, core, odd, jnp.int32(samples_all)]).astype(jnp.int32)
    step_rows = min(1024, depth)
    steps = depth // step_rows
    wide = pl.BlockSpec((step_rows, width), lambda k: (k, 0))
    flat = pl.BlockSpec((width, step_rows), lambda k: (0, k))
    whole = lambda *dims: pl.BlockSpec(dims, lambda k: (0,) * len(dims))

    bytes_block, tile_flops = 2 * depth * width, 2 * depth * width * width

    def call(kernel, name, grid, in_specs, out_specs, out_shape, scratch=(), flops=0, moved=0):
        return pl.pallas_call(
            kernel, grid=grid, in_specs=in_specs, out_specs=out_specs, out_shape=out_shape, scratch_shapes=scratch,
            compiler_params=SOME, name=name,
            cost_estimate=pl.CostEstimate(flops=flops, bytes_accessed=moved, transcendentals=0))

    part_block = pl.BlockSpec((step_rows, half), lambda k: (k, 0))
    chunk_0 = call(lambda *refs: cut_kernel(0, *refs), "first_chunk", (steps,), [wide], part_block,
                   shape(depth, half, dtype=BF16), moved=bytes_block)(dosage)
    w_raw_0 = send(chunk_0, z_main)
    chunk_1, local = call(lambda *refs: local_kernel(steps, *refs), "second_chunk_and_local_stats", (steps,), [wide],
                          [part_block, whole(2, width)], [shape(depth, half, dtype=BF16), shape(2, width)],
                          [pltpu.VMEM((1, width), F32)] + [pltpu.VMEM((8, width), F32)] * 2,
                          5 * depth * width, 2 * bytes_block)(lax.optimization_barrier((dosage, chunk_0))[0])
    others = [send(local, [(at(a, b), at(a, b ^ flip)) for a, b in everyone]) for flip in (1, 2, 3)]
    stat, chunked = call(stat_kernel, "stats", (), [SMEM] * 3 + [VMEM] * 4, [VMEM] * 2, [shape(4, width)] * 2)(
        pos, live_counts, pair_offsets, local, *others)
    chunk_1, stat = lax.optimization_barrier((chunk_1, stat))
    w_raw_1 = send(chunk_1, z_main)
    w_stat, y_stat = send(chunked, z_cross), send(stat, y_cross)

    turned, diag_keep, diag_send = call(
        own_kernel, "own_tile", (steps,), [SMEM, wide, whole(4, width)],
        [flat, whole(2, strip, width), whole(2, strip, width)],
        [shape(width, depth, dtype=BF16), shape(2, strip, width), shape(2, strip, width)],
        [pltpu.VMEM((width, width), F32)], tile_flops, 2 * bytes_block)(pos, dosage, stat)
    diag_mine, diag_other = call(diag_kernel, "own_tile_strips", (), [SMEM, VMEM, VMEM], [VMEM] * 2, [shape(strip, width)] * 2)(
        pos, diag_keep, send(diag_send, sibling))
    diag_got = send(diag_other, across)

    def far(part, w_raw):
        stats = pl.BlockSpec((4, half), lambda k: (0, part))
        return call(
            far_kernel, f"far_tile_{part}", (steps,), [SMEM, flat, part_block, stats, stats],
            [whole(3, half, strip)] * 2 + [part_block],
            [shape(3, half, strip)] * 2 + [shape(depth, half, dtype=BF16)],
            [pltpu.VMEM((width, half), F32)], tile_flops // 2, 2 * bytes_block)(pos, turned, w_raw, chunked, w_stat)

    def far_strips(part, keep, got):
        return call(lambda *refs: far_strips_kernel(part, *refs), f"far_strips_{part}", (), [SMEM] + [VMEM] * 2, [VMEM] * 2,
                    [shape(half, half), shape(strip, width)])(pos, keep, got)

    def near_strips(name, keep, got):
        return call(near_strips_kernel, name, (), [SMEM] + [VMEM] * 2, [VMEM] * 2, [shape(half, width)] * 2)(pos, keep, got)

    stats, quarters = whole(4, width), [whole(3, half, half)] * 2
    keep_c0, send_c0, w_0 = far(0, w_raw_0)
    send_c0, diag_got = lax.optimization_barrier((send_c0, diag_got))
    got_c0 = send(send_c0, across)
    keep_b, send_b, y = call(
        near_kernel, "near_tile", (steps,), [SMEM, flat, wide, stats, stats], quarters + [flat],
        [shape(3, half, half)] * 2 + [shape(width, depth, dtype=BF16)],
        [pltpu.VMEM((width, width), F32)], tile_flops, 3 * bytes_block)(pos, turned, y_raw, stat, y_stat)
    send_b, got_c0 = lax.optimization_barrier((send_b, got_c0))
    w_raw_1, send_b = lax.optimization_barrier((w_raw_1, send_b))
    got_b = send(send_b, across_active)
    held_c0, to_z_c0 = far_strips(0, keep_c0, got_c0)
    keep_c1, send_c1, w_1 = far(1, w_raw_1)
    keep_d, send_d = call(
        cross_kernel, "cross_tile", (steps,), [SMEM, flat, part_block, part_block, stats, stats], quarters,
        [shape(3, half, half)] * 2, [pltpu.VMEM((width, half), F32)] * 2 + [pltpu.VMEM((width, width), F32)],
        tile_flops, 2 * bytes_block)(pos, y, w_0, w_1, y_stat, w_stat)
    send_d, send_c1, to_z_c0, got_b = lax.optimization_barrier((send_d, send_c1, to_z_c0, got_b))
    from_z_c0 = send(to_z_c0, z_cross)
    got_d = send(send_d, across_active)
    got_c1 = send(send_c1, across)
    held_b, to_y_b = near_strips("near_strips", keep_b, got_b)
    from_y_b = send(to_y_b, y_cross)
    to_y_d, to_z_d = near_strips("cross_strips", keep_d, got_d)
    from_y_d, from_z_d = send(to_y_d, y_cross), send(to_z_d, z_cross_active)
    held_c1, to_z_c1 = far_strips(1, keep_c1, got_c1)
    from_z_c1 = send(to_z_c1, z_cross)

    mine, sib = call(combine_kernel, "combine", (), [SMEM] + [VMEM] * 8, [VMEM] * 2, [shape(3, strip, width)] * 2)(
        pos, held_b, held_c0, held_c1, from_y_b, from_y_d, from_z_c0, from_z_c1, from_z_d)
    return call(finish_kernel, "finish", (), [SMEM] * 2 + [VMEM] * 4, [VMEM] * 2,
                [shape(1, SLOTS, strip, width, dtype=BF16), shape(1, 2, strip, width, dtype=BF16)])(
        pos, pair_offsets, diag_mine, diag_got, mine, send(sib, sibling))


def solution(mesh):
    in_specs = (P("samp", "var"), P("var", None), P("var"))
    out_specs = (P("var", None, "samp", None), P("var", None, "samp", None))
    return jax.shard_map(body, mesh=mesh, in_specs=in_specs, out_specs=out_specs, check_vma=False)
```

```python
import jax
import jax.numpy as jnp
from jax import lax
from jax.experimental import pallas as pl
from jax.experimental.pallas import tpu as pltpu
from jax.sharding import PartitionSpec as P

SLOTS = 3
AXES = ("var", "samp")
F32 = jnp.float32
BF16 = jnp.bfloat16
VMEM = pl.BlockSpec(memory_space=pltpu.VMEM)
SMEM = pl.BlockSpec(memory_space=pltpu.SMEM)
SOME = pltpu.CompilerParams(vmem_limit_bytes=24 << 20)
HALVES = BF16


def dot(a, b):
    return jnp.dot(a, b, preferred_element_type=F32)


def standardized(raw, stat_ref):
    return ((raw.astype(F32) - stat_ref[0:1, :]) * stat_ref[1:2, :]).astype(BF16)


def local_kernel(steps, x_ref, out_ref, center, total, square):
    step = pl.program_id(0)
    rows, width = x_ref.shape
    group = min(64, rows)

    @pl.when(step == 0)
    def _():
        center[...] = jnp.mean(x_ref[:group, :].astype(F32), axis=0, keepdims=True)
        total[...] = jnp.zeros_like(total)
        square[...] = jnp.zeros_like(square)

    middle = center[...]

    def add(i, sums):
        x = x_ref[pl.ds(pl.multiple_of(i * group, group), group), :].astype(F32) - middle
        x = x.reshape(group // 8, 8, width)
        return sums[0] + jnp.sum(x, axis=0), sums[1] + jnp.sum(x * x, axis=0)

    sums = lax.fori_loop(0, rows // group, add, (total[...], square[...]))
    total[...], square[...] = sums

    @pl.when(step == steps - 1)
    def _():
        count = float(rows * steps)
        shift = jnp.sum(total[...], axis=0, keepdims=True) * (1.0 / count)
        around = jnp.sum(square[...], axis=0, keepdims=True) - shift * shift * count
        out_ref[0:1, :] = middle + shift
        out_ref[1:2, :] = jnp.maximum(around, 0.0)


def stat_kernel(pos_ref, live_ref, offsets_ref, own_ref, sib_ref, far_ref, cross_ref, stat_ref):
    width = own_ref.shape[1]
    samples = pos_ref[4].astype(F32)

    def merged(values):
        return (values[0] + values[1]) + (values[2] + values[3])

    groups = (own_ref, sib_ref, far_ref, cross_ref)
    mean = merged([ref[0:1, :] for ref in groups]) * 0.25
    between = merged([jnp.square(ref[0:1, :] - mean) for ref in groups]) * (samples * 0.25)
    spread = (merged([ref[1:2, :] for ref in groups]) + between) / samples
    live = lax.broadcasted_iota(jnp.int32, (1, width), 1) < live_ref[0]
    stat_ref[0:1, :] = mean
    stat_ref[1:2, :] = jnp.where(live, lax.rsqrt(spread + 1e-05), 0.0)
    for step in (1, 2):
        listed = offsets_ref[0, 0] == step
        for slot in range(1, SLOTS):
            listed = jnp.logical_or(listed, offsets_ref[0, slot] == step)
        stat_ref[1 + step:2 + step, :] = jnp.full((1, width), jnp.where(listed, 1.0, 0.0), F32)


def own_kernel(pos_ref, x_ref, stat_ref, turned_ref, keep_ref, send_ref, acc):
    step = pl.program_id(0)
    z = standardized(x_ref[...], stat_ref)
    zt = z.T
    turned_ref[...] = zt
    part = dot(zt, z)

    @pl.when(step == 0)
    def _():
        acc[...] = part

    @pl.when(step > 0)
    def _():
        acc[...] += part

    @pl.when(step == pl.num_programs(0) - 1)
    def _():
        rows = keep_ref.shape[1]
        for far in range(2):
            for core, out in ((pos_ref[2], keep_ref), (1 - pos_ref[2], send_ref)):
                out[far] = acc[pl.ds(pl.multiple_of((2 * far + core) * rows, rows), rows), :]


def diag_kernel(pos_ref, keep_ref, got_ref, mine_ref, send_ref):
    mine_ref[...] = keep_ref[pos_ref[0]] + got_ref[pos_ref[0]]
    send_ref[...] = keep_ref[1 - pos_ref[0]] + got_ref[1 - pos_ref[0]]


def put_quarters(x, source, keep, send):
    half = keep.shape[-1]
    for out, near in ((keep, x), (send, 1 - x)):
        for index, (row, col) in enumerate(((near, near), (near, 1 - near), (1 - near, near))):
            rows = pl.ds(pl.multiple_of(row * half, half), half)
            cols = pl.ds(pl.multiple_of(col * half, half), half)
            out[index] = source[rows, cols].astype(out.dtype)


def far_kernel(pos_ref, turned_ref, w_ref, stat_ref, wstat_ref, keep_ref, send_ref, w_out, acc):
    step = pl.program_id(0)

    @pl.when(step == 0)
    def _():
        acc[...] = jnp.zeros_like(acc)

    w = standardized(w_ref[...], wstat_ref)
    w_out[...] = w
    acc[...] += dot(turned_ref[...], w)

    @pl.when(step == pl.num_programs(0) - 1)
    def _():
        listed = jnp.where(pos_ref[2] == 0, stat_ref[3:4, :], wstat_ref[3:4, :])
        acc[...] *= listed * (1.0 / pos_ref[4].astype(F32))
        put_quarters(pos_ref[0], acc, keep_ref, send_ref)


def near_kernel(pos_ref, turned_ref, y_ref, w_ref, stat_ref, ystat_ref, wstat_ref, keep_b, send_b, keep_d, send_d, acc_b, acc_d):
    step = pl.program_id(0)

    @pl.when(pos_ref[1] == 1)
    def _():
        @pl.when(step == 0)
        def _():
            acc_b[...] = jnp.zeros_like(acc_b)
            acc_d[...] = jnp.zeros_like(acc_d)

        y = standardized(y_ref[...], ystat_ref)
        acc_b[...] += dot(turned_ref[...], y)
        acc_d[...] += dot(y.T, w_ref[...])

        @pl.when(step == pl.num_programs(0) - 1)
        def _():
            first = pos_ref[2] == 0
            share = 1.0 / pos_ref[4].astype(F32)
            acc_b[...] *= jnp.where(first, stat_ref[2:3, :], ystat_ref[2:3, :]) * share
            acc_d[...] *= jnp.where(first, ystat_ref[2:3, :], wstat_ref[2:3, :]) * share
            put_quarters(pos_ref[0], acc_b, keep_b, send_b)
            put_quarters(pos_ref[0], acc_d, keep_d, send_d)


def add_halves(x, keep, got, rows_out, cols_out):
    half = keep.shape[-1]
    here = pl.ds(pl.multiple_of(x * half, half), half)
    there = pl.ds(pl.multiple_of((1 - x) * half, half), half)
    corner = keep[0] + got[0].astype(F32)
    rows_out[:, here] = corner.astype(rows_out.dtype)
    rows_out[:, there] = (keep[1] + got[1].astype(F32)).astype(rows_out.dtype)
    cols_out[:, here] = corner.T.astype(cols_out.dtype)
    cols_out[:, there] = (keep[2] + got[2].astype(F32)).T.astype(cols_out.dtype)


def far_strips_kernel(pos_ref, keep, got, held, to_z):
    add_halves(pos_ref[0], keep, got, held, to_z)


def near_strips_kernel(pos_ref, keep, got, rows_out, cols_out):
    @pl.when(pos_ref[1] == 1)
    def _():
        add_halves(pos_ref[0], keep, got, rows_out, cols_out)


def combine_kernel(pos_ref, held_b, held_c, from_y_b, from_y_d, from_z_c, from_z_d, mine, sib):
    rows = mine.shape[1]
    for core, out in ((pos_ref[2], mine), (1 - pos_ref[2], sib)):
        at = pl.ds(pl.multiple_of(core * rows, rows), rows)
        out[1] = held_c[at, :] + from_z_c[at, :]

        @pl.when(pos_ref[1] == 1)
        def _():
            out[0] = held_b[at, :] + from_y_b[at, :]
            out[2] = from_y_d[at, :]

        @pl.when(pos_ref[1] == 0)
        def _():
            out[2] = from_z_d[at, :]


def finish_kernel(pos_ref, offsets_ref, diag_mine, diag_got, mine, sib, upper, mirror):
    active = pos_ref[1] == 1
    first_core = pos_ref[2] == 0
    even = pos_ref[3] == 0
    pick = jnp.where
    near = pick(active, mine[0], sib[0])
    far = mine[2] + sib[2]
    upper_1 = pick(even, near, far)
    upper_2 = pick(first_core, mine[1], sib[1])
    mirror[0, 0] = pick(even, far, near).astype(BF16)
    mirror[0, 1] = pick(first_core, sib[1], mine[1]).astype(BF16)
    self_tile = (diag_mine[...] + diag_got[...]) * (1.0 / pos_ref[4].astype(F32))
    for slot in range(SLOTS):
        offset = offsets_ref[0, slot]
        tile = pick(offset == 0, self_tile, pick(offset == 1, upper_1, pick(offset == 2, upper_2, 0.0)))
        upper[0, slot] = tile.astype(BF16)


def body(dosage, pair_offsets, live_counts):
    n_var = lax.axis_size("var")
    n_samp = lax.axis_size("samp")
    depth, width = dosage.shape
    half = width // 2
    strip = width // n_samp
    samples_all = depth * n_samp
    v = lax.axis_index("var")
    s = lax.axis_index("samp")
    x, core, odd = s // 2, s % 2, v % 2
    active = (core == odd).astype(jnp.int32)

    def at(var, samp):
        return var * n_samp + samp

    def active_on(var, samp):
        return var % 2 == samp % 2

    def send(value, pairs):
        return lax.ppermute(value, AXES, pairs)

    def shape(*dims, dtype=F32):
        return jax.ShapeDtypeStruct(dims, dtype)

    everyone = [(var, samp) for var in range(n_var) for samp in range(n_samp)]
    z_main = [(at(a, b), at(a - 2 if b % 2 == 0 else a + 2, b)) for a, b in everyone
              if 0 <= (a - 2 if b % 2 == 0 else a + 2) < n_var]
    y_main = [(at(a, b), at(a ^ 1, b)) for a, b in everyone if not active_on(a, b)]
    z_step = [(a, b, a + 2 if b % 2 == 0 else a - 2) for a, b in everyone]
    z_cross = [(at(a, b), at(t, b ^ 1)) for a, b, t in z_step if 0 <= t < n_var]
    z_cross_active = [(at(a, b), at(t, b ^ 1)) for a, b, t in z_step if 0 <= t < n_var and active_on(a, b)]
    y_cross = [(at(a, b), at(a ^ 1, b ^ 1)) for a, b in everyone if active_on(a, b)]
    across = [(at(a, b), at(a, b ^ 2)) for a, b in everyone]
    across_active = [(at(a, b), at(a, b ^ 2)) for a, b in everyone if active_on(a, b)]
    sibling = [(at(a, b), at(a, b ^ 1)) for a, b in everyone]

    w_raw, y_raw = send(dosage, z_main), send(dosage, y_main)

    pos = jnp.stack([x, active, core, odd, jnp.int32(samples_all)]).astype(jnp.int32)
    step_rows = min(1024, depth)
    steps = depth // step_rows
    wide = pl.BlockSpec((step_rows, width), lambda k: (k, 0))
    flat = pl.BlockSpec((width, step_rows), lambda k: (0, k))
    whole = lambda *dims: pl.BlockSpec(dims, lambda k: (0,) * len(dims))

    def call(kernel, name, grid, in_specs, out_specs, out_shape, scratch=(), flops=0, moved=0):
        return pl.pallas_call(
            kernel, grid=grid, in_specs=in_specs, out_specs=out_specs, out_shape=out_shape, scratch_shapes=scratch,
            compiler_params=SOME, name=name,
            cost_estimate=pl.CostEstimate(flops=flops, bytes_accessed=moved, transcendentals=0))

    bytes_block, tile_flops = 2 * depth * width, 2 * depth * width * width
    local = call(lambda *refs: local_kernel(steps, *refs), "local_stats", (steps,), [wide], whole(2, width), shape(2, width),
                 [pltpu.VMEM((1, width), F32)] + [pltpu.VMEM((8, width), F32)] * 2, 5 * depth * width, bytes_block)(dosage)
    others = [send(local, [(at(a, b), at(a, b ^ flip)) for a, b in everyone]) for flip in (1, 2, 3)]
    stat = call(stat_kernel, "stats", (), [SMEM] * 3 + [VMEM] * 4, VMEM, shape(4, width))(
        pos, live_counts, pair_offsets, local, *others)
    w_stat, y_stat = send(stat, z_cross), send(stat, y_cross)

    turned, diag_keep, diag_send = call(
        own_kernel, "own_tile", (steps,), [SMEM, wide, whole(4, width)],
        [flat, whole(2, strip, width), whole(2, strip, width)],
        [shape(width, depth, dtype=BF16), shape(2, strip, width), shape(2, strip, width)],
        [pltpu.VMEM((width, width), F32)], tile_flops, 2 * bytes_block)(pos, dosage, stat)
    diag_mine, diag_other = call(diag_kernel, "own_tile_strips", (), [SMEM, VMEM, VMEM], [VMEM] * 2, [shape(strip, width)] * 2)(
        pos, diag_keep, send(diag_send, sibling))
    diag_got = send(diag_other, across)

    keep_c, send_c, w = call(
        far_kernel, "far_tile", (steps,), [SMEM, flat, wide, whole(4, width), whole(4, width)],
        [whole(3, half, half)] * 2 + [wide],
        [shape(3, half, half), shape(3, half, half, dtype=HALVES), shape(depth, width, dtype=BF16)],
        [pltpu.VMEM((width, width), F32)], tile_flops, 3 * bytes_block)(pos, turned, w_raw, stat, w_stat)
    send_c, diag_got = lax.optimization_barrier((send_c, diag_got))
    got_c = send(send_c, across)

    keep_b, send_b, keep_d, send_d = call(
        near_kernel, "near_tiles", (steps,), [SMEM, flat, wide, wide] + [whole(4, width)] * 3,
        [whole(3, half, half)] * 4, [shape(3, half, half, dtype=kind) for kind in (F32, HALVES)] * 2,
        [pltpu.VMEM((width, width), F32)] * 2, 2 * tile_flops, 3 * bytes_block)(pos, turned, y_raw, w, stat, y_stat, w_stat)
    got_b = send(send_b, across_active)
    send_d, got_c = lax.optimization_barrier((send_d, got_c))
    got_d = send(send_d, across_active)

    held_c, to_z_c = call(far_strips_kernel, "far_strips", (), [SMEM] + [VMEM] * 2, [VMEM] * 2,
                          [shape(half, width)] * 2)(pos, keep_c, got_c)
    from_z_c = send(to_z_c, z_cross)

    def near_strips(name, keep, got):
        return call(near_strips_kernel, name, (), [SMEM] + [VMEM] * 2, [VMEM] * 2, [shape(half, width)] * 2)(pos, keep, got)

    held_b, to_y_b = near_strips("near_strips", keep_b, got_b)
    from_y_b = send(to_y_b, y_cross)
    got_d, to_y_b = lax.optimization_barrier((got_d, to_y_b))
    to_y_d, to_z_d = near_strips("cross_strips", keep_d, got_d)
    from_y_d, from_z_d = send(to_y_d, y_cross), send(to_z_d, z_cross_active)

    mine, sib = call(combine_kernel, "combine", (), [SMEM] + [VMEM] * 6, [VMEM] * 2, [shape(3, strip, width)] * 2)(
        pos, held_b, held_c, from_y_b, from_y_d, from_z_c, from_z_d)
    return call(finish_kernel, "finish", (), [SMEM] * 2 + [VMEM] * 4, [VMEM] * 2,
                [shape(1, SLOTS, strip, width, dtype=BF16), shape(1, 2, strip, width, dtype=BF16)])(
        pos, pair_offsets, diag_mine, diag_got, mine, send(sib, sibling))


def solution(mesh):
    in_specs = (P("samp", "var"), P("var", None), P("var"))
    out_specs = (P("var", None, "samp", None), P("var", None, "samp", None))
    return jax.shard_map(body, mesh=mesh, in_specs=in_specs, out_specs=out_specs, check_vma=False)
```

```python
import jax
import jax.numpy as jnp
from jax import lax
from jax.experimental import pallas as pl
from jax.experimental.pallas import tpu as pltpu
from jax.sharding import PartitionSpec as P

SLOTS = 3
AXES = ("var", "samp")
F32 = jnp.float32
BF16 = jnp.bfloat16
VMEM = pl.BlockSpec(memory_space=pltpu.VMEM)
SMEM = pl.BlockSpec(memory_space=pltpu.SMEM)
SOME = pltpu.CompilerParams(vmem_limit_bytes=24 << 20)
HALVES = BF16


def dot(a, b):
    return jnp.dot(a, b, preferred_element_type=F32)


def standardized(raw, stat_ref):
    return ((raw.astype(F32) - stat_ref[0:1, :]) * stat_ref[1:2, :]).astype(BF16)


def local_kernel(steps, x_ref, out_ref, center, total, square):
    step = pl.program_id(0)
    rows, width = x_ref.shape
    group = min(64, rows)

    @pl.when(step == 0)
    def _():
        center[...] = jnp.mean(x_ref[:group, :].astype(F32), axis=0, keepdims=True)
        total[...] = jnp.zeros_like(total)
        square[...] = jnp.zeros_like(square)

    middle = center[...]

    def add(i, sums):
        x = x_ref[pl.ds(pl.multiple_of(i * group, group), group), :].astype(F32) - middle
        x = x.reshape(group // 8, 8, width)
        return sums[0] + jnp.sum(x, axis=0), sums[1] + jnp.sum(x * x, axis=0)

    sums = lax.fori_loop(0, rows // group, add, (total[...], square[...]))
    total[...], square[...] = sums

    @pl.when(step == steps - 1)
    def _():
        count = float(rows * steps)
        shift = jnp.sum(total[...], axis=0, keepdims=True) * (1.0 / count)
        around = jnp.sum(square[...], axis=0, keepdims=True) - shift * shift * count
        out_ref[0:1, :] = middle + shift
        out_ref[1:2, :] = jnp.maximum(around, 0.0)


def stat_kernel(pos_ref, live_ref, offsets_ref, own_ref, sib_ref, far_ref, cross_ref, stat_ref):
    width = own_ref.shape[1]
    samples = pos_ref[4].astype(F32)

    def merged(values):
        return (values[0] + values[1]) + (values[2] + values[3])

    groups = (own_ref, sib_ref, far_ref, cross_ref)
    mean = merged([ref[0:1, :] for ref in groups]) * 0.25
    between = merged([jnp.square(ref[0:1, :] - mean) for ref in groups]) * (samples * 0.25)
    spread = (merged([ref[1:2, :] for ref in groups]) + between) / samples
    live = lax.broadcasted_iota(jnp.int32, (1, width), 1) < live_ref[0]
    stat_ref[0:1, :] = mean
    stat_ref[1:2, :] = jnp.where(live, lax.rsqrt(spread + 1e-05), 0.0)
    for step in (1, 2):
        listed = offsets_ref[0, 0] == step
        for slot in range(1, SLOTS):
            listed = jnp.logical_or(listed, offsets_ref[0, slot] == step)
        stat_ref[1 + step:2 + step, :] = jnp.full((1, width), jnp.where(listed, 1.0, 0.0), F32)


def own_kernel(pos_ref, x_ref, stat_ref, turned_ref, keep_ref, send_ref, acc):
    step = pl.program_id(0)
    z = standardized(x_ref[...], stat_ref)
    zt = z.T
    turned_ref[...] = zt
    part = dot(zt, z)

    @pl.when(step == 0)
    def _():
        acc[...] = part

    @pl.when(step > 0)
    def _():
        acc[...] += part

    @pl.when(step == pl.num_programs(0) - 1)
    def _():
        rows = keep_ref.shape[1]
        for far in range(2):
            for core, out in ((pos_ref[2], keep_ref), (1 - pos_ref[2], send_ref)):
                out[far] = acc[pl.ds(pl.multiple_of((2 * far + core) * rows, rows), rows), :]


def diag_kernel(pos_ref, keep_ref, got_ref, mine_ref, send_ref):
    mine_ref[...] = keep_ref[pos_ref[0]] + got_ref[pos_ref[0]]
    send_ref[...] = keep_ref[1 - pos_ref[0]] + got_ref[1 - pos_ref[0]]


def put_quarters(x, source, keep, send):
    half = keep.shape[-1]
    for out, near in ((keep, x), (send, 1 - x)):
        for index, (row, col) in enumerate(((near, near), (near, 1 - near), (1 - near, near))):
            rows = pl.ds(pl.multiple_of(row * half, half), half)
            cols = pl.ds(pl.multiple_of(col * half, half), half)
            out[index] = source[rows, cols].astype(out.dtype)


def fetched(source, parts, sems):
    rows = parts.shape[1]
    copies = [pltpu.make_async_copy(source.at[pl.ds(k * rows, rows), :], parts.at[k], sems.at[k])
              for k in range(parts.shape[0])]
    for copy in copies:
        copy.start()
    return [(slice(k * rows, (k + 1) * rows), copy.wait) for k, copy in enumerate(copies)]


def far_kernel(pos_ref, turned_ref, w_ref, stat_ref, wstat_ref, keep_ref, send_ref, w_out, acc, parts, sems):
    for k, (rows, wait) in enumerate(fetched(w_ref, parts, sems)):
        wait()
        w = standardized(parts[k], wstat_ref)
        w_out[rows, :] = w
        part = dot(turned_ref[:, rows], w)
        acc[...] = part if k == 0 else acc[...] + part
    listed = jnp.where(pos_ref[2] == 0, stat_ref[3:4, :], wstat_ref[3:4, :])
    acc[...] *= listed * (1.0 / pos_ref[4].astype(F32))
    put_quarters(pos_ref[0], acc, keep_ref, send_ref)


def near_kernel(pos_ref, turned_ref, y_ref, w_ref, stat_ref, ystat_ref, wstat_ref, keep_b, send_b, keep_d, send_d,
                acc_b, acc_d, parts, sems):
    @pl.when(pos_ref[1] == 1)
    def _():
        for k, (rows, wait) in enumerate(fetched(y_ref, parts, sems)):
            wait()
            y = standardized(parts[k], ystat_ref)
            part_b, part_d = dot(turned_ref[:, rows], y), dot(y.T, w_ref[rows, :])
            acc_b[...] = part_b if k == 0 else acc_b[...] + part_b
            acc_d[...] = part_d if k == 0 else acc_d[...] + part_d
        first = pos_ref[2] == 0
        share = 1.0 / pos_ref[4].astype(F32)
        acc_b[...] *= jnp.where(first, stat_ref[2:3, :], ystat_ref[2:3, :]) * share
        acc_d[...] *= jnp.where(first, ystat_ref[2:3, :], wstat_ref[2:3, :]) * share
        put_quarters(pos_ref[0], acc_b, keep_b, send_b)
        put_quarters(pos_ref[0], acc_d, keep_d, send_d)


def add_halves(x, keep, got, rows_out, cols_out):
    half = keep.shape[-1]
    here = pl.ds(pl.multiple_of(x * half, half), half)
    there = pl.ds(pl.multiple_of((1 - x) * half, half), half)
    corner = keep[0] + got[0].astype(F32)
    rows_out[:, here] = corner.astype(rows_out.dtype)
    rows_out[:, there] = (keep[1] + got[1].astype(F32)).astype(rows_out.dtype)
    cols_out[:, here] = corner.T.astype(cols_out.dtype)
    cols_out[:, there] = (keep[2] + got[2].astype(F32)).T.astype(cols_out.dtype)


def far_strips_kernel(pos_ref, keep, got, held, to_z):
    add_halves(pos_ref[0], keep, got, held, to_z)


def near_strips_kernel(pos_ref, keep, got, rows_out, cols_out):
    @pl.when(pos_ref[1] == 1)
    def _():
        add_halves(pos_ref[0], keep, got, rows_out, cols_out)


def combine_kernel(pos_ref, held_b, held_c, from_y_b, from_y_d, from_z_c, from_z_d, mine, sib):
    rows = mine.shape[1]
    for core, out in ((pos_ref[2], mine), (1 - pos_ref[2], sib)):
        at = pl.ds(pl.multiple_of(core * rows, rows), rows)
        out[1] = held_c[at, :] + from_z_c[at, :]

        @pl.when(pos_ref[1] == 1)
        def _():
            out[0] = held_b[at, :] + from_y_b[at, :]
            out[2] = from_y_d[at, :]

        @pl.when(pos_ref[1] == 0)
        def _():
            out[2] = from_z_d[at, :]


def finish_kernel(pos_ref, offsets_ref, diag_mine, diag_got, mine, sib, upper, mirror):
    active = pos_ref[1] == 1
    first_core = pos_ref[2] == 0
    even = pos_ref[3] == 0
    pick = jnp.where
    near = pick(active, mine[0], sib[0])
    far = mine[2] + sib[2]
    upper_1 = pick(even, near, far)
    upper_2 = pick(first_core, mine[1], sib[1])
    mirror[0, 0] = pick(even, far, near).astype(BF16)
    mirror[0, 1] = pick(first_core, sib[1], mine[1]).astype(BF16)
    self_tile = (diag_mine[...] + diag_got[...]) * (1.0 / pos_ref[4].astype(F32))
    for slot in range(SLOTS):
        offset = offsets_ref[0, slot]
        tile = pick(offset == 0, self_tile, pick(offset == 1, upper_1, pick(offset == 2, upper_2, 0.0)))
        upper[0, slot] = tile.astype(BF16)


def body(dosage, pair_offsets, live_counts):
    n_var = lax.axis_size("var")
    n_samp = lax.axis_size("samp")
    depth, width = dosage.shape
    half = width // 2
    strip = width // n_samp
    samples_all = depth * n_samp
    v = lax.axis_index("var")
    s = lax.axis_index("samp")
    x, core, odd = s // 2, s % 2, v % 2
    active = (core == odd).astype(jnp.int32)

    def at(var, samp):
        return var * n_samp + samp

    def active_on(var, samp):
        return var % 2 == samp % 2

    def send(value, pairs):
        return lax.ppermute(value, AXES, pairs)

    def shape(*dims, dtype=F32):
        return jax.ShapeDtypeStruct(dims, dtype)

    everyone = [(var, samp) for var in range(n_var) for samp in range(n_samp)]
    z_main = [(at(a, b), at(a - 2 if b % 2 == 0 else a + 2, b)) for a, b in everyone
              if 0 <= (a - 2 if b % 2 == 0 else a + 2) < n_var]
    y_main = [(at(a, b), at(a ^ 1, b)) for a, b in everyone if not active_on(a, b)]
    z_step = [(a, b, a + 2 if b % 2 == 0 else a - 2) for a, b in everyone]
    z_cross = [(at(a, b), at(t, b ^ 1)) for a, b, t in z_step if 0 <= t < n_var]
    z_cross_active = [(at(a, b), at(t, b ^ 1)) for a, b, t in z_step if 0 <= t < n_var and active_on(a, b)]
    y_cross = [(at(a, b), at(a ^ 1, b ^ 1)) for a, b in everyone if active_on(a, b)]
    across = [(at(a, b), at(a, b ^ 2)) for a, b in everyone]
    across_active = [(at(a, b), at(a, b ^ 2)) for a, b in everyone if active_on(a, b)]
    sibling = [(at(a, b), at(a, b ^ 1)) for a, b in everyone]

    w_raw, y_raw = send(dosage, z_main), send(dosage, y_main)

    pos = jnp.stack([x, active, core, odd, jnp.int32(samples_all)]).astype(jnp.int32)
    step_rows = min(1024, depth)
    steps = depth // step_rows
    wide = pl.BlockSpec((step_rows, width), lambda k: (k, 0))
    flat = pl.BlockSpec((width, step_rows), lambda k: (0, k))
    whole = lambda *dims: pl.BlockSpec(dims, lambda k: (0,) * len(dims))

    def call(kernel, name, grid, in_specs, out_specs, out_shape, scratch=(), flops=0, moved=0):
        return pl.pallas_call(
            kernel, grid=grid, in_specs=in_specs, out_specs=out_specs, out_shape=out_shape, scratch_shapes=scratch,
            compiler_params=SOME, name=name,
            cost_estimate=pl.CostEstimate(flops=flops, bytes_accessed=moved, transcendentals=0))

    bytes_block, tile_flops = 2 * depth * width, 2 * depth * width * width
    local = call(lambda *refs: local_kernel(steps, *refs), "local_stats", (steps,), [wide], whole(2, width), shape(2, width),
                 [pltpu.VMEM((1, width), F32)] + [pltpu.VMEM((8, width), F32)] * 2, 5 * depth * width, bytes_block)(dosage)
    others = [send(local, [(at(a, b), at(a, b ^ flip)) for a, b in everyone]) for flip in (1, 2, 3)]
    stat = call(stat_kernel, "stats", (), [SMEM] * 3 + [VMEM] * 4, VMEM, shape(4, width))(
        pos, live_counts, pair_offsets, local, *others)
    w_stat, y_stat = send(stat, z_cross), send(stat, y_cross)

    turned, diag_keep, diag_send = call(
        own_kernel, "own_tile", (steps,), [SMEM, wide, whole(4, width)],
        [flat, whole(2, strip, width), whole(2, strip, width)],
        [shape(width, depth, dtype=BF16), shape(2, strip, width), shape(2, strip, width)],
        [pltpu.VMEM((width, width), F32)], tile_flops, 2 * bytes_block)(pos, dosage, stat)
    diag_mine, diag_other = call(diag_kernel, "own_tile_strips", (), [SMEM, VMEM, VMEM], [VMEM] * 2, [shape(strip, width)] * 2)(
        pos, diag_keep, send(diag_send, sibling))
    diag_got = send(diag_other, across)

    anywhere = pl.BlockSpec(memory_space=pl.ANY)
    parts = [pltpu.VMEM((steps, step_rows, width), BF16), pltpu.SemaphoreType.DMA((steps,))]
    sums = pltpu.VMEM((width, width), F32)
    pair = [shape(3, half, half), shape(3, half, half, dtype=HALVES)]
    keep_c, send_c, w = call(
        far_kernel, "far_tile", (), [SMEM, VMEM, anywhere, VMEM, VMEM], [VMEM] * 3,
        pair + [shape(depth, width, dtype=BF16)], [sums] + parts, tile_flops, 3 * bytes_block)(
        pos, turned, w_raw, stat, w_stat)
    send_c, diag_got = lax.optimization_barrier((send_c, diag_got))
    got_c = send(send_c, across)

    keep_b, send_b, keep_d, send_d = call(
        near_kernel, "near_tiles", (), [SMEM, VMEM, anywhere] + [VMEM] * 4, [VMEM] * 4, pair * 2, [sums] * 2 + parts,
        2 * tile_flops, 3 * bytes_block)(pos, turned, y_raw, w, stat, y_stat, w_stat)
    got_b = send(send_b, across_active)
    send_d, got_c = lax.optimization_barrier((send_d, got_c))
    got_d = send(send_d, across_active)

    held_c, to_z_c = call(far_strips_kernel, "far_strips", (), [SMEM] + [VMEM] * 2, [VMEM] * 2,
                          [shape(half, width)] * 2)(pos, keep_c, got_c)
    from_z_c = send(to_z_c, z_cross)
    got_b, to_z_c = lax.optimization_barrier((got_b, to_z_c))

    def near_strips(name, keep, got):
        return call(near_strips_kernel, name, (), [SMEM] + [VMEM] * 2, [VMEM] * 2, [shape(half, width)] * 2)(pos, keep, got)

    held_b, to_y_b = near_strips("near_strips", keep_b, got_b)
    from_y_b = send(to_y_b, y_cross)
    got_d, to_y_b = lax.optimization_barrier((got_d, to_y_b))
    to_y_d, to_z_d = near_strips("cross_strips", keep_d, got_d)
    from_y_d, from_z_d = send(to_y_d, y_cross), send(to_z_d, z_cross_active)

    mine, sib = call(combine_kernel, "combine", (), [SMEM] + [VMEM] * 6, [VMEM] * 2, [shape(3, strip, width)] * 2)(
        pos, held_b, held_c, from_y_b, from_y_d, from_z_c, from_z_d)
    return call(finish_kernel, "finish", (), [SMEM] * 2 + [VMEM] * 4, [VMEM] * 2,
                [shape(1, SLOTS, strip, width, dtype=BF16), shape(1, 2, strip, width, dtype=BF16)])(
        pos, pair_offsets, diag_mine, diag_got, mine, send(sib, sibling))


def solution(mesh):
    in_specs = (P("samp", "var"), P("var", None), P("var"))
    out_specs = (P("var", None, "samp", None), P("var", None, "samp", None))
    return jax.shard_map(body, mesh=mesh, in_specs=in_specs, out_specs=out_specs, check_vma=False)
```

```python
import jax
import jax.numpy as jnp
from jax import lax
from jax.experimental import pallas as pl
from jax.experimental.pallas import tpu as pltpu
from jax.sharding import PartitionSpec as P

SLOTS = 3
AXES = ("var", "samp")
F32 = jnp.float32
BF16 = jnp.bfloat16
VMEM = pl.BlockSpec(memory_space=pltpu.VMEM)
SMEM = pl.BlockSpec(memory_space=pltpu.SMEM)
SOME = pltpu.CompilerParams(vmem_limit_bytes=24 << 20)
HALVES = BF16


def dot(a, b):
    return jnp.dot(a, b, preferred_element_type=F32)


def standardized(raw, stat_ref):
    return ((raw.astype(F32) - stat_ref[0:1, :]) * stat_ref[1:2, :]).astype(BF16)


def local_kernel(steps, x_ref, out_ref, center, total, square):
    step = pl.program_id(0)
    rows, width = x_ref.shape
    group = min(64, rows)

    @pl.when(step == 0)
    def _():
        center[...] = jnp.mean(x_ref[:group, :].astype(F32), axis=0, keepdims=True)
        total[...] = jnp.zeros_like(total)
        square[...] = jnp.zeros_like(square)

    middle = center[...]

    def add(i, sums):
        x = x_ref[pl.ds(pl.multiple_of(i * group, group), group), :].astype(F32) - middle
        x = x.reshape(group // 8, 8, width)
        return sums[0] + jnp.sum(x, axis=0), sums[1] + jnp.sum(x * x, axis=0)

    sums = lax.fori_loop(0, rows // group, add, (total[...], square[...]))
    total[...], square[...] = sums

    @pl.when(step == steps - 1)
    def _():
        count = float(rows * steps)
        shift = jnp.sum(total[...], axis=0, keepdims=True) * (1.0 / count)
        around = jnp.sum(square[...], axis=0, keepdims=True) - shift * shift * count
        out_ref[0:1, :] = middle + shift
        out_ref[1:2, :] = jnp.maximum(around, 0.0)


def stat_kernel(pos_ref, live_ref, offsets_ref, own_ref, sib_ref, far_ref, cross_ref, stat_ref):
    width = own_ref.shape[1]
    samples = pos_ref[4].astype(F32)

    def merged(values):
        return (values[0] + values[1]) + (values[2] + values[3])

    groups = (own_ref, sib_ref, far_ref, cross_ref)
    mean = merged([ref[0:1, :] for ref in groups]) * 0.25
    between = merged([jnp.square(ref[0:1, :] - mean) for ref in groups]) * (samples * 0.25)
    spread = (merged([ref[1:2, :] for ref in groups]) + between) / samples
    live = lax.broadcasted_iota(jnp.int32, (1, width), 1) < live_ref[0]
    stat_ref[0:1, :] = mean
    stat_ref[1:2, :] = jnp.where(live, lax.rsqrt(spread + 1e-05), 0.0)
    for step in (1, 2):
        listed = offsets_ref[0, 0] == step
        for slot in range(1, SLOTS):
            listed = jnp.logical_or(listed, offsets_ref[0, slot] == step)
        stat_ref[1 + step:2 + step, :] = jnp.full((1, width), jnp.where(listed, 1.0, 0.0), F32)


def own_kernel(pos_ref, x_ref, stat_ref, turned_ref, keep_ref, send_ref, acc):
    step = pl.program_id(0)
    z = standardized(x_ref[...], stat_ref)
    zt = z.T
    turned_ref[...] = zt
    part = dot(zt, z)

    @pl.when(step == 0)
    def _():
        acc[...] = part

    @pl.when(step > 0)
    def _():
        acc[...] += part

    @pl.when(step == pl.num_programs(0) - 1)
    def _():
        rows = keep_ref.shape[1]
        for far in range(2):
            for core, out in ((pos_ref[2], keep_ref), (1 - pos_ref[2], send_ref)):
                out[far] = acc[pl.ds(pl.multiple_of((2 * far + core) * rows, rows), rows), :]


def diag_kernel(pos_ref, keep_ref, got_ref, mine_ref, send_ref):
    mine_ref[...] = keep_ref[pos_ref[0]] + got_ref[pos_ref[0]]
    send_ref[...] = keep_ref[1 - pos_ref[0]] + got_ref[1 - pos_ref[0]]


def put_quarters(x, source, keep, send):
    half = keep.shape[-1]
    for out, near in ((keep, x), (send, 1 - x)):
        for index, (row, col) in enumerate(((near, near), (near, 1 - near), (1 - near, near))):
            rows = pl.ds(pl.multiple_of(row * half, half), half)
            cols = pl.ds(pl.multiple_of(col * half, half), half)
            out[index] = source[rows, cols].astype(out.dtype)


def fetched(source, parts, sems):
    rows = parts.shape[1]
    copies = [pltpu.make_async_copy(source.at[pl.ds(k * rows, rows), :], parts.at[k], sems.at[k])
              for k in range(parts.shape[0])]
    for copy in copies:
        copy.start()
    return [(slice(k * rows, (k + 1) * rows), copy.wait) for k, copy in enumerate(copies)]


def near_kernel(pos_ref, turned_ref, y_ref, stat_ref, ystat_ref, keep_ref, send_ref, y_out, acc, parts, sems):
    @pl.when(pos_ref[1] == 1)
    def _():
        for k, (rows, wait) in enumerate(fetched(y_ref, parts, sems)):
            wait()
            y = standardized(parts[k], ystat_ref)
            y_out[:, rows] = y.T
            part = dot(turned_ref[:, rows], y)
            acc[...] = part if k == 0 else acc[...] + part
        listed = jnp.where(pos_ref[2] == 0, stat_ref[2:3, :], ystat_ref[2:3, :])
        acc[...] *= listed * (1.0 / pos_ref[4].astype(F32))
        put_quarters(pos_ref[0], acc, keep_ref, send_ref)


def far_kernel(pos_ref, turned_ref, w_ref, y_ref, stat_ref, ystat_ref, wstat_ref, keep_c, send_c, keep_d, send_d,
               acc_c, acc_d, parts, sems):
    first = pos_ref[2] == 0
    share = 1.0 / pos_ref[4].astype(F32)

    def run(with_y):
        for k, (rows, wait) in enumerate(fetched(w_ref, parts, sems)):
            wait()
            w = standardized(parts[k], wstat_ref)
            part = dot(turned_ref[:, rows], w)
            acc_c[...] = part if k == 0 else acc_c[...] + part
            if with_y:
                part = dot(y_ref[:, rows], w)
                acc_d[...] = part if k == 0 else acc_d[...] + part
        acc_c[...] *= jnp.where(first, stat_ref[3:4, :], wstat_ref[3:4, :]) * share
        put_quarters(pos_ref[0], acc_c, keep_c, send_c)
        if with_y:
            acc_d[...] *= jnp.where(first, ystat_ref[2:3, :], wstat_ref[2:3, :]) * share
            put_quarters(pos_ref[0], acc_d, keep_d, send_d)

    for with_y in (True, False):
        @pl.when((pos_ref[1] == 1) == with_y)
        def _():
            run(with_y)


def add_halves(x, keep, got, rows_out, cols_out):
    half = keep.shape[-1]
    here = pl.ds(pl.multiple_of(x * half, half), half)
    there = pl.ds(pl.multiple_of((1 - x) * half, half), half)
    corner = keep[0] + got[0].astype(F32)
    rows_out[:, here] = corner.astype(rows_out.dtype)
    rows_out[:, there] = (keep[1] + got[1].astype(F32)).astype(rows_out.dtype)
    cols_out[:, here] = corner.T.astype(cols_out.dtype)
    cols_out[:, there] = (keep[2] + got[2].astype(F32)).T.astype(cols_out.dtype)


def far_strips_kernel(pos_ref, keep, got, held, to_z):
    add_halves(pos_ref[0], keep, got, held, to_z)


def near_strips_kernel(pos_ref, keep, got, rows_out, cols_out):
    @pl.when(pos_ref[1] == 1)
    def _():
        add_halves(pos_ref[0], keep, got, rows_out, cols_out)


def combine_kernel(pos_ref, held_b, held_c, from_y_b, from_y_d, from_z_c, from_z_d, mine, sib):
    rows = mine.shape[1]
    for core, out in ((pos_ref[2], mine), (1 - pos_ref[2], sib)):
        at = pl.ds(pl.multiple_of(core * rows, rows), rows)
        out[1] = held_c[at, :] + from_z_c[at, :]

        @pl.when(pos_ref[1] == 1)
        def _():
            out[0] = held_b[at, :] + from_y_b[at, :]
            out[2] = from_y_d[at, :]

        @pl.when(pos_ref[1] == 0)
        def _():
            out[2] = from_z_d[at, :]


def finish_kernel(pos_ref, offsets_ref, diag_mine, diag_got, mine, sib, upper, mirror):
    active = pos_ref[1] == 1
    first_core = pos_ref[2] == 0
    even = pos_ref[3] == 0
    pick = jnp.where
    near = pick(active, mine[0], sib[0])
    far = mine[2] + sib[2]
    upper_1 = pick(even, near, far)
    upper_2 = pick(first_core, mine[1], sib[1])
    mirror[0, 0] = pick(even, far, near).astype(BF16)
    mirror[0, 1] = pick(first_core, sib[1], mine[1]).astype(BF16)
    self_tile = (diag_mine[...] + diag_got[...]) * (1.0 / pos_ref[4].astype(F32))
    for slot in range(SLOTS):
        offset = offsets_ref[0, slot]
        tile = pick(offset == 0, self_tile, pick(offset == 1, upper_1, pick(offset == 2, upper_2, 0.0)))
        upper[0, slot] = tile.astype(BF16)


def body(dosage, pair_offsets, live_counts):
    n_var = lax.axis_size("var")
    n_samp = lax.axis_size("samp")
    depth, width = dosage.shape
    half = width // 2
    strip = width // n_samp
    samples_all = depth * n_samp
    v = lax.axis_index("var")
    s = lax.axis_index("samp")
    x, core, odd = s // 2, s % 2, v % 2
    active = (core == odd).astype(jnp.int32)

    def at(var, samp):
        return var * n_samp + samp

    def active_on(var, samp):
        return var % 2 == samp % 2

    def send(value, pairs):
        return lax.ppermute(value, AXES, pairs)

    def shape(*dims, dtype=F32):
        return jax.ShapeDtypeStruct(dims, dtype)

    everyone = [(var, samp) for var in range(n_var) for samp in range(n_samp)]
    z_main = [(at(a, b), at(a - 2 if b % 2 == 0 else a + 2, b)) for a, b in everyone
              if 0 <= (a - 2 if b % 2 == 0 else a + 2) < n_var]
    y_main = [(at(a, b), at(a ^ 1, b)) for a, b in everyone if not active_on(a, b)]
    z_step = [(a, b, a + 2 if b % 2 == 0 else a - 2) for a, b in everyone]
    z_cross = [(at(a, b), at(t, b ^ 1)) for a, b, t in z_step if 0 <= t < n_var]
    z_cross_active = [(at(a, b), at(t, b ^ 1)) for a, b, t in z_step if 0 <= t < n_var and active_on(a, b)]
    y_cross = [(at(a, b), at(a ^ 1, b ^ 1)) for a, b in everyone if active_on(a, b)]
    across = [(at(a, b), at(a, b ^ 2)) for a, b in everyone]
    across_active = [(at(a, b), at(a, b ^ 2)) for a, b in everyone if active_on(a, b)]
    sibling = [(at(a, b), at(a, b ^ 1)) for a, b in everyone]

    y_raw, w_raw = send(dosage, y_main), send(dosage, z_main)

    pos = jnp.stack([x, active, core, odd, jnp.int32(samples_all)]).astype(jnp.int32)
    step_rows = min(1024, depth)
    steps = depth // step_rows
    wide = pl.BlockSpec((step_rows, width), lambda k: (k, 0))
    flat = pl.BlockSpec((width, step_rows), lambda k: (0, k))
    whole = lambda *dims: pl.BlockSpec(dims, lambda k: (0,) * len(dims))

    def call(kernel, name, grid, in_specs, out_specs, out_shape, scratch=(), flops=0, moved=0):
        return pl.pallas_call(
            kernel, grid=grid, in_specs=in_specs, out_specs=out_specs, out_shape=out_shape, scratch_shapes=scratch,
            compiler_params=SOME, name=name,
            cost_estimate=pl.CostEstimate(flops=flops, bytes_accessed=moved, transcendentals=0))

    bytes_block, tile_flops = 2 * depth * width, 2 * depth * width * width
    local = call(lambda *refs: local_kernel(steps, *refs), "local_stats", (steps,), [wide], whole(2, width), shape(2, width),
                 [pltpu.VMEM((1, width), F32)] + [pltpu.VMEM((8, width), F32)] * 2, 5 * depth * width, bytes_block)(dosage)
    others = [send(local, [(at(a, b), at(a, b ^ flip)) for a, b in everyone]) for flip in (1, 2, 3)]
    stat = call(stat_kernel, "stats", (), [SMEM] * 3 + [VMEM] * 4, VMEM, shape(4, width))(
        pos, live_counts, pair_offsets, local, *others)
    w_stat, y_stat = send(stat, z_cross), send(stat, y_cross)

    turned, diag_keep, diag_send = call(
        own_kernel, "own_tile", (steps,), [SMEM, wide, whole(4, width)],
        [flat, whole(2, strip, width), whole(2, strip, width)],
        [shape(width, depth, dtype=BF16), shape(2, strip, width), shape(2, strip, width)],
        [pltpu.VMEM((width, width), F32)], tile_flops, 2 * bytes_block)(pos, dosage, stat)
    diag_mine, diag_other = call(diag_kernel, "own_tile_strips", (), [SMEM, VMEM, VMEM], [VMEM] * 2, [shape(strip, width)] * 2)(
        pos, diag_keep, send(diag_send, sibling))
    diag_got = send(diag_other, across)

    anywhere = pl.BlockSpec(memory_space=pl.ANY)
    parts = [pltpu.VMEM((steps, step_rows, width), BF16), pltpu.SemaphoreType.DMA((steps,))]
    sums = pltpu.VMEM((width, width), F32)
    pair = [shape(3, half, half), shape(3, half, half, dtype=HALVES)]
    keep_b, send_b, y = call(
        near_kernel, "near_tile", (), [SMEM, VMEM, anywhere, VMEM, VMEM], [VMEM] * 3,
        pair + [shape(width, depth, dtype=BF16)], [sums] + parts, tile_flops, 3 * bytes_block)(
        pos, turned, y_raw, stat, y_stat)
    send_b, diag_got = lax.optimization_barrier((send_b, diag_got))
    got_b = send(send_b, across_active)
    keep_c, send_c, keep_d, send_d = call(
        far_kernel, "far_tiles", (), [SMEM, VMEM, anywhere] + [VMEM] * 4, [VMEM] * 4, pair * 2, [sums] * 2 + parts,
        2 * tile_flops, 3 * bytes_block)(pos, turned, w_raw, y, stat, y_stat, w_stat)
    send_d, got_b = lax.optimization_barrier((send_d, got_b))
    got_d, got_c = send(send_d, across_active), send(send_c, across)

    def near_strips(name, keep, got):
        return call(near_strips_kernel, name, (), [SMEM] + [VMEM] * 2, [VMEM] * 2, [shape(half, width)] * 2)(pos, keep, got)

    held_b, to_y_b = near_strips("near_strips", keep_b, got_b)
    from_y_b = send(to_y_b, y_cross)
    got_d, to_y_b = lax.optimization_barrier((got_d, to_y_b))
    to_y_d, to_z_d = near_strips("cross_strips", keep_d, got_d)
    from_y_d, from_z_d = send(to_y_d, y_cross), send(to_z_d, z_cross_active)
    got_c, to_y_d, to_z_d = lax.optimization_barrier((got_c, to_y_d, to_z_d))
    held_c, to_z_c = call(far_strips_kernel, "far_strips", (), [SMEM] + [VMEM] * 2, [VMEM] * 2,
                          [shape(half, width)] * 2)(pos, keep_c, got_c)
    to_z_c, from_z_d = lax.optimization_barrier((to_z_c, from_z_d))
    from_z_c = send(to_z_c, z_cross)

    mine, sib = call(combine_kernel, "combine", (), [SMEM] + [VMEM] * 6, [VMEM] * 2, [shape(3, strip, width)] * 2)(
        pos, held_b, held_c, from_y_b, from_y_d, from_z_c, from_z_d)
    return call(finish_kernel, "finish", (), [SMEM] * 2 + [VMEM] * 4, [VMEM] * 2,
                [shape(1, SLOTS, strip, width, dtype=BF16), shape(1, 2, strip, width, dtype=BF16)])(
        pos, pair_offsets, diag_mine, diag_got, mine, send(sib, sibling))


def solution(mesh):
    in_specs = (P("samp", "var"), P("var", None), P("var"))
    out_specs = (P("var", None, "samp", None), P("var", None, "samp", None))
    return jax.shard_map(body, mesh=mesh, in_specs=in_specs, out_specs=out_specs, check_vma=False)
```

```python
import jax
import jax.numpy as jnp
from jax import lax
from jax.experimental import pallas as pl
from jax.experimental.pallas import tpu as pltpu
from jax.sharding import PartitionSpec as P

SLOTS = 3
AXES = ("var", "samp")
F32 = jnp.float32
BF16 = jnp.bfloat16
VMEM = pl.BlockSpec(memory_space=pltpu.VMEM)
SMEM = pl.BlockSpec(memory_space=pltpu.SMEM)
SOME = pltpu.CompilerParams(vmem_limit_bytes=24 << 20)
HALVES = BF16


def dot(a, b):
    return jnp.dot(a, b, preferred_element_type=F32)


def standardized(raw, stat_ref):
    return ((raw.astype(F32) - stat_ref[0:1, :]) * stat_ref[1:2, :]).astype(BF16)


def local_kernel(steps, x_ref, out_ref, center, total, square):
    step = pl.program_id(0)
    rows, width = x_ref.shape
    group = min(64, rows)

    @pl.when(step == 0)
    def _():
        center[...] = jnp.mean(x_ref[:group, :].astype(F32), axis=0, keepdims=True)
        total[...] = jnp.zeros_like(total)
        square[...] = jnp.zeros_like(square)

    middle = center[...]

    def add(i, sums):
        x = x_ref[pl.ds(pl.multiple_of(i * group, group), group), :].astype(F32) - middle
        x = x.reshape(group // 8, 8, width)
        return sums[0] + jnp.sum(x, axis=0), sums[1] + jnp.sum(x * x, axis=0)

    sums = lax.fori_loop(0, rows // group, add, (total[...], square[...]))
    total[...], square[...] = sums

    @pl.when(step == steps - 1)
    def _():
        count = float(rows * steps)
        shift = jnp.sum(total[...], axis=0, keepdims=True) * (1.0 / count)
        around = jnp.sum(square[...], axis=0, keepdims=True) - shift * shift * count
        out_ref[0:1, :] = middle + shift
        out_ref[1:2, :] = jnp.maximum(around, 0.0)


def stat_kernel(pos_ref, live_ref, offsets_ref, own_ref, sib_ref, far_ref, cross_ref, stat_ref):
    width = own_ref.shape[1]
    samples = pos_ref[4].astype(F32)

    def merged(values):
        return (values[0] + values[1]) + (values[2] + values[3])

    groups = (own_ref, sib_ref, far_ref, cross_ref)
    mean = merged([ref[0:1, :] for ref in groups]) * 0.25
    between = merged([jnp.square(ref[0:1, :] - mean) for ref in groups]) * (samples * 0.25)
    spread = (merged([ref[1:2, :] for ref in groups]) + between) / samples
    live = lax.broadcasted_iota(jnp.int32, (1, width), 1) < live_ref[0]
    stat_ref[0:1, :] = mean
    stat_ref[1:2, :] = jnp.where(live, lax.rsqrt(spread + 1e-05), 0.0)
    for step in (1, 2):
        listed = offsets_ref[0, 0] == step
        for slot in range(1, SLOTS):
            listed = jnp.logical_or(listed, offsets_ref[0, slot] == step)
        stat_ref[1 + step:2 + step, :] = jnp.full((1, width), jnp.where(listed, 1.0, 0.0), F32)


def own_kernel(pos_ref, x_ref, stat_ref, turned_ref, keep_ref, send_ref, acc):
    step = pl.program_id(0)
    z = standardized(x_ref[...], stat_ref)
    zt = z.T
    turned_ref[...] = zt
    part = dot(zt, z)

    @pl.when(step == 0)
    def _():
        acc[...] = part

    @pl.when(step > 0)
    def _():
        acc[...] += part

    @pl.when(step == pl.num_programs(0) - 1)
    def _():
        rows = keep_ref.shape[1]
        for far in range(2):
            for core, out in ((pos_ref[2], keep_ref), (1 - pos_ref[2], send_ref)):
                out[far] = acc[pl.ds(pl.multiple_of((2 * far + core) * rows, rows), rows), :]


def diag_kernel(pos_ref, keep_ref, got_ref, mine_ref, send_ref):
    mine_ref[...] = keep_ref[pos_ref[0]] + got_ref[pos_ref[0]]
    send_ref[...] = keep_ref[1 - pos_ref[0]] + got_ref[1 - pos_ref[0]]


def put_quarters(x, source, keep, send):
    half = keep.shape[-1]
    for out, near in ((keep, x), (send, 1 - x)):
        for index, (row, col) in enumerate(((near, near), (near, 1 - near), (1 - near, near))):
            rows = pl.ds(pl.multiple_of(row * half, half), half)
            cols = pl.ds(pl.multiple_of(col * half, half), half)
            out[index] = source[rows, cols].astype(out.dtype)


def fetched(source, parts, sems):
    rows = parts.shape[1]
    copies = [pltpu.make_async_copy(source.at[pl.ds(k * rows, rows), :], parts.at[k], sems.at[k])
              for k in range(parts.shape[0])]
    for copy in copies:
        copy.start()
    return [(slice(k * rows, (k + 1) * rows), copy.wait) for k, copy in enumerate(copies)]


def far_kernel(last, pos_ref, turned_ref, w_ref, stat_ref, wstat_ref, *refs):
    if last:
        before, keep_ref, send_ref, w_out, acc, parts, sems = refs
    else:
        acc, w_out, parts, sems = refs
    skip = w_ref.shape[0] if last else 0
    for k, (rows, wait) in enumerate(fetched(w_ref, parts, sems)):
        wait()
        w = standardized(parts[k], wstat_ref)
        w_out[rows, :] = w
        part = dot(turned_ref[:, skip + rows.start:skip + rows.stop], w)
        if k == 0:
            acc[...] = before[...] + part if last else part
        else:
            acc[...] += part
    if last:
        listed = jnp.where(pos_ref[2] == 0, stat_ref[3:4, :], wstat_ref[3:4, :])
        acc[...] *= listed * (1.0 / pos_ref[4].astype(F32))
        put_quarters(pos_ref[0], acc, keep_ref, send_ref)


def near_kernel(last, pos_ref, turned_ref, y_ref, w_ref, stat_ref, ystat_ref, wstat_ref, *refs):
    if last:
        before_b, before_d, keep_b, send_b, keep_d, send_d, acc_b, acc_d, parts, sems = refs
    else:
        acc_b, acc_d, parts, sems = refs
    skip = y_ref.shape[0] if last else 0

    @pl.when(pos_ref[1] == 1)
    def _():
        for k, (rows, wait) in enumerate(fetched(y_ref, parts, sems)):
            wait()
            y = standardized(parts[k], ystat_ref)
            part_b = dot(turned_ref[:, skip + rows.start:skip + rows.stop], y)
            part_d = dot(y.T, w_ref[rows, :])
            if k == 0:
                acc_b[...] = before_b[...] + part_b if last else part_b
                acc_d[...] = before_d[...] + part_d if last else part_d
            else:
                acc_b[...] += part_b
                acc_d[...] += part_d
        if last:
            first = pos_ref[2] == 0
            share = 1.0 / pos_ref[4].astype(F32)
            acc_b[...] *= jnp.where(first, stat_ref[2:3, :], ystat_ref[2:3, :]) * share
            acc_d[...] *= jnp.where(first, ystat_ref[2:3, :], wstat_ref[2:3, :]) * share
            put_quarters(pos_ref[0], acc_b, keep_b, send_b)
            put_quarters(pos_ref[0], acc_d, keep_d, send_d)


def add_halves(x, keep, got, rows_out, cols_out):
    half = keep.shape[-1]
    here = pl.ds(pl.multiple_of(x * half, half), half)
    there = pl.ds(pl.multiple_of((1 - x) * half, half), half)
    corner = keep[0] + got[0].astype(F32)
    rows_out[:, here] = corner.astype(rows_out.dtype)
    rows_out[:, there] = (keep[1] + got[1].astype(F32)).astype(rows_out.dtype)
    cols_out[:, here] = corner.T.astype(cols_out.dtype)
    cols_out[:, there] = (keep[2] + got[2].astype(F32)).T.astype(cols_out.dtype)


def far_strips_kernel(pos_ref, keep, got, held, to_z):
    add_halves(pos_ref[0], keep, got, held, to_z)


def near_strips_kernel(pos_ref, keep, got, rows_out, cols_out):
    @pl.when(pos_ref[1] == 1)
    def _():
        add_halves(pos_ref[0], keep, got, rows_out, cols_out)


def combine_kernel(pos_ref, held_b, held_c, from_y_b, from_y_d, from_z_c, from_z_d, mine, sib):
    rows = mine.shape[1]
    for core, out in ((pos_ref[2], mine), (1 - pos_ref[2], sib)):
        at = pl.ds(pl.multiple_of(core * rows, rows), rows)
        out[1] = held_c[at, :] + from_z_c[at, :]

        @pl.when(pos_ref[1] == 1)
        def _():
            out[0] = held_b[at, :] + from_y_b[at, :]
            out[2] = from_y_d[at, :]

        @pl.when(pos_ref[1] == 0)
        def _():
            out[2] = from_z_d[at, :]


def finish_kernel(pos_ref, offsets_ref, diag_mine, diag_got, mine, sib, upper, mirror):
    active = pos_ref[1] == 1
    first_core = pos_ref[2] == 0
    even = pos_ref[3] == 0
    pick = jnp.where
    near = pick(active, mine[0], sib[0])
    far = mine[2] + sib[2]
    upper_1 = pick(even, near, far)
    upper_2 = pick(first_core, mine[1], sib[1])
    mirror[0, 0] = pick(even, far, near).astype(BF16)
    mirror[0, 1] = pick(first_core, sib[1], mine[1]).astype(BF16)
    self_tile = (diag_mine[...] + diag_got[...]) * (1.0 / pos_ref[4].astype(F32))
    for slot in range(SLOTS):
        offset = offsets_ref[0, slot]
        tile = pick(offset == 0, self_tile, pick(offset == 1, upper_1, pick(offset == 2, upper_2, 0.0)))
        upper[0, slot] = tile.astype(BF16)


def body(dosage, pair_offsets, live_counts):
    n_var = lax.axis_size("var")
    n_samp = lax.axis_size("samp")
    depth, width = dosage.shape
    half = width // 2
    strip = width // n_samp
    samples_all = depth * n_samp
    v = lax.axis_index("var")
    s = lax.axis_index("samp")
    x, core, odd = s // 2, s % 2, v % 2
    active = (core == odd).astype(jnp.int32)

    def at(var, samp):
        return var * n_samp + samp

    def active_on(var, samp):
        return var % 2 == samp % 2

    def send(value, pairs):
        return lax.ppermute(value, AXES, pairs)

    def shape(*dims, dtype=F32):
        return jax.ShapeDtypeStruct(dims, dtype)

    everyone = [(var, samp) for var in range(n_var) for samp in range(n_samp)]
    z_main = [(at(a, b), at(a - 2 if b % 2 == 0 else a + 2, b)) for a, b in everyone
              if 0 <= (a - 2 if b % 2 == 0 else a + 2) < n_var]
    y_main = [(at(a, b), at(a ^ 1, b)) for a, b in everyone if not active_on(a, b)]
    z_step = [(a, b, a + 2 if b % 2 == 0 else a - 2) for a, b in everyone]
    z_cross = [(at(a, b), at(t, b ^ 1)) for a, b, t in z_step if 0 <= t < n_var]
    z_cross_active = [(at(a, b), at(t, b ^ 1)) for a, b, t in z_step if 0 <= t < n_var and active_on(a, b)]
    y_cross = [(at(a, b), at(a ^ 1, b ^ 1)) for a, b in everyone if active_on(a, b)]
    across = [(at(a, b), at(a, b ^ 2)) for a, b in everyone]
    across_active = [(at(a, b), at(a, b ^ 2)) for a, b in everyone if active_on(a, b)]
    sibling = [(at(a, b), at(a, b ^ 1)) for a, b in everyone]

    upper_rows = dosage[:depth // 2]
    w_raw, y_raw = send(upper_rows, z_main), send(upper_rows, y_main)

    pos = jnp.stack([x, active, core, odd, jnp.int32(samples_all)]).astype(jnp.int32)
    step_rows = min(1024, depth)
    steps = depth // step_rows
    wide = pl.BlockSpec((step_rows, width), lambda k: (k, 0))
    flat = pl.BlockSpec((width, step_rows), lambda k: (0, k))
    whole = lambda *dims: pl.BlockSpec(dims, lambda k: (0,) * len(dims))

    def call(kernel, name, grid, in_specs, out_specs, out_shape, scratch=(), flops=0, moved=0):
        return pl.pallas_call(
            kernel, grid=grid, in_specs=in_specs, out_specs=out_specs, out_shape=out_shape, scratch_shapes=scratch,
            compiler_params=SOME, name=name,
            cost_estimate=pl.CostEstimate(flops=flops, bytes_accessed=moved, transcendentals=0))

    bytes_block, tile_flops = 2 * depth * width, 2 * depth * width * width
    local = call(lambda *refs: local_kernel(steps, *refs), "local_stats", (steps,), [wide], whole(2, width), shape(2, width),
                 [pltpu.VMEM((1, width), F32)] + [pltpu.VMEM((8, width), F32)] * 2, 5 * depth * width, bytes_block)(dosage)
    below, local = lax.optimization_barrier((dosage, local))
    lower_rows = below[depth // 2:]
    w_last, y_last = send(lower_rows, z_main), send(lower_rows, y_main)
    others = [send(local, [(at(a, b), at(a, b ^ flip)) for a, b in everyone]) for flip in (1, 2, 3)]
    stat = call(stat_kernel, "stats", (), [SMEM] * 3 + [VMEM] * 4, VMEM, shape(4, width))(
        pos, live_counts, pair_offsets, local, *others)
    w_stat, y_stat = send(stat, z_cross), send(stat, y_cross)

    turned, diag_keep, diag_send = call(
        own_kernel, "own_tile", (steps,), [SMEM, wide, whole(4, width)],
        [flat, whole(2, strip, width), whole(2, strip, width)],
        [shape(width, depth, dtype=BF16), shape(2, strip, width), shape(2, strip, width)],
        [pltpu.VMEM((width, width), F32)], tile_flops, 2 * bytes_block)(pos, dosage, stat)
    diag_mine, diag_other = call(diag_kernel, "own_tile_strips", (), [SMEM, VMEM, VMEM], [VMEM] * 2, [shape(strip, width)] * 2)(
        pos, diag_keep, send(diag_send, sibling))
    diag_got = send(diag_other, across)

    anywhere = pl.BlockSpec(memory_space=pl.ANY)
    pieces = max(steps // 2, 1)
    parts = [pltpu.VMEM((pieces, depth // 2 // pieces, width), BF16), pltpu.SemaphoreType.DMA((pieces,))]
    sums, total = pltpu.VMEM((width, width), F32), shape(width, width)
    rows_out = shape(depth // 2, width, dtype=BF16)
    pair = [shape(3, half, half), shape(3, half, half, dtype=HALVES)]
    far_in, near_in = [SMEM, VMEM, anywhere, VMEM, VMEM], [SMEM, VMEM, anywhere] + [VMEM] * 4
    sum_c, w = call(lambda *refs: far_kernel(False, *refs), "far_tile_0", (), far_in, [VMEM] * 2, [total, rows_out],
                    parts, tile_flops // 2, bytes_block)(pos, turned, w_raw, stat, w_stat)
    sum_b, sum_d = call(lambda *refs: near_kernel(False, *refs), "near_tiles_0", (), near_in, [VMEM] * 2, [total] * 2,
                        parts, tile_flops, bytes_block)(pos, turned, y_raw, w, stat, y_stat, w_stat)
    w_last, sum_b = lax.optimization_barrier((w_last, sum_b))
    keep_c, send_c, w = call(
        lambda *refs: far_kernel(True, *refs), "far_tile_1", (), far_in + [VMEM], [VMEM] * 3, pair + [rows_out],
        [sums] + parts, tile_flops // 2, bytes_block)(pos, turned, w_last, stat, w_stat, sum_c)
    send_c, diag_got = lax.optimization_barrier((send_c, diag_got))
    got_c = send(send_c, across)

    keep_b, send_b, keep_d, send_d = call(
        lambda *refs: near_kernel(True, *refs), "near_tiles_1", (), near_in + [VMEM] * 2, [VMEM] * 4, pair * 2,
        [sums] * 2 + parts, tile_flops, bytes_block)(pos, turned, y_last, w, stat, y_stat, w_stat, sum_b, sum_d)
    got_b = send(send_b, across_active)
    send_d, got_c = lax.optimization_barrier((send_d, got_c))
    got_d = send(send_d, across_active)

    held_c, to_z_c = call(far_strips_kernel, "far_strips", (), [SMEM] + [VMEM] * 2, [VMEM] * 2,
                          [shape(half, width)] * 2)(pos, keep_c, got_c)
    from_z_c = send(to_z_c, z_cross)
    got_b, to_z_c = lax.optimization_barrier((got_b, to_z_c))

    def near_strips(name, keep, got):
        return call(near_strips_kernel, name, (), [SMEM] + [VMEM] * 2, [VMEM] * 2, [shape(half, width)] * 2)(pos, keep, got)

    held_b, to_y_b = near_strips("near_strips", keep_b, got_b)
    from_y_b = send(to_y_b, y_cross)
    got_d, to_y_b = lax.optimization_barrier((got_d, to_y_b))
    to_y_d, to_z_d = near_strips("cross_strips", keep_d, got_d)
    from_y_d, from_z_d = send(to_y_d, y_cross), send(to_z_d, z_cross_active)

    mine, sib = call(combine_kernel, "combine", (), [SMEM] + [VMEM] * 6, [VMEM] * 2, [shape(3, strip, width)] * 2)(
        pos, held_b, held_c, from_y_b, from_y_d, from_z_c, from_z_d)
    return call(finish_kernel, "finish", (), [SMEM] * 2 + [VMEM] * 4, [VMEM] * 2,
                [shape(1, SLOTS, strip, width, dtype=BF16), shape(1, 2, strip, width, dtype=BF16)])(
        pos, pair_offsets, diag_mine, diag_got, mine, send(sib, sibling))


def solution(mesh):
    in_specs = (P("samp", "var"), P("var", None), P("var"))
    out_specs = (P("var", None, "samp", None), P("var", None, "samp", None))
    return jax.shard_map(body, mesh=mesh, in_specs=in_specs, out_specs=out_specs, check_vma=False)
```

```python
import jax
import jax.numpy as jnp
from jax import lax
from jax.experimental import pallas as pl
from jax.experimental.pallas import tpu as pltpu
from jax.sharding import PartitionSpec as P

SLOTS = 3
AXES = ("var", "samp")
F32 = jnp.float32
BF16 = jnp.bfloat16
VMEM = pl.BlockSpec(memory_space=pltpu.VMEM)
SMEM = pl.BlockSpec(memory_space=pltpu.SMEM)
SOME = pltpu.CompilerParams(vmem_limit_bytes=24 << 20)
HALVES, CROSS = BF16, BF16


def dot(a, b):
    return jnp.dot(a, b, preferred_element_type=F32)


def standardized(raw, stat_ref):
    return ((raw.astype(F32) - stat_ref[0:1, :]) * stat_ref[1:2, :]).astype(BF16)


def local_kernel(steps, x_ref, out_ref, center, total, square):
    step = pl.program_id(0)
    rows, width = x_ref.shape
    group = min(64, rows)

    @pl.when(step == 0)
    def _():
        center[...] = jnp.mean(x_ref[:group, :].astype(F32), axis=0, keepdims=True)
        total[...] = jnp.zeros_like(total)
        square[...] = jnp.zeros_like(square)

    middle = center[...]

    def add(i, sums):
        x = x_ref[pl.ds(pl.multiple_of(i * group, group), group), :].astype(F32) - middle
        x = x.reshape(group // 8, 8, width)
        return sums[0] + jnp.sum(x, axis=0), sums[1] + jnp.sum(x * x, axis=0)

    sums = lax.fori_loop(0, rows // group, add, (total[...], square[...]))
    total[...], square[...] = sums

    @pl.when(step == steps - 1)
    def _():
        count = float(rows * steps)
        shift = jnp.sum(total[...], axis=0, keepdims=True) * (1.0 / count)
        around = jnp.sum(square[...], axis=0, keepdims=True) - shift * shift * count
        out_ref[0:1, :] = middle + shift
        out_ref[1:2, :] = jnp.maximum(around, 0.0)


def stat_kernel(pos_ref, live_ref, offsets_ref, own_ref, sib_ref, far_ref, cross_ref, stat_ref):
    width = own_ref.shape[1]
    samples = pos_ref[4].astype(F32)

    def merged(values):
        return (values[0] + values[1]) + (values[2] + values[3])

    groups = (own_ref, sib_ref, far_ref, cross_ref)
    mean = merged([ref[0:1, :] for ref in groups]) * 0.25
    between = merged([jnp.square(ref[0:1, :] - mean) for ref in groups]) * (samples * 0.25)
    spread = (merged([ref[1:2, :] for ref in groups]) + between) / samples
    live = lax.broadcasted_iota(jnp.int32, (1, width), 1) < live_ref[0]
    stat_ref[0:1, :] = mean
    stat_ref[1:2, :] = jnp.where(live, lax.rsqrt(spread + 1e-05), 0.0)
    for step in (1, 2):
        listed = offsets_ref[0, 0] == step
        for slot in range(1, SLOTS):
            listed = jnp.logical_or(listed, offsets_ref[0, slot] == step)
        stat_ref[1 + step:2 + step, :] = jnp.full((1, width), jnp.where(listed, 1.0, 0.0), F32)


def own_kernel(pos_ref, x_ref, stat_ref, turned_ref, keep_ref, send_ref, acc):
    step = pl.program_id(0)
    z = standardized(x_ref[...], stat_ref)
    zt = z.T
    turned_ref[...] = zt
    part = dot(zt, z)

    @pl.when(step == 0)
    def _():
        acc[...] = part

    @pl.when(step > 0)
    def _():
        acc[...] += part

    @pl.when(step == pl.num_programs(0) - 1)
    def _():
        rows = keep_ref.shape[1]
        for far in range(2):
            for core, out in ((pos_ref[2], keep_ref), (1 - pos_ref[2], send_ref)):
                out[far] = acc[pl.ds(pl.multiple_of((2 * far + core) * rows, rows), rows), :]


def diag_kernel(pos_ref, keep_ref, got_ref, mine_ref, send_ref):
    mine_ref[...] = keep_ref[pos_ref[0]] + got_ref[pos_ref[0]]
    send_ref[...] = keep_ref[1 - pos_ref[0]] + got_ref[1 - pos_ref[0]]


def put_quarters(x, source, keep, send):
    half = keep.shape[-1]
    for out, near in ((keep, x), (send, 1 - x)):
        for index, (row, col) in enumerate(((near, near), (near, 1 - near), (1 - near, near))):
            rows = pl.ds(pl.multiple_of(row * half, half), half)
            cols = pl.ds(pl.multiple_of(col * half, half), half)
            out[index] = source[rows, cols].astype(out.dtype)


def fetched(source, parts, sems):
    rows = parts.shape[1]
    copies = [pltpu.make_async_copy(source.at[pl.ds(k * rows, rows), :], parts.at[k], sems.at[k])
              for k in range(parts.shape[0])]
    for copy in copies:
        copy.start()
    return [(slice(k * rows, (k + 1) * rows), copy.wait) for k, copy in enumerate(copies)]


def far_kernel(pos_ref, turned_ref, w_ref, stat_ref, wstat_ref, keep_ref, send_ref, w_out, acc, parts, sems):
    for k, (rows, wait) in enumerate(fetched(w_ref, parts, sems)):
        wait()
        w = standardized(parts[k], wstat_ref)
        w_out[rows, :] = w
        part = dot(turned_ref[:, rows], w)
        acc[...] = part if k == 0 else acc[...] + part
    listed = jnp.where(pos_ref[2] == 0, stat_ref[3:4, :], wstat_ref[3:4, :])
    acc[...] *= listed * (1.0 / pos_ref[4].astype(F32))
    put_quarters(pos_ref[0], acc, keep_ref, send_ref)


def near_kernel(pos_ref, turned_ref, y_ref, w_ref, stat_ref, ystat_ref, wstat_ref, keep_b, send_b, keep_d, send_d,
                acc_b, acc_d, parts, sems):
    @pl.when(pos_ref[1] == 1)
    def _():
        for k, (rows, wait) in enumerate(fetched(y_ref, parts, sems)):
            wait()
            y = standardized(parts[k], ystat_ref)
            part_b, part_d = dot(turned_ref[:, rows], y), dot(y.T, w_ref[rows, :])
            acc_b[...] = part_b if k == 0 else acc_b[...] + part_b
            acc_d[...] = part_d if k == 0 else acc_d[...] + part_d
        first = pos_ref[2] == 0
        share = 1.0 / pos_ref[4].astype(F32)
        acc_b[...] *= jnp.where(first, stat_ref[2:3, :], ystat_ref[2:3, :]) * share
        acc_d[...] *= jnp.where(first, ystat_ref[2:3, :], wstat_ref[2:3, :]) * share
        put_quarters(pos_ref[0], acc_b, keep_b, send_b)
        put_quarters(pos_ref[0], acc_d, keep_d, send_d)


def add_halves(x, keep, got, rows_out, cols_out):
    half = keep.shape[-1]
    here = pl.ds(pl.multiple_of(x * half, half), half)
    there = pl.ds(pl.multiple_of((1 - x) * half, half), half)
    corner = keep[0] + got[0].astype(F32)
    rows_out[:, here] = corner.astype(rows_out.dtype)
    rows_out[:, there] = (keep[1] + got[1].astype(F32)).astype(rows_out.dtype)
    cols_out[:, here] = corner.T.astype(cols_out.dtype)
    cols_out[:, there] = (keep[2] + got[2].astype(F32)).T.astype(cols_out.dtype)


def far_strips_kernel(pos_ref, keep, got, held, to_z):
    add_halves(pos_ref[0], keep, got, held, to_z)


def near_strips_kernel(pos_ref, keep, got, rows_out, cols_out):
    @pl.when(pos_ref[1] == 1)
    def _():
        add_halves(pos_ref[0], keep, got, rows_out, cols_out)


def combine_kernel(pos_ref, held_b, held_c, from_y_b, from_y_d, from_z_c, from_z_d, mine, sib):
    rows = mine.shape[1]
    for core, out in ((pos_ref[2], mine), (1 - pos_ref[2], sib)):
        at = pl.ds(pl.multiple_of(core * rows, rows), rows)
        out[1] = held_c[at, :] + from_z_c[at, :]

        @pl.when(pos_ref[1] == 1)
        def _():
            out[0] = held_b[at, :] + from_y_b[at, :]
            out[2] = from_y_d[at, :].astype(F32)

        @pl.when(pos_ref[1] == 0)
        def _():
            out[2] = from_z_d[at, :].astype(F32)


def finish_kernel(pos_ref, offsets_ref, diag_mine, diag_got, mine, sib, upper, mirror):
    active = pos_ref[1] == 1
    first_core = pos_ref[2] == 0
    even = pos_ref[3] == 0
    pick = jnp.where
    near = pick(active, mine[0], sib[0])
    far = mine[2] + sib[2]
    upper_1 = pick(even, near, far)
    upper_2 = pick(first_core, mine[1], sib[1])
    mirror[0, 0] = pick(even, far, near).astype(BF16)
    mirror[0, 1] = pick(first_core, sib[1], mine[1]).astype(BF16)
    self_tile = (diag_mine[...] + diag_got[...]) * (1.0 / pos_ref[4].astype(F32))
    for slot in range(SLOTS):
        offset = offsets_ref[0, slot]
        tile = pick(offset == 0, self_tile, pick(offset == 1, upper_1, pick(offset == 2, upper_2, 0.0)))
        upper[0, slot] = tile.astype(BF16)


def body(dosage, pair_offsets, live_counts):
    n_var = lax.axis_size("var")
    n_samp = lax.axis_size("samp")
    depth, width = dosage.shape
    half = width // 2
    strip = width // n_samp
    samples_all = depth * n_samp
    v = lax.axis_index("var")
    s = lax.axis_index("samp")
    x, core, odd = s // 2, s % 2, v % 2
    active = (core == odd).astype(jnp.int32)

    def at(var, samp):
        return var * n_samp + samp

    def active_on(var, samp):
        return var % 2 == samp % 2

    def send(value, pairs):
        return lax.ppermute(value, AXES, pairs)

    def shape(*dims, dtype=F32):
        return jax.ShapeDtypeStruct(dims, dtype)

    everyone = [(var, samp) for var in range(n_var) for samp in range(n_samp)]
    z_main = [(at(a, b), at(a - 2 if b % 2 == 0 else a + 2, b)) for a, b in everyone
              if 0 <= (a - 2 if b % 2 == 0 else a + 2) < n_var]
    y_main = [(at(a, b), at(a ^ 1, b)) for a, b in everyone if not active_on(a, b)]
    z_step = [(a, b, a + 2 if b % 2 == 0 else a - 2) for a, b in everyone]
    z_cross = [(at(a, b), at(t, b ^ 1)) for a, b, t in z_step if 0 <= t < n_var]
    z_cross_active = [(at(a, b), at(t, b ^ 1)) for a, b, t in z_step if 0 <= t < n_var and active_on(a, b)]
    y_cross = [(at(a, b), at(a ^ 1, b ^ 1)) for a, b in everyone if active_on(a, b)]
    across = [(at(a, b), at(a, b ^ 2)) for a, b in everyone]
    across_active = [(at(a, b), at(a, b ^ 2)) for a, b in everyone if active_on(a, b)]
    sibling = [(at(a, b), at(a, b ^ 1)) for a, b in everyone]

    w_raw, y_raw = send(dosage, z_main), send(dosage, y_main)

    pos = jnp.stack([x, active, core, odd, jnp.int32(samples_all)]).astype(jnp.int32)
    step_rows = min(1024, depth)
    steps = depth // step_rows
    wide = pl.BlockSpec((step_rows, width), lambda k: (k, 0))
    flat = pl.BlockSpec((width, step_rows), lambda k: (0, k))
    whole = lambda *dims: pl.BlockSpec(dims, lambda k: (0,) * len(dims))

    def call(kernel, name, grid, in_specs, out_specs, out_shape, scratch=(), flops=0, moved=0):
        return pl.pallas_call(
            kernel, grid=grid, in_specs=in_specs, out_specs=out_specs, out_shape=out_shape, scratch_shapes=scratch,
            compiler_params=SOME, name=name,
            cost_estimate=pl.CostEstimate(flops=flops, bytes_accessed=moved, transcendentals=0))

    bytes_block, tile_flops = 2 * depth * width, 2 * depth * width * width
    local = call(lambda *refs: local_kernel(steps, *refs), "local_stats", (steps,), [wide], whole(2, width), shape(2, width),
                 [pltpu.VMEM((1, width), F32)] + [pltpu.VMEM((8, width), F32)] * 2, 5 * depth * width, bytes_block)(dosage)
    others = [send(local, [(at(a, b), at(a, b ^ flip)) for a, b in everyone]) for flip in (1, 2, 3)]
    stat = call(stat_kernel, "stats", (), [SMEM] * 3 + [VMEM] * 4, VMEM, shape(4, width))(
        pos, live_counts, pair_offsets, local, *others)
    w_stat, y_stat = send(stat, z_cross), send(stat, y_cross)

    turned, diag_keep, diag_send = call(
        own_kernel, "own_tile", (steps,), [SMEM, wide, whole(4, width)],
        [flat, whole(2, strip, width), whole(2, strip, width)],
        [shape(width, depth, dtype=BF16), shape(2, strip, width), shape(2, strip, width)],
        [pltpu.VMEM((width, width), F32)], tile_flops, 2 * bytes_block)(pos, dosage, stat)
    diag_mine, diag_other = call(diag_kernel, "own_tile_strips", (), [SMEM, VMEM, VMEM], [VMEM] * 2, [shape(strip, width)] * 2)(
        pos, diag_keep, send(diag_send, sibling))
    diag_got = send(diag_other, across)

    anywhere = pl.BlockSpec(memory_space=pl.ANY)
    parts = [pltpu.VMEM((steps, step_rows, width), BF16), pltpu.SemaphoreType.DMA((steps,))]
    sums = pltpu.VMEM((width, width), F32)
    pair = [shape(3, half, half), shape(3, half, half, dtype=HALVES)]
    keep_c, send_c, w = call(
        far_kernel, "far_tile", (), [SMEM, VMEM, anywhere, VMEM, VMEM], [VMEM] * 3,
        pair + [shape(depth, width, dtype=BF16)], [sums] + parts, tile_flops, 3 * bytes_block)(
        pos, turned, w_raw, stat, w_stat)
    send_c, diag_got = lax.optimization_barrier((send_c, diag_got))
    got_c = send(send_c, across)

    keep_b, send_b, keep_d, send_d = call(
        near_kernel, "near_tiles", (), [SMEM, VMEM, anywhere] + [VMEM] * 4, [VMEM] * 4, pair * 2, [sums] * 2 + parts,
        2 * tile_flops, 3 * bytes_block)(pos, turned, y_raw, w, stat, y_stat, w_stat)
    got_b = send(send_b, across_active)
    send_d, got_c = lax.optimization_barrier((send_d, got_c))
    got_d = send(send_d, across_active)

    held_c, to_z_c = call(far_strips_kernel, "far_strips", (), [SMEM] + [VMEM] * 2, [VMEM] * 2,
                          [shape(half, width)] * 2)(pos, keep_c, got_c)
    from_z_c = send(to_z_c, z_cross)
    got_b, to_z_c = lax.optimization_barrier((got_b, to_z_c))

    def near_strips(name, kind, keep, got):
        return call(near_strips_kernel, name, (), [SMEM] + [VMEM] * 2, [VMEM] * 2, [shape(half, width, dtype=kind)] * 2)(
            pos, keep, got)

    held_b, to_y_b = near_strips("near_strips", F32, keep_b, got_b)
    from_y_b = send(to_y_b, y_cross)
    got_d, to_y_b = lax.optimization_barrier((got_d, to_y_b))
    to_y_d, to_z_d = near_strips("cross_strips", CROSS, keep_d, got_d)
    from_y_d, from_z_d = send(to_y_d, y_cross), send(to_z_d, z_cross_active)

    mine, sib = call(combine_kernel, "combine", (), [SMEM] + [VMEM] * 6, [VMEM] * 2, [shape(3, strip, width)] * 2)(
        pos, held_b, held_c, from_y_b, from_y_d, from_z_c, from_z_d)
    return call(finish_kernel, "finish", (), [SMEM] * 2 + [VMEM] * 4, [VMEM] * 2,
                [shape(1, SLOTS, strip, width, dtype=BF16), shape(1, 2, strip, width, dtype=BF16)])(
        pos, pair_offsets, diag_mine, diag_got, mine, send(sib, sibling))


def solution(mesh):
    in_specs = (P("samp", "var"), P("var", None), P("var"))
    out_specs = (P("var", None, "samp", None), P("var", None, "samp", None))
    return jax.shard_map(body, mesh=mesh, in_specs=in_specs, out_specs=out_specs, check_vma=False)
```

```python
import jax
import jax.numpy as jnp
from jax import lax
from jax.experimental import pallas as pl
from jax.experimental.pallas import tpu as pltpu
from jax.sharding import PartitionSpec as P

SLOTS = 3
AXES = ("var", "samp")
F32 = jnp.float32
BF16 = jnp.bfloat16
VMEM = pl.BlockSpec(memory_space=pltpu.VMEM)
SMEM = pl.BlockSpec(memory_space=pltpu.SMEM)
SOME = pltpu.CompilerParams(vmem_limit_bytes=24 << 20)
HALVES, CROSS = BF16, BF16


def dot(a, b):
    return jnp.dot(a, b, preferred_element_type=F32)


def standardized(raw, stat_ref):
    return ((raw.astype(F32) - stat_ref[0:1, :]) * stat_ref[1:2, :]).astype(BF16)


def local_kernel(steps, x_ref, out_ref, center, total, square):
    step = pl.program_id(0)
    rows, width = x_ref.shape
    group = min(64, rows)

    @pl.when(step == 0)
    def _():
        center[...] = jnp.mean(x_ref[:group, :].astype(F32), axis=0, keepdims=True)
        total[...] = jnp.zeros_like(total)
        square[...] = jnp.zeros_like(square)

    middle = center[...]

    def add(i, sums):
        x = x_ref[pl.ds(pl.multiple_of(i * group, group), group), :].astype(F32) - middle
        x = x.reshape(group // 8, 8, width)
        return sums[0] + jnp.sum(x, axis=0), sums[1] + jnp.sum(x * x, axis=0)

    sums = lax.fori_loop(0, rows // group, add, (total[...], square[...]))
    total[...], square[...] = sums

    @pl.when(step == steps - 1)
    def _():
        count = float(rows * steps)
        shift = jnp.sum(total[...], axis=0, keepdims=True) * (1.0 / count)
        around = jnp.sum(square[...], axis=0, keepdims=True) - shift * shift * count
        out_ref[0:1, :] = middle + shift
        out_ref[1:2, :] = jnp.maximum(around, 0.0)


def stat_kernel(pos_ref, live_ref, offsets_ref, own_ref, sib_ref, far_ref, cross_ref, stat_ref):
    width = own_ref.shape[1]
    samples = pos_ref[4].astype(F32)

    def merged(values):
        return (values[0] + values[1]) + (values[2] + values[3])

    groups = (own_ref, sib_ref, far_ref, cross_ref)
    mean = merged([ref[0:1, :] for ref in groups]) * 0.25
    between = merged([jnp.square(ref[0:1, :] - mean) for ref in groups]) * (samples * 0.25)
    spread = (merged([ref[1:2, :] for ref in groups]) + between) / samples
    live = lax.broadcasted_iota(jnp.int32, (1, width), 1) < live_ref[0]
    stat_ref[0:1, :] = mean
    stat_ref[1:2, :] = jnp.where(live, lax.rsqrt(spread + 1e-05), 0.0)
    for step in (1, 2):
        listed = offsets_ref[0, 0] == step
        for slot in range(1, SLOTS):
            listed = jnp.logical_or(listed, offsets_ref[0, slot] == step)
        stat_ref[1 + step:2 + step, :] = jnp.full((1, width), jnp.where(listed, 1.0, 0.0), F32)


def own_kernel(pos_ref, x_ref, stat_ref, turned_ref, keep_ref, send_ref, acc):
    step = pl.program_id(0)
    z = standardized(x_ref[...], stat_ref)
    zt = z.T
    turned_ref[...] = zt
    part = dot(zt, z)

    @pl.when(step == 0)
    def _():
        acc[...] = part

    @pl.when(step > 0)
    def _():
        acc[...] += part

    @pl.when(step == pl.num_programs(0) - 1)
    def _():
        rows = keep_ref.shape[1]
        for far in range(2):
            for core, out in ((pos_ref[2], keep_ref), (1 - pos_ref[2], send_ref)):
                out[far] = acc[pl.ds(pl.multiple_of((2 * far + core) * rows, rows), rows), :]


def diag_kernel(pos_ref, keep_ref, got_ref, mine_ref, send_ref):
    mine_ref[...] = keep_ref[pos_ref[0]] + got_ref[pos_ref[0]]
    send_ref[...] = keep_ref[1 - pos_ref[0]] + got_ref[1 - pos_ref[0]]


def put_quarters(x, source, scale, keep, send):
    half = keep.shape[-1]
    scale = scale[:, :half]
    for out, near in ((keep, x), (send, 1 - x)):
        for index, (row, col) in enumerate(((near, near), (near, 1 - near), (1 - near, near))):
            rows = pl.ds(pl.multiple_of(row * half, half), half)
            cols = pl.ds(pl.multiple_of(col * half, half), half)
            out[index] = (source[rows, cols] * scale).astype(out.dtype)


def fetched(source, parts, sems):
    rows = parts.shape[1]
    copies = [pltpu.make_async_copy(source.at[pl.ds(k * rows, rows), :], parts.at[k], sems.at[k])
              for k in range(parts.shape[0])]
    for copy in copies:
        copy.start()
    return [(slice(k * rows, (k + 1) * rows), copy.wait) for k, copy in enumerate(copies)]


def far_kernel(pos_ref, turned_ref, w_ref, stat_ref, wstat_ref, keep_ref, send_ref, w_out, acc, parts, sems):
    for k, (rows, wait) in enumerate(fetched(w_ref, parts, sems)):
        wait()
        w = standardized(parts[k], wstat_ref)
        w_out[rows, :] = w
        part = dot(turned_ref[:, rows], w)
        acc[...] = part if k == 0 else acc[...] + part
    listed = jnp.where(pos_ref[2] == 0, stat_ref[3:4, :], wstat_ref[3:4, :])
    put_quarters(pos_ref[0], acc, listed * (1.0 / pos_ref[4].astype(F32)), keep_ref, send_ref)


def near_kernel(pos_ref, turned_ref, y_ref, w_ref, stat_ref, ystat_ref, wstat_ref, keep_b, send_b, keep_d, send_d,
                acc_b, acc_d, parts, sems):
    @pl.when(pos_ref[1] == 1)
    def _():
        for k, (rows, wait) in enumerate(fetched(y_ref, parts, sems)):
            wait()
            y = standardized(parts[k], ystat_ref)
            part_b, part_d = dot(turned_ref[:, rows], y), dot(y.T, w_ref[rows, :])
            acc_b[...] = part_b if k == 0 else acc_b[...] + part_b
            acc_d[...] = part_d if k == 0 else acc_d[...] + part_d
        first = pos_ref[2] == 0
        share = 1.0 / pos_ref[4].astype(F32)
        put_quarters(pos_ref[0], acc_b, jnp.where(first, stat_ref[2:3, :], ystat_ref[2:3, :]) * share, keep_b, send_b)
        put_quarters(pos_ref[0], acc_d, jnp.where(first, ystat_ref[2:3, :], wstat_ref[2:3, :]) * share, keep_d, send_d)


def add_halves(x, keep, got, rows_out, cols_out):
    half = keep.shape[-1]
    here = pl.ds(pl.multiple_of(x * half, half), half)
    there = pl.ds(pl.multiple_of((1 - x) * half, half), half)
    corner = keep[0] + got[0].astype(F32)
    rows_out[:, here] = corner.astype(rows_out.dtype)
    rows_out[:, there] = (keep[1] + got[1].astype(F32)).astype(rows_out.dtype)
    cols_out[:, here] = corner.T.astype(cols_out.dtype)
    cols_out[:, there] = (keep[2] + got[2].astype(F32)).T.astype(cols_out.dtype)


def far_strips_kernel(pos_ref, keep, got, held, to_z):
    add_halves(pos_ref[0], keep, got, held, to_z)


def near_strips_kernel(pos_ref, keep, got, rows_out, cols_out):
    @pl.when(pos_ref[1] == 1)
    def _():
        add_halves(pos_ref[0], keep, got, rows_out, cols_out)


def combine_kernel(pos_ref, held_b, held_c, from_y_b, from_y_d, from_z_c, from_z_d, mine, sib):
    rows = mine.shape[1]
    for core, out in ((pos_ref[2], mine), (1 - pos_ref[2], sib)):
        at = pl.ds(pl.multiple_of(core * rows, rows), rows)
        out[1] = held_c[at, :] + from_z_c[at, :]

        @pl.when(pos_ref[1] == 1)
        def _():
            out[0] = held_b[at, :] + from_y_b[at, :]
            out[2] = from_y_d[at, :].astype(F32)

        @pl.when(pos_ref[1] == 0)
        def _():
            out[2] = from_z_d[at, :].astype(F32)


def finish_kernel(pos_ref, offsets_ref, diag_mine, diag_got, mine, sib, upper, mirror):
    active = pos_ref[1] == 1
    first_core = pos_ref[2] == 0
    even = pos_ref[3] == 0
    pick = jnp.where
    near = pick(active, mine[0], sib[0])
    far = mine[2] + sib[2]
    upper_1 = pick(even, near, far)
    upper_2 = pick(first_core, mine[1], sib[1])
    mirror[0, 0] = pick(even, far, near).astype(BF16)
    mirror[0, 1] = pick(first_core, sib[1], mine[1]).astype(BF16)
    self_tile = (diag_mine[...] + diag_got[...]) * (1.0 / pos_ref[4].astype(F32))
    for slot in range(SLOTS):
        offset = offsets_ref[0, slot]
        tile = pick(offset == 0, self_tile, pick(offset == 1, upper_1, pick(offset == 2, upper_2, 0.0)))
        upper[0, slot] = tile.astype(BF16)


def body(dosage, pair_offsets, live_counts):
    n_var = lax.axis_size("var")
    n_samp = lax.axis_size("samp")
    depth, width = dosage.shape
    half = width // 2
    strip = width // n_samp
    samples_all = depth * n_samp
    v = lax.axis_index("var")
    s = lax.axis_index("samp")
    x, core, odd = s // 2, s % 2, v % 2
    active = (core == odd).astype(jnp.int32)

    def at(var, samp):
        return var * n_samp + samp

    def active_on(var, samp):
        return var % 2 == samp % 2

    def send(value, pairs):
        return lax.ppermute(value, AXES, pairs)

    def shape(*dims, dtype=F32):
        return jax.ShapeDtypeStruct(dims, dtype)

    everyone = [(var, samp) for var in range(n_var) for samp in range(n_samp)]
    z_main = [(at(a, b), at(a - 2 if b % 2 == 0 else a + 2, b)) for a, b in everyone
              if 0 <= (a - 2 if b % 2 == 0 else a + 2) < n_var]
    y_main = [(at(a, b), at(a ^ 1, b)) for a, b in everyone if not active_on(a, b)]
    z_step = [(a, b, a + 2 if b % 2 == 0 else a - 2) for a, b in everyone]
    z_cross = [(at(a, b), at(t, b ^ 1)) for a, b, t in z_step if 0 <= t < n_var]
    z_cross_active = [(at(a, b), at(t, b ^ 1)) for a, b, t in z_step if 0 <= t < n_var and active_on(a, b)]
    y_cross = [(at(a, b), at(a ^ 1, b ^ 1)) for a, b in everyone if active_on(a, b)]
    across = [(at(a, b), at(a, b ^ 2)) for a, b in everyone]
    across_active = [(at(a, b), at(a, b ^ 2)) for a, b in everyone if active_on(a, b)]
    sibling = [(at(a, b), at(a, b ^ 1)) for a, b in everyone]

    w_raw, y_raw = send(dosage, z_main), send(dosage, y_main)

    pos = jnp.stack([x, active, core, odd, jnp.int32(samples_all)]).astype(jnp.int32)
    step_rows = min(1024, depth)
    steps = depth // step_rows
    wide = pl.BlockSpec((step_rows, width), lambda k: (k, 0))
    flat = pl.BlockSpec((width, step_rows), lambda k: (0, k))
    whole = lambda *dims: pl.BlockSpec(dims, lambda k: (0,) * len(dims))

    def call(kernel, name, grid, in_specs, out_specs, out_shape, scratch=(), flops=0, moved=0):
        return pl.pallas_call(
            kernel, grid=grid, in_specs=in_specs, out_specs=out_specs, out_shape=out_shape, scratch_shapes=scratch,
            compiler_params=SOME, name=name,
            cost_estimate=pl.CostEstimate(flops=flops, bytes_accessed=moved, transcendentals=0))

    bytes_block, tile_flops = 2 * depth * width, 2 * depth * width * width
    local = call(lambda *refs: local_kernel(steps, *refs), "local_stats", (steps,), [wide], whole(2, width), shape(2, width),
                 [pltpu.VMEM((1, width), F32)] + [pltpu.VMEM((8, width), F32)] * 2, 5 * depth * width, bytes_block)(dosage)
    others = [send(local, [(at(a, b), at(a, b ^ flip)) for a, b in everyone]) for flip in (1, 2, 3)]
    stat = call(stat_kernel, "stats", (), [SMEM] * 3 + [VMEM] * 4, VMEM, shape(4, width))(
        pos, live_counts, pair_offsets, local, *others)
    w_stat, y_stat = send(stat, z_cross), send(stat, y_cross)

    turned, diag_keep, diag_send = call(
        own_kernel, "own_tile", (steps,), [SMEM, wide, whole(4, width)],
        [flat, whole(2, strip, width), whole(2, strip, width)],
        [shape(width, depth, dtype=BF16), shape(2, strip, width), shape(2, strip, width)],
        [pltpu.VMEM((width, width), F32)], tile_flops, 2 * bytes_block)(pos, dosage, stat)
    diag_mine, diag_other = call(diag_kernel, "own_tile_strips", (), [SMEM, VMEM, VMEM], [VMEM] * 2, [shape(strip, width)] * 2)(
        pos, diag_keep, send(diag_send, sibling))
    diag_got = send(diag_other, across)

    anywhere = pl.BlockSpec(memory_space=pl.ANY)
    parts = [pltpu.VMEM((steps, step_rows, width), BF16), pltpu.SemaphoreType.DMA((steps,))]
    sums = pltpu.VMEM((width, width), F32)
    pair = [shape(3, half, half), shape(3, half, half, dtype=HALVES)]
    keep_c, send_c, w = call(
        far_kernel, "far_tile", (), [SMEM, VMEM, anywhere, VMEM, VMEM], [VMEM] * 3,
        pair + [shape(depth, width, dtype=BF16)], [sums] + parts, tile_flops, 3 * bytes_block)(
        pos, turned, w_raw, stat, w_stat)
    send_c, diag_got = lax.optimization_barrier((send_c, diag_got))
    got_c = send(send_c, across)

    keep_b, send_b, keep_d, send_d = call(
        near_kernel, "near_tiles", (), [SMEM, VMEM, anywhere] + [VMEM] * 4, [VMEM] * 4, pair * 2, [sums] * 2 + parts,
        2 * tile_flops, 3 * bytes_block)(pos, turned, y_raw, w, stat, y_stat, w_stat)
    got_b = send(send_b, across_active)
    send_d, got_c = lax.optimization_barrier((send_d, got_c))
    got_d = send(send_d, across_active)

    held_c, to_z_c = call(far_strips_kernel, "far_strips", (), [SMEM] + [VMEM] * 2, [VMEM] * 2,
                          [shape(half, width)] * 2)(pos, keep_c, got_c)
    from_z_c = send(to_z_c, z_cross)
    got_b, to_z_c = lax.optimization_barrier((got_b, to_z_c))

    def near_strips(name, kind, keep, got):
        return call(near_strips_kernel, name, (), [SMEM] + [VMEM] * 2, [VMEM] * 2, [shape(half, width, dtype=kind)] * 2)(
            pos, keep, got)

    held_b, to_y_b = near_strips("near_strips", F32, keep_b, got_b)
    from_y_b = send(to_y_b, y_cross)
    got_d, to_y_b = lax.optimization_barrier((got_d, to_y_b))
    to_y_d, to_z_d = near_strips("cross_strips", CROSS, keep_d, got_d)
    to_z_d, from_z_c = lax.optimization_barrier((to_z_d, from_z_c))
    from_y_d, from_z_d = send(to_y_d, y_cross), send(to_z_d, z_cross_active)

    mine, sib = call(combine_kernel, "combine", (), [SMEM] + [VMEM] * 6, [VMEM] * 2, [shape(3, strip, width)] * 2)(
        pos, held_b, held_c, from_y_b, from_y_d, from_z_c, from_z_d)
    return call(finish_kernel, "finish", (), [SMEM] * 2 + [VMEM] * 4, [VMEM] * 2,
                [shape(1, SLOTS, strip, width, dtype=BF16), shape(1, 2, strip, width, dtype=BF16)])(
        pos, pair_offsets, diag_mine, diag_got, mine, send(sib, sibling))


def solution(mesh):
    in_specs = (P("samp", "var"), P("var", None), P("var"))
    out_specs = (P("var", None, "samp", None), P("var", None, "samp", None))
    return jax.shard_map(body, mesh=mesh, in_specs=in_specs, out_specs=out_specs, check_vma=False)
```

```python
import jax
import jax.numpy as jnp
from jax import lax
from jax.experimental import pallas as pl
from jax.experimental.pallas import tpu as pltpu
from jax.sharding import PartitionSpec as P

SLOTS = 3
AXES = ("var", "samp")
F32 = jnp.float32
BF16 = jnp.bfloat16
VMEM = pl.BlockSpec(memory_space=pltpu.VMEM)
SMEM = pl.BlockSpec(memory_space=pltpu.SMEM)
SOME = pltpu.CompilerParams(vmem_limit_bytes=24 << 20)
HALVES, CROSS = BF16, BF16


def dot(a, b):
    return jnp.dot(a, b, preferred_element_type=F32)


def standardized(raw, stat_ref):
    return ((raw.astype(F32) - stat_ref[0:1, :]) * stat_ref[1:2, :]).astype(BF16)


def local_kernel(steps, x_ref, out_ref, center, total, square):
    step = pl.program_id(0)
    rows, width = x_ref.shape
    group = min(64, rows)

    @pl.when(step == 0)
    def _():
        center[...] = jnp.mean(x_ref[:group, :].astype(F32), axis=0, keepdims=True)
        total[...] = jnp.zeros_like(total)
        square[...] = jnp.zeros_like(square)

    middle = center[...]

    def add(i, sums):
        x = x_ref[pl.ds(pl.multiple_of(i * group, group), group), :].astype(F32) - middle
        x = x.reshape(group // 8, 8, width)
        return sums[0] + jnp.sum(x, axis=0), sums[1] + jnp.sum(x * x, axis=0)

    sums = lax.fori_loop(0, rows // group, add, (total[...], square[...]))
    total[...], square[...] = sums

    @pl.when(step == steps - 1)
    def _():
        count = float(rows * steps)
        shift = jnp.sum(total[...], axis=0, keepdims=True) * (1.0 / count)
        around = jnp.sum(square[...], axis=0, keepdims=True) - shift * shift * count
        out_ref[0:1, :] = middle + shift
        out_ref[1:2, :] = jnp.maximum(around, 0.0)


def stat_kernel(pos_ref, live_ref, offsets_ref, own_ref, sib_ref, far_ref, cross_ref, stat_ref):
    width = own_ref.shape[1]
    samples = pos_ref[4].astype(F32)

    def merged(values):
        return (values[0] + values[1]) + (values[2] + values[3])

    groups = (own_ref, sib_ref, far_ref, cross_ref)
    mean = merged([ref[0:1, :] for ref in groups]) * 0.25
    between = merged([jnp.square(ref[0:1, :] - mean) for ref in groups]) * (samples * 0.25)
    spread = (merged([ref[1:2, :] for ref in groups]) + between) / samples
    live = lax.broadcasted_iota(jnp.int32, (1, width), 1) < live_ref[0]
    stat_ref[0:1, :] = mean
    stat_ref[1:2, :] = jnp.where(live, lax.rsqrt(spread + 1e-05), 0.0)
    for step in (1, 2):
        listed = offsets_ref[0, 0] == step
        for slot in range(1, SLOTS):
            listed = jnp.logical_or(listed, offsets_ref[0, slot] == step)
        stat_ref[1 + step:2 + step, :] = jnp.full((1, width), jnp.where(listed, 1.0, 0.0), F32)


def own_kernel(pos_ref, x_ref, stat_ref, turned_ref, keep_ref, send_ref, acc):
    step = pl.program_id(0)
    z = standardized(x_ref[...], stat_ref)
    zt = z.T
    turned_ref[...] = zt
    part = dot(zt, z)

    @pl.when(step == 0)
    def _():
        acc[...] = part

    @pl.when(step > 0)
    def _():
        acc[...] += part

    @pl.when(step == pl.num_programs(0) - 1)
    def _():
        rows = keep_ref.shape[1]
        for far in range(2):
            for core, out in ((pos_ref[2], keep_ref), (1 - pos_ref[2], send_ref)):
                out[far] = acc[pl.ds(pl.multiple_of((2 * far + core) * rows, rows), rows), :]


def diag_kernel(pos_ref, keep_ref, got_ref, mine_ref, send_ref):
    mine_ref[...] = keep_ref[pos_ref[0]] + got_ref[pos_ref[0]]
    send_ref[...] = keep_ref[1 - pos_ref[0]] + got_ref[1 - pos_ref[0]]


def put_quarters(x, source, scale, keep, send):
    half = keep.shape[-1]
    scale = scale[:, :half]
    for out, near in ((keep, x), (send, 1 - x)):
        for index, (row, col) in enumerate(((near, near), (near, 1 - near), (1 - near, near))):
            rows = pl.ds(pl.multiple_of(row * half, half), half)
            cols = pl.ds(pl.multiple_of(col * half, half), half)
            out[index] = (source[rows, cols] * scale).astype(out.dtype)


def fetched(source, parts, sems):
    rows = parts.shape[1]
    copies = [pltpu.make_async_copy(source.at[pl.ds(k * rows, rows), :], parts.at[k], sems.at[k])
              for k in range(parts.shape[0])]
    for copy in copies:
        copy.start()
    return [(slice(k * rows, (k + 1) * rows), copy.wait) for k, copy in enumerate(copies)]


def far_kernel(pos_ref, turned_ref, w_ref, stat_ref, wstat_ref, keep_ref, send_ref, w_out, acc, parts, sems):
    for k, (rows, wait) in enumerate(fetched(w_ref, parts, sems)):
        wait()
        w = standardized(parts[k], wstat_ref)
        w_out[rows, :] = w
        part = dot(turned_ref[:, rows], w)
        acc[...] = part if k == 0 else acc[...] + part
    listed = jnp.where(pos_ref[2] == 0, stat_ref[3:4, :], wstat_ref[3:4, :])
    put_quarters(pos_ref[0], acc, listed * (1.0 / pos_ref[4].astype(F32)), keep_ref, send_ref)


def near_kernel(pos_ref, turned_ref, y_ref, stat_ref, ystat_ref, keep_ref, send_ref, y_out, acc, parts, sems):
    @pl.when(pos_ref[1] == 1)
    def _():
        for k, (rows, wait) in enumerate(fetched(y_ref, parts, sems)):
            wait()
            y = standardized(parts[k], ystat_ref)
            y_out[:, rows] = y.T
            part = dot(turned_ref[:, rows], y)
            acc[...] = part if k == 0 else acc[...] + part
        listed = jnp.where(pos_ref[2] == 0, stat_ref[2:3, :], ystat_ref[2:3, :])
        put_quarters(pos_ref[0], acc, listed * (1.0 / pos_ref[4].astype(F32)), keep_ref, send_ref)


def cross_kernel(steps, pos_ref, y_ref, w_ref, ystat_ref, wstat_ref, keep_ref, send_ref, acc):
    @pl.when(pos_ref[1] == 1)
    def _():
        size = w_ref.shape[0] // steps
        for k in range(steps):
            rows = slice(k * size, (k + 1) * size)
            part = dot(y_ref[:, rows], w_ref[rows, :])
            acc[...] = part if k == 0 else acc[...] + part
        listed = jnp.where(pos_ref[2] == 0, ystat_ref[2:3, :], wstat_ref[2:3, :])
        put_quarters(pos_ref[0], acc, listed * (1.0 / pos_ref[4].astype(F32)), keep_ref, send_ref)


def add_halves(x, keep, got, rows_out, cols_out):
    half = keep.shape[-1]
    here = pl.ds(pl.multiple_of(x * half, half), half)
    there = pl.ds(pl.multiple_of((1 - x) * half, half), half)
    corner = keep[0] + got[0].astype(F32)
    rows_out[:, here] = corner.astype(rows_out.dtype)
    rows_out[:, there] = (keep[1] + got[1].astype(F32)).astype(rows_out.dtype)
    cols_out[:, here] = corner.T.astype(cols_out.dtype)
    cols_out[:, there] = (keep[2] + got[2].astype(F32)).T.astype(cols_out.dtype)


def far_strips_kernel(pos_ref, keep, got, held, to_z):
    add_halves(pos_ref[0], keep, got, held, to_z)


def near_strips_kernel(pos_ref, keep, got, rows_out, cols_out):
    @pl.when(pos_ref[1] == 1)
    def _():
        add_halves(pos_ref[0], keep, got, rows_out, cols_out)


def combine_kernel(pos_ref, held_b, held_c, from_y_b, from_y_d, from_z_c, from_z_d, mine, sib):
    rows = mine.shape[1]
    for core, out in ((pos_ref[2], mine), (1 - pos_ref[2], sib)):
        at = pl.ds(pl.multiple_of(core * rows, rows), rows)
        out[1] = held_c[at, :] + from_z_c[at, :]

        @pl.when(pos_ref[1] == 1)
        def _():
            out[0] = held_b[at, :] + from_y_b[at, :]
            out[2] = from_y_d[at, :].astype(F32)

        @pl.when(pos_ref[1] == 0)
        def _():
            out[2] = from_z_d[at, :].astype(F32)


def finish_kernel(pos_ref, offsets_ref, diag_mine, diag_got, mine, sib, upper, mirror):
    active = pos_ref[1] == 1
    first_core = pos_ref[2] == 0
    even = pos_ref[3] == 0
    pick = jnp.where
    near = pick(active, mine[0], sib[0])
    far = mine[2] + sib[2]
    upper_1 = pick(even, near, far)
    upper_2 = pick(first_core, mine[1], sib[1])
    mirror[0, 0] = pick(even, far, near).astype(BF16)
    mirror[0, 1] = pick(first_core, sib[1], mine[1]).astype(BF16)
    self_tile = (diag_mine[...] + diag_got[...]) * (1.0 / pos_ref[4].astype(F32))
    for slot in range(SLOTS):
        offset = offsets_ref[0, slot]
        tile = pick(offset == 0, self_tile, pick(offset == 1, upper_1, pick(offset == 2, upper_2, 0.0)))
        upper[0, slot] = tile.astype(BF16)


def body(dosage, pair_offsets, live_counts):
    n_var = lax.axis_size("var")
    n_samp = lax.axis_size("samp")
    depth, width = dosage.shape
    half = width // 2
    strip = width // n_samp
    samples_all = depth * n_samp
    v = lax.axis_index("var")
    s = lax.axis_index("samp")
    x, core, odd = s // 2, s % 2, v % 2
    active = (core == odd).astype(jnp.int32)

    def at(var, samp):
        return var * n_samp + samp

    def active_on(var, samp):
        return var % 2 == samp % 2

    def send(value, pairs):
        return lax.ppermute(value, AXES, pairs)

    def shape(*dims, dtype=F32):
        return jax.ShapeDtypeStruct(dims, dtype)

    everyone = [(var, samp) for var in range(n_var) for samp in range(n_samp)]
    z_main = [(at(a, b), at(a - 2 if b % 2 == 0 else a + 2, b)) for a, b in everyone
              if 0 <= (a - 2 if b % 2 == 0 else a + 2) < n_var]
    y_main = [(at(a, b), at(a ^ 1, b)) for a, b in everyone if not active_on(a, b)]
    z_step = [(a, b, a + 2 if b % 2 == 0 else a - 2) for a, b in everyone]
    z_cross = [(at(a, b), at(t, b ^ 1)) for a, b, t in z_step if 0 <= t < n_var]
    z_cross_active = [(at(a, b), at(t, b ^ 1)) for a, b, t in z_step if 0 <= t < n_var and active_on(a, b)]
    y_cross = [(at(a, b), at(a ^ 1, b ^ 1)) for a, b in everyone if active_on(a, b)]
    across = [(at(a, b), at(a, b ^ 2)) for a, b in everyone]
    across_active = [(at(a, b), at(a, b ^ 2)) for a, b in everyone if active_on(a, b)]
    sibling = [(at(a, b), at(a, b ^ 1)) for a, b in everyone]

    w_raw, y_raw = send(dosage, z_main), send(dosage, y_main)

    pos = jnp.stack([x, active, core, odd, jnp.int32(samples_all)]).astype(jnp.int32)
    step_rows = min(1024, depth)
    steps = depth // step_rows
    wide = pl.BlockSpec((step_rows, width), lambda k: (k, 0))
    flat = pl.BlockSpec((width, step_rows), lambda k: (0, k))
    whole = lambda *dims: pl.BlockSpec(dims, lambda k: (0,) * len(dims))

    def call(kernel, name, grid, in_specs, out_specs, out_shape, scratch=(), flops=0, moved=0):
        return pl.pallas_call(
            kernel, grid=grid, in_specs=in_specs, out_specs=out_specs, out_shape=out_shape, scratch_shapes=scratch,
            compiler_params=SOME, name=name,
            cost_estimate=pl.CostEstimate(flops=flops, bytes_accessed=moved, transcendentals=0))

    bytes_block, tile_flops = 2 * depth * width, 2 * depth * width * width
    local = call(lambda *refs: local_kernel(steps, *refs), "local_stats", (steps,), [wide], whole(2, width), shape(2, width),
                 [pltpu.VMEM((1, width), F32)] + [pltpu.VMEM((8, width), F32)] * 2, 5 * depth * width, bytes_block)(dosage)
    others = [send(local, [(at(a, b), at(a, b ^ flip)) for a, b in everyone]) for flip in (1, 2, 3)]
    stat = call(stat_kernel, "stats", (), [SMEM] * 3 + [VMEM] * 4, VMEM, shape(4, width))(
        pos, live_counts, pair_offsets, local, *others)
    w_stat, y_stat = send(stat, z_cross), send(stat, y_cross)

    turned, diag_keep, diag_send = call(
        own_kernel, "own_tile", (steps,), [SMEM, wide, whole(4, width)],
        [flat, whole(2, strip, width), whole(2, strip, width)],
        [shape(width, depth, dtype=BF16), shape(2, strip, width), shape(2, strip, width)],
        [pltpu.VMEM((width, width), F32)], tile_flops, 2 * bytes_block)(pos, dosage, stat)
    diag_mine, diag_other = call(diag_kernel, "own_tile_strips", (), [SMEM, VMEM, VMEM], [VMEM] * 2, [shape(strip, width)] * 2)(
        pos, diag_keep, send(diag_send, sibling))
    diag_got = send(diag_other, across)

    anywhere = pl.BlockSpec(memory_space=pl.ANY)
    parts = [pltpu.VMEM((steps, step_rows, width), BF16), pltpu.SemaphoreType.DMA((steps,))]
    sums = pltpu.VMEM((width, width), F32)
    pair = [shape(3, half, half), shape(3, half, half, dtype=HALVES)]
    keep_c, send_c, w = call(
        far_kernel, "far_tile", (), [SMEM, VMEM, anywhere, VMEM, VMEM], [VMEM] * 3,
        pair + [shape(depth, width, dtype=BF16)], [sums] + parts, tile_flops, 3 * bytes_block)(
        pos, turned, w_raw, stat, w_stat)
    send_c, diag_got = lax.optimization_barrier((send_c, diag_got))
    got_c = send(send_c, across)

    keep_b, send_b, y = call(
        near_kernel, "near_tile", (), [SMEM, VMEM, anywhere, VMEM, VMEM], [VMEM] * 3,
        pair + [shape(width, depth, dtype=BF16)], [sums] + parts, tile_flops, 3 * bytes_block)(
        pos, turned, y_raw, stat, y_stat)
    got_b = send(send_b, across_active)
    keep_d, send_d = call(
        lambda *refs: cross_kernel(steps, *refs), "cross_tile", (), [SMEM] + [VMEM] * 4, [VMEM] * 2, pair, [sums],
        tile_flops, 2 * bytes_block)(pos, y, w, y_stat, w_stat)
    send_d, got_c = lax.optimization_barrier((send_d, got_c))
    got_d = send(send_d, across_active)

    held_c, to_z_c = call(far_strips_kernel, "far_strips", (), [SMEM] + [VMEM] * 2, [VMEM] * 2,
                          [shape(half, width)] * 2)(pos, keep_c, got_c)
    from_z_c = send(to_z_c, z_cross)
    got_b, to_z_c = lax.optimization_barrier((got_b, to_z_c))

    def near_strips(name, kind, keep, got):
        return call(near_strips_kernel, name, (), [SMEM] + [VMEM] * 2, [VMEM] * 2, [shape(half, width, dtype=kind)] * 2)(
            pos, keep, got)

    held_b, to_y_b = near_strips("near_strips", F32, keep_b, got_b)
    from_y_b = send(to_y_b, y_cross)
    got_d, to_y_b = lax.optimization_barrier((got_d, to_y_b))
    to_y_d, to_z_d = near_strips("cross_strips", CROSS, keep_d, got_d)
    to_z_d, from_z_c = lax.optimization_barrier((to_z_d, from_z_c))
    from_y_d, from_z_d = send(to_y_d, y_cross), send(to_z_d, z_cross_active)

    mine, sib = call(combine_kernel, "combine", (), [SMEM] + [VMEM] * 6, [VMEM] * 2, [shape(3, strip, width)] * 2)(
        pos, held_b, held_c, from_y_b, from_y_d, from_z_c, from_z_d)
    return call(finish_kernel, "finish", (), [SMEM] * 2 + [VMEM] * 4, [VMEM] * 2,
                [shape(1, SLOTS, strip, width, dtype=BF16), shape(1, 2, strip, width, dtype=BF16)])(
        pos, pair_offsets, diag_mine, diag_got, mine, send(sib, sibling))


def solution(mesh):
    in_specs = (P("samp", "var"), P("var", None), P("var"))
    out_specs = (P("var", None, "samp", None), P("var", None, "samp", None))
    return jax.shard_map(body, mesh=mesh, in_specs=in_specs, out_specs=out_specs, check_vma=False)
```

```python
import jax
import jax.numpy as jnp
from jax import lax
from jax.experimental import pallas as pl
from jax.experimental.pallas import tpu as pltpu
from jax.sharding import PartitionSpec as P

SLOTS = 3
AXES = ("var", "samp")
F32 = jnp.float32
BF16 = jnp.bfloat16
VMEM = pl.BlockSpec(memory_space=pltpu.VMEM)
SMEM = pl.BlockSpec(memory_space=pltpu.SMEM)
SOME = pltpu.CompilerParams(vmem_limit_bytes=24 << 20)
HALVES, CROSS = BF16, BF16


def dot(a, b):
    return jnp.dot(a, b, preferred_element_type=F32)


def standardized(raw, stat_ref):
    return ((raw.astype(F32) - stat_ref[0:1, :]) * stat_ref[1:2, :]).astype(BF16)


def local_kernel(steps, x_ref, out_ref, center, total, square):
    step = pl.program_id(0)
    rows, width = x_ref.shape
    group = min(64, rows)

    @pl.when(step == 0)
    def _():
        center[...] = jnp.mean(x_ref[:group, :].astype(F32), axis=0, keepdims=True)
        total[...] = jnp.zeros_like(total)
        square[...] = jnp.zeros_like(square)

    middle = center[...]

    def add(i, sums):
        x = x_ref[pl.ds(pl.multiple_of(i * group, group), group), :].astype(F32) - middle
        x = x.reshape(group // 8, 8, width)
        return sums[0] + jnp.sum(x, axis=0), sums[1] + jnp.sum(x * x, axis=0)

    sums = lax.fori_loop(0, rows // group, add, (total[...], square[...]))
    total[...], square[...] = sums

    @pl.when(step == steps - 1)
    def _():
        count = float(rows * steps)
        shift = jnp.sum(total[...], axis=0, keepdims=True) * (1.0 / count)
        around = jnp.sum(square[...], axis=0, keepdims=True) - shift * shift * count
        out_ref[0:1, :] = middle + shift
        out_ref[1:2, :] = jnp.maximum(around, 0.0)


def stat_kernel(pos_ref, live_ref, offsets_ref, own_ref, sib_ref, far_ref, cross_ref, stat_ref):
    width = own_ref.shape[1]
    samples = pos_ref[4].astype(F32)

    def merged(values):
        return (values[0] + values[1]) + (values[2] + values[3])

    groups = (own_ref, sib_ref, far_ref, cross_ref)
    mean = merged([ref[0:1, :] for ref in groups]) * 0.25
    between = merged([jnp.square(ref[0:1, :] - mean) for ref in groups]) * (samples * 0.25)
    spread = (merged([ref[1:2, :] for ref in groups]) + between) / samples
    live = lax.broadcasted_iota(jnp.int32, (1, width), 1) < live_ref[0]
    stat_ref[0:1, :] = mean
    stat_ref[1:2, :] = jnp.where(live, lax.rsqrt(spread + 1e-05), 0.0)
    for step in (1, 2):
        listed = offsets_ref[0, 0] == step
        for slot in range(1, SLOTS):
            listed = jnp.logical_or(listed, offsets_ref[0, slot] == step)
        stat_ref[1 + step:2 + step, :] = jnp.full((1, width), jnp.where(listed, 1.0, 0.0), F32)


def own_kernel(pos_ref, x_ref, stat_ref, turned_ref, keep_ref, send_ref, acc):
    step = pl.program_id(0)
    z = standardized(x_ref[...], stat_ref)
    zt = z.T
    turned_ref[...] = zt
    part = dot(zt, z)

    @pl.when(step == 0)
    def _():
        acc[...] = part

    @pl.when(step > 0)
    def _():
        acc[...] += part

    @pl.when(step == pl.num_programs(0) - 1)
    def _():
        rows = keep_ref.shape[1]
        for far in range(2):
            for core, out in ((pos_ref[2], keep_ref), (1 - pos_ref[2], send_ref)):
                out[far] = acc[pl.ds(pl.multiple_of((2 * far + core) * rows, rows), rows), :]


def diag_kernel(pos_ref, keep_ref, got_ref, mine_ref, send_ref):
    mine_ref[...] = keep_ref[pos_ref[0]] + got_ref[pos_ref[0]]
    send_ref[...] = keep_ref[1 - pos_ref[0]] + got_ref[1 - pos_ref[0]]


def put_quarters(x, source, scale, keep, send):
    half = keep.shape[-1]
    scale = scale[:, :half]
    for out, near in ((keep, x), (send, 1 - x)):
        for index, (row, col) in enumerate(((near, near), (near, 1 - near), (1 - near, near))):
            rows = pl.ds(pl.multiple_of(row * half, half), half)
            cols = pl.ds(pl.multiple_of(col * half, half), half)
            out[index] = (source[rows, cols] * scale).astype(out.dtype)


def fetched(source, parts, sems):
    rows = parts.shape[1]
    copies = [pltpu.make_async_copy(source.at[pl.ds(k * rows, rows), :], parts.at[k], sems.at[k])
              for k in range(parts.shape[0])]
    for copy in copies:
        copy.start()
    return [(slice(k * rows, (k + 1) * rows), copy.wait) for k, copy in enumerate(copies)]


def far_kernel(pos_ref, turned_ref, w_ref, stat_ref, wstat_ref, keep_ref, send_ref, w_out, acc, parts, sems):
    for k, (rows, wait) in enumerate(fetched(w_ref, parts, sems)):
        wait()
        w = standardized(parts[k], wstat_ref)
        w_out[rows, :] = w
        part = dot(turned_ref[:, rows], w)
        acc[...] = part if k == 0 else acc[...] + part
    listed = jnp.where(pos_ref[2] == 0, stat_ref[3:4, :], wstat_ref[3:4, :])
    put_quarters(pos_ref[0], acc, listed * (1.0 / pos_ref[4].astype(F32)), keep_ref, send_ref)


def near_kernel(pos_ref, turned_ref, y_ref, stat_ref, ystat_ref, keep_ref, send_ref, y_out, acc, parts, sems):
    @pl.when(pos_ref[1] == 1)
    def _():
        for k, (rows, wait) in enumerate(fetched(y_ref, parts, sems)):
            wait()
            y = standardized(parts[k], ystat_ref)
            y_out[:, rows] = y.T
            part = dot(turned_ref[:, rows], y)
            acc[...] = part if k == 0 else acc[...] + part
        listed = jnp.where(pos_ref[2] == 0, stat_ref[2:3, :], ystat_ref[2:3, :])
        put_quarters(pos_ref[0], acc, listed * (1.0 / pos_ref[4].astype(F32)), keep_ref, send_ref)


def cross_kernel(steps, pos_ref, y_ref, w_ref, ystat_ref, wstat_ref, keep_ref, send_ref, acc):
    @pl.when(pos_ref[1] == 1)
    def _():
        size = w_ref.shape[0] // steps
        for k in range(steps):
            rows = slice(k * size, (k + 1) * size)
            part = dot(y_ref[:, rows], w_ref[rows, :])
            acc[...] = part if k == 0 else acc[...] + part
        listed = jnp.where(pos_ref[2] == 0, ystat_ref[2:3, :], wstat_ref[2:3, :])
        put_quarters(pos_ref[0], acc, listed * (1.0 / pos_ref[4].astype(F32)), keep_ref, send_ref)


def add_halves(x, keep, got, rows_out, cols_out):
    half = keep.shape[-1]
    here = pl.ds(pl.multiple_of(x * half, half), half)
    there = pl.ds(pl.multiple_of((1 - x) * half, half), half)
    corner = keep[0] + got[0].astype(F32)
    rows_out[:, here] = corner.astype(rows_out.dtype)
    rows_out[:, there] = (keep[1] + got[1].astype(F32)).astype(rows_out.dtype)
    cols_out[:, here] = corner.T.astype(cols_out.dtype)
    cols_out[:, there] = (keep[2] + got[2].astype(F32)).T.astype(cols_out.dtype)


def far_strips_kernel(pos_ref, keep, got, held, to_z):
    add_halves(pos_ref[0], keep, got, held, to_z)


def near_strips_kernel(pos_ref, keep, got, rows_out, cols_out):
    @pl.when(pos_ref[1] == 1)
    def _():
        add_halves(pos_ref[0], keep, got, rows_out, cols_out)


def combine_kernel(pos_ref, held_b, held_c, from_y_b, from_y_d, from_z_c, from_z_d, mine, sib):
    rows = mine.shape[1]
    for core, out in ((pos_ref[2], mine), (1 - pos_ref[2], sib)):
        at = pl.ds(pl.multiple_of(core * rows, rows), rows)
        out[1] = held_c[at, :] + from_z_c[at, :]

        @pl.when(pos_ref[1] == 1)
        def _():
            out[0] = held_b[at, :] + from_y_b[at, :]
            out[2] = from_y_d[at, :].astype(F32)

        @pl.when(pos_ref[1] == 0)
        def _():
            out[2] = from_z_d[at, :].astype(F32)


def finish_kernel(pos_ref, offsets_ref, diag_mine, diag_got, mine, sib, upper, mirror):
    active = pos_ref[1] == 1
    first_core = pos_ref[2] == 0
    even = pos_ref[3] == 0
    pick = jnp.where
    near = pick(active, mine[0], sib[0])
    far = mine[2] + sib[2]
    upper_1 = pick(even, near, far)
    upper_2 = pick(first_core, mine[1], sib[1])
    mirror[0, 0] = pick(even, far, near).astype(BF16)
    mirror[0, 1] = pick(first_core, sib[1], mine[1]).astype(BF16)
    self_tile = (diag_mine[...] + diag_got[...]) * (1.0 / pos_ref[4].astype(F32))
    for slot in range(SLOTS):
        offset = offsets_ref[0, slot]
        tile = pick(offset == 0, self_tile, pick(offset == 1, upper_1, pick(offset == 2, upper_2, 0.0)))
        upper[0, slot] = tile.astype(BF16)


def body(dosage, pair_offsets, live_counts):
    n_var = lax.axis_size("var")
    n_samp = lax.axis_size("samp")
    depth, width = dosage.shape
    half = width // 2
    strip = width // n_samp
    samples_all = depth * n_samp
    v = lax.axis_index("var")
    s = lax.axis_index("samp")
    x, core, odd = s // 2, s % 2, v % 2
    active = (core == odd).astype(jnp.int32)

    def at(var, samp):
        return var * n_samp + samp

    def active_on(var, samp):
        return var % 2 == samp % 2

    def send(value, pairs):
        return lax.ppermute(value, AXES, pairs)

    def shape(*dims, dtype=F32):
        return jax.ShapeDtypeStruct(dims, dtype)

    everyone = [(var, samp) for var in range(n_var) for samp in range(n_samp)]
    z_main = [(at(a, b), at(a - 2 if b % 2 == 0 else a + 2, b)) for a, b in everyone
              if 0 <= (a - 2 if b % 2 == 0 else a + 2) < n_var]
    y_main = [(at(a, b), at(a ^ 1, b)) for a, b in everyone if not active_on(a, b)]
    z_step = [(a, b, a + 2 if b % 2 == 0 else a - 2) for a, b in everyone]
    z_cross = [(at(a, b), at(t, b ^ 1)) for a, b, t in z_step if 0 <= t < n_var]
    z_cross_active = [(at(a, b), at(t, b ^ 1)) for a, b, t in z_step if 0 <= t < n_var and active_on(a, b)]
    y_cross = [(at(a, b), at(a ^ 1, b ^ 1)) for a, b in everyone if active_on(a, b)]
    across = [(at(a, b), at(a, b ^ 2)) for a, b in everyone]
    across_active = [(at(a, b), at(a, b ^ 2)) for a, b in everyone if active_on(a, b)]
    sibling = [(at(a, b), at(a, b ^ 1)) for a, b in everyone]

    w_raw, y_raw = send(dosage, z_main), send(dosage, y_main)

    pos = jnp.stack([x, active, core, odd, jnp.int32(samples_all)]).astype(jnp.int32)
    step_rows = min(1024, depth)
    steps = depth // step_rows
    wide = pl.BlockSpec((step_rows, width), lambda k: (k, 0))
    flat = pl.BlockSpec((width, step_rows), lambda k: (0, k))
    whole = lambda *dims: pl.BlockSpec(dims, lambda k: (0,) * len(dims))

    def call(kernel, name, grid, in_specs, out_specs, out_shape, scratch=(), flops=0, moved=0):
        return pl.pallas_call(
            kernel, grid=grid, in_specs=in_specs, out_specs=out_specs, out_shape=out_shape, scratch_shapes=scratch,
            compiler_params=SOME, name=name,
            cost_estimate=pl.CostEstimate(flops=flops, bytes_accessed=moved, transcendentals=0))

    bytes_block, tile_flops = 2 * depth * width, 2 * depth * width * width
    local = call(lambda *refs: local_kernel(steps, *refs), "local_stats", (steps,), [wide], whole(2, width), shape(2, width),
                 [pltpu.VMEM((1, width), F32)] + [pltpu.VMEM((8, width), F32)] * 2, 5 * depth * width, bytes_block)(dosage)
    others = [send(local, [(at(a, b), at(a, b ^ flip)) for a, b in everyone]) for flip in (1, 2, 3)]
    stat = call(stat_kernel, "stats", (), [SMEM] * 3 + [VMEM] * 4, VMEM, shape(4, width))(
        pos, live_counts, pair_offsets, local, *others)
    w_stat, y_stat = send(stat, z_cross), send(stat, y_cross)

    turned, diag_keep, diag_send = call(
        own_kernel, "own_tile", (steps,), [SMEM, wide, whole(4, width)],
        [flat, whole(2, strip, width), whole(2, strip, width)],
        [shape(width, depth, dtype=BF16), shape(2, strip, width), shape(2, strip, width)],
        [pltpu.VMEM((width, width), F32)], tile_flops, 2 * bytes_block)(pos, dosage, stat)
    diag_mine, diag_other = call(diag_kernel, "own_tile_strips", (), [SMEM, VMEM, VMEM], [VMEM] * 2, [shape(strip, width)] * 2)(
        pos, diag_keep, send(diag_send, sibling))
    diag_got = send(diag_other, across)

    anywhere = pl.BlockSpec(memory_space=pl.ANY)
    parts = [pltpu.VMEM((steps, step_rows, width), BF16), pltpu.SemaphoreType.DMA((steps,))]
    sums = pltpu.VMEM((width, width), F32)
    pair = [shape(3, half, half), shape(3, half, half, dtype=HALVES)]
    keep_c, send_c, w = call(
        far_kernel, "far_tile", (), [SMEM, VMEM, anywhere, VMEM, VMEM], [VMEM] * 3,
        pair + [shape(depth, width, dtype=BF16)], [sums] + parts, tile_flops, 3 * bytes_block)(
        pos, turned, w_raw, stat, w_stat)
    send_c, diag_got = lax.optimization_barrier((send_c, diag_got))
    got_c = send(send_c, across)

    keep_b, send_b, y = call(
        near_kernel, "near_tile", (), [SMEM, VMEM, anywhere, VMEM, VMEM], [VMEM] * 3,
        pair + [shape(width, depth, dtype=BF16)], [sums] + parts, tile_flops, 3 * bytes_block)(
        pos, turned, y_raw, stat, y_stat)
    got_b = send(send_b, across_active)
    keep_d, send_d = call(
        lambda *refs: cross_kernel(steps, *refs), "cross_tile", (), [SMEM] + [VMEM] * 4, [VMEM] * 2, pair, [sums],
        tile_flops, 2 * bytes_block)(pos, y, w, y_stat, w_stat)
    send_d, got_c = lax.optimization_barrier((send_d, got_c))
    got_d = send(send_d, across_active)

    held_c, to_z_c = call(far_strips_kernel, "far_strips", (), [SMEM] + [VMEM] * 2, [VMEM] * 2,
                          [shape(half, width)] * 2)(pos, keep_c, got_c)
    from_z_c = send(to_z_c, z_cross)
    got_b, to_z_c = lax.optimization_barrier((got_b, to_z_c))

    def near_strips(name, kind, keep, got):
        return call(near_strips_kernel, name, (), [SMEM] + [VMEM] * 2, [VMEM] * 2, [shape(half, width, dtype=kind)] * 2)(
            pos, keep, got)

    held_b, to_y_b = near_strips("near_strips", F32, keep_b, got_b)
    from_y_b = send(to_y_b, y_cross)
    got_d, to_y_b = lax.optimization_barrier((got_d, to_y_b))
    to_y_d, to_z_d = near_strips("cross_strips", CROSS, keep_d, got_d)
    from_y_d, from_z_d = send(to_y_d, y_cross), send(to_z_d, z_cross_active)

    mine, sib = call(combine_kernel, "combine", (), [SMEM] + [VMEM] * 6, [VMEM] * 2, [shape(3, strip, width)] * 2)(
        pos, held_b, held_c, from_y_b, from_y_d, from_z_c, from_z_d)
    return call(finish_kernel, "finish", (), [SMEM] * 2 + [VMEM] * 4, [VMEM] * 2,
                [shape(1, SLOTS, strip, width, dtype=BF16), shape(1, 2, strip, width, dtype=BF16)])(
        pos, pair_offsets, diag_mine, diag_got, mine, send(sib, sibling))


def solution(mesh):
    in_specs = (P("samp", "var"), P("var", None), P("var"))
    out_specs = (P("var", None, "samp", None), P("var", None, "samp", None))
    return jax.shard_map(body, mesh=mesh, in_specs=in_specs, out_specs=out_specs, check_vma=False)
```

```python
import jax
import jax.numpy as jnp
from jax import lax
from jax.experimental import pallas as pl
from jax.experimental.pallas import tpu as pltpu
from jax.sharding import PartitionSpec as P

SLOTS = 3
AXES = ("var", "samp")
F32 = jnp.float32
BF16 = jnp.bfloat16
VMEM = pl.BlockSpec(memory_space=pltpu.VMEM)
SMEM = pl.BlockSpec(memory_space=pltpu.SMEM)
SOME = pltpu.CompilerParams(vmem_limit_bytes=24 << 20)
HALVES, CROSS = BF16, BF16


def dot(a, b):
    return jnp.dot(a, b, preferred_element_type=F32)


def standardized(raw, stat_ref):
    return ((raw.astype(F32) - stat_ref[0:1, :]) * stat_ref[1:2, :]).astype(BF16)


def local_kernel(steps, x_ref, out_ref, center, total, square):
    step = pl.program_id(0)
    rows, width = x_ref.shape
    group = min(64, rows)

    @pl.when(step == 0)
    def _():
        center[...] = jnp.mean(x_ref[:group, :].astype(F32), axis=0, keepdims=True)
        total[...] = jnp.zeros_like(total)
        square[...] = jnp.zeros_like(square)

    middle = center[...]

    def add(i, sums):
        x = x_ref[pl.ds(pl.multiple_of(i * group, group), group), :].astype(F32) - middle
        x = x.reshape(group // 8, 8, width)
        return sums[0] + jnp.sum(x, axis=0), sums[1] + jnp.sum(x * x, axis=0)

    sums = lax.fori_loop(0, rows // group, add, (total[...], square[...]))
    total[...], square[...] = sums

    @pl.when(step == steps - 1)
    def _():
        count = float(rows * steps)
        shift = jnp.sum(total[...], axis=0, keepdims=True) * (1.0 / count)
        around = jnp.sum(square[...], axis=0, keepdims=True) - shift * shift * count
        out_ref[0:1, :] = middle + shift
        out_ref[1:2, :] = jnp.maximum(around, 0.0)


def stat_kernel(pos_ref, live_ref, offsets_ref, own_ref, sib_ref, far_ref, cross_ref, stat_ref):
    width = own_ref.shape[1]
    samples = pos_ref[4].astype(F32)

    def merged(values):
        return (values[0] + values[1]) + (values[2] + values[3])

    groups = (own_ref, sib_ref, far_ref, cross_ref)
    mean = merged([ref[0:1, :] for ref in groups]) * 0.25
    between = merged([jnp.square(ref[0:1, :] - mean) for ref in groups]) * (samples * 0.25)
    spread = (merged([ref[1:2, :] for ref in groups]) + between) / samples
    live = lax.broadcasted_iota(jnp.int32, (1, width), 1) < live_ref[0]
    stat_ref[0:1, :] = mean
    stat_ref[1:2, :] = jnp.where(live, lax.rsqrt(spread + 1e-05), 0.0)
    for step in (1, 2):
        listed = offsets_ref[0, 0] == step
        for slot in range(1, SLOTS):
            listed = jnp.logical_or(listed, offsets_ref[0, slot] == step)
        stat_ref[1 + step:2 + step, :] = jnp.full((1, width), jnp.where(listed, 1.0, 0.0), F32)


def own_kernel(pos_ref, x_ref, stat_ref, turned_ref, keep_ref, send_ref, acc):
    step = pl.program_id(0)
    z = standardized(x_ref[...], stat_ref)
    zt = z.T
    turned_ref[...] = zt
    part = dot(zt, z)

    @pl.when(step == 0)
    def _():
        acc[...] = part

    @pl.when(step > 0)
    def _():
        acc[...] += part

    @pl.when(step == pl.num_programs(0) - 1)
    def _():
        rows = keep_ref.shape[1]
        for far in range(2):
            for core, out in ((pos_ref[2], keep_ref), (1 - pos_ref[2], send_ref)):
                out[far] = acc[pl.ds(pl.multiple_of((2 * far + core) * rows, rows), rows), :]


def diag_kernel(pos_ref, keep_ref, got_ref, mine_ref, send_ref):
    mine_ref[...] = keep_ref[pos_ref[0]] + got_ref[pos_ref[0]]
    send_ref[...] = keep_ref[1 - pos_ref[0]] + got_ref[1 - pos_ref[0]]


def put_quarters(x, source, scale, keep, send):
    half = keep.shape[-1]
    scale = scale[:, :half]
    for out, near in ((keep, x), (send, 1 - x)):
        for index, (row, col) in enumerate(((near, near), (near, 1 - near), (1 - near, near))):
            rows = pl.ds(pl.multiple_of(row * half, half), half)
            cols = pl.ds(pl.multiple_of(col * half, half), half)
            out[index] = (source[rows, cols] * scale).astype(out.dtype)


def fetched(source, parts, sems):
    rows = parts.shape[1]
    copies = [pltpu.make_async_copy(source.at[pl.ds(k * rows, rows), :], parts.at[k], sems.at[k])
              for k in range(parts.shape[0])]
    for copy in copies:
        copy.start()
    return [(slice(k * rows, (k + 1) * rows), copy.wait) for k, copy in enumerate(copies)]


def far_kernel(pos_ref, turned_ref, w_ref, stat_ref, wstat_ref, keep_ref, send_ref, w_out, acc, parts, sems):
    for k, (rows, wait) in enumerate(fetched(w_ref, parts, sems)):
        wait()
        w = standardized(parts[k], wstat_ref)
        w_out[rows, :] = w
        part = dot(turned_ref[:, rows], w)
        acc[...] = part if k == 0 else acc[...] + part
    listed = jnp.where(pos_ref[2] == 0, stat_ref[3:4, :], wstat_ref[3:4, :])
    put_quarters(pos_ref[0], acc, listed * (1.0 / pos_ref[4].astype(F32)), keep_ref, send_ref)


def near_kernel(pos_ref, turned_ref, y_ref, stat_ref, ystat_ref, keep_ref, send_ref, y_out, acc, parts, sems):
    @pl.when(pos_ref[1] == 1)
    def _():
        for k, (rows, wait) in enumerate(fetched(y_ref, parts, sems)):
            wait()
            y = standardized(parts[k], ystat_ref)
            y_out[:, rows] = y.T
            part = dot(turned_ref[:, rows], y)
            acc[...] = part if k == 0 else acc[...] + part
        listed = jnp.where(pos_ref[2] == 0, stat_ref[2:3, :], ystat_ref[2:3, :])
        put_quarters(pos_ref[0], acc, listed * (1.0 / pos_ref[4].astype(F32)), keep_ref, send_ref)


def cross_kernel(steps, pos_ref, y_ref, w_ref, ystat_ref, wstat_ref, keep_ref, send_ref, acc):
    @pl.when(pos_ref[1] == 1)
    def _():
        size = w_ref.shape[0] // steps
        for k in range(steps):
            rows = slice(k * size, (k + 1) * size)
            part = dot(y_ref[:, rows], w_ref[rows, :])
            acc[...] = part if k == 0 else acc[...] + part
        listed = jnp.where(pos_ref[2] == 0, ystat_ref[2:3, :], wstat_ref[2:3, :])
        put_quarters(pos_ref[0], acc, listed * (1.0 / pos_ref[4].astype(F32)), keep_ref, send_ref)


def add_halves(x, keep, got, rows_out, cols_out):
    half = keep.shape[-1]
    here = pl.ds(pl.multiple_of(x * half, half), half)
    there = pl.ds(pl.multiple_of((1 - x) * half, half), half)
    corner = keep[0] + got[0].astype(F32)
    rows_out[:, here] = corner.astype(rows_out.dtype)
    rows_out[:, there] = (keep[1] + got[1].astype(F32)).astype(rows_out.dtype)
    cols_out[:, here] = corner.T.astype(cols_out.dtype)
    cols_out[:, there] = (keep[2] + got[2].astype(F32)).T.astype(cols_out.dtype)


def far_strips_kernel(pos_ref, keep, got, held, to_z):
    add_halves(pos_ref[0], keep, got, held, to_z)


def near_strips_kernel(pos_ref, keep, got, rows_out, cols_out):
    @pl.when(pos_ref[1] == 1)
    def _():
        add_halves(pos_ref[0], keep, got, rows_out, cols_out)


def combine_kernel(pos_ref, held_b, held_c, from_y_b, from_y_d, from_z_c, from_z_d, mine, sib):
    rows = mine.shape[1]
    for core, out in ((pos_ref[2], mine), (1 - pos_ref[2], sib)):
        at = pl.ds(pl.multiple_of(core * rows, rows), rows)
        out[1] = held_c[at, :] + from_z_c[at, :]

        @pl.when(pos_ref[1] == 1)
        def _():
            out[0] = held_b[at, :] + from_y_b[at, :]
            out[2] = from_y_d[at, :].astype(F32)

        @pl.when(pos_ref[1] == 0)
        def _():
            out[2] = from_z_d[at, :].astype(F32)


def finish_kernel(pos_ref, offsets_ref, diag_mine, diag_got, mine, sib, upper, mirror):
    active = pos_ref[1] == 1
    first_core = pos_ref[2] == 0
    even = pos_ref[3] == 0
    pick = jnp.where
    near = pick(active, mine[0], sib[0])
    far = mine[2] + sib[2]
    upper_1 = pick(even, near, far)
    upper_2 = pick(first_core, mine[1], sib[1])
    mirror[0, 0] = pick(even, far, near).astype(BF16)
    mirror[0, 1] = pick(first_core, sib[1], mine[1]).astype(BF16)
    self_tile = (diag_mine[...] + diag_got[...]) * (1.0 / pos_ref[4].astype(F32))
    for slot in range(SLOTS):
        offset = offsets_ref[0, slot]
        tile = pick(offset == 0, self_tile, pick(offset == 1, upper_1, pick(offset == 2, upper_2, 0.0)))
        upper[0, slot] = tile.astype(BF16)


def body(dosage, pair_offsets, live_counts):
    n_var = lax.axis_size("var")
    n_samp = lax.axis_size("samp")
    depth, width = dosage.shape
    half = width // 2
    strip = width // n_samp
    samples_all = depth * n_samp
    v = lax.axis_index("var")
    s = lax.axis_index("samp")
    x, core, odd = s // 2, s % 2, v % 2
    active = (core == odd).astype(jnp.int32)

    def at(var, samp):
        return var * n_samp + samp

    def active_on(var, samp):
        return var % 2 == samp % 2

    def send(value, pairs):
        return lax.ppermute(value, AXES, pairs)

    def shape(*dims, dtype=F32):
        return jax.ShapeDtypeStruct(dims, dtype)

    everyone = [(var, samp) for var in range(n_var) for samp in range(n_samp)]
    z_main = [(at(a, b), at(a - 2 if b % 2 == 0 else a + 2, b)) for a, b in everyone
              if 0 <= (a - 2 if b % 2 == 0 else a + 2) < n_var]
    y_main = [(at(a, b), at(a ^ 1, b)) for a, b in everyone if not active_on(a, b)]
    z_step = [(a, b, a + 2 if b % 2 == 0 else a - 2) for a, b in everyone]
    z_cross = [(at(a, b), at(t, b ^ 1)) for a, b, t in z_step if 0 <= t < n_var]
    z_cross_active = [(at(a, b), at(t, b ^ 1)) for a, b, t in z_step if 0 <= t < n_var and active_on(a, b)]
    y_cross = [(at(a, b), at(a ^ 1, b ^ 1)) for a, b in everyone if active_on(a, b)]
    across = [(at(a, b), at(a, b ^ 2)) for a, b in everyone]
    across_active = [(at(a, b), at(a, b ^ 2)) for a, b in everyone if active_on(a, b)]
    sibling = [(at(a, b), at(a, b ^ 1)) for a, b in everyone]

    w_raw, y_raw = send(dosage, z_main), send(dosage, y_main)

    pos = jnp.stack([x, active, core, odd, jnp.int32(samples_all)]).astype(jnp.int32)
    step_rows = min(1024, depth)
    steps = depth // step_rows
    wide = pl.BlockSpec((step_rows, width), lambda k: (k, 0))
    flat = pl.BlockSpec((width, step_rows), lambda k: (0, k))
    whole = lambda *dims: pl.BlockSpec(dims, lambda k: (0,) * len(dims))

    def call(kernel, name, grid, in_specs, out_specs, out_shape, scratch=(), flops=0, moved=0):
        return pl.pallas_call(
            kernel, grid=grid, in_specs=in_specs, out_specs=out_specs, out_shape=out_shape, scratch_shapes=scratch,
            compiler_params=SOME, name=name,
            cost_estimate=pl.CostEstimate(flops=flops, bytes_accessed=moved, transcendentals=0))

    bytes_block, tile_flops = 2 * depth * width, 2 * depth * width * width
    local = call(lambda *refs: local_kernel(steps, *refs), "local_stats", (steps,), [wide], whole(2, width), shape(2, width),
                 [pltpu.VMEM((1, width), F32)] + [pltpu.VMEM((8, width), F32)] * 2, 5 * depth * width, bytes_block)(dosage)
    others = [send(local, [(at(a, b), at(a, b ^ flip)) for a, b in everyone]) for flip in (1, 2, 3)]
    stat = call(stat_kernel, "stats", (), [SMEM] * 3 + [VMEM] * 4, VMEM, shape(4, width))(
        pos, live_counts, pair_offsets, local, *others)
    w_stat, y_stat = send(stat, z_cross), send(stat, y_cross)

    turned, diag_keep, diag_send = call(
        own_kernel, "own_tile", (steps,), [SMEM, wide, whole(4, width)],
        [flat, whole(2, strip, width), whole(2, strip, width)],
        [shape(width, depth, dtype=BF16), shape(2, strip, width), shape(2, strip, width)],
        [pltpu.VMEM((width, width), F32)], tile_flops, 2 * bytes_block)(pos, dosage, stat)
    diag_mine, diag_other = call(diag_kernel, "own_tile_strips", (), [SMEM, VMEM, VMEM], [VMEM] * 2, [shape(strip, width)] * 2)(
        pos, diag_keep, send(diag_send, sibling))
    diag_got = send(diag_other, across)

    anywhere = pl.BlockSpec(memory_space=pl.ANY)
    parts = [pltpu.VMEM((steps, step_rows, width), BF16), pltpu.SemaphoreType.DMA((steps,))]
    sums = pltpu.VMEM((width, width), F32)
    pair = [shape(3, half, half), shape(3, half, half, dtype=HALVES)]
    keep_c, send_c, w = call(
        far_kernel, "far_tile", (), [SMEM, VMEM, anywhere, VMEM, VMEM], [VMEM] * 3,
        pair + [shape(depth, width, dtype=BF16)], [sums] + parts, tile_flops, 3 * bytes_block)(
        pos, turned, w_raw, stat, w_stat)
    send_c, diag_got = lax.optimization_barrier((send_c, diag_got))
    got_c = send(send_c, across)

    keep_b, send_b, y = call(
        near_kernel, "near_tile", (), [SMEM, VMEM, anywhere, VMEM, VMEM], [VMEM] * 3,
        pair + [shape(width, depth, dtype=BF16)], [sums] + parts, tile_flops, 3 * bytes_block)(
        pos, turned, y_raw, stat, y_stat)
    got_b = send(send_b, across_active)
    keep_d, send_d = call(
        lambda *refs: cross_kernel(steps, *refs), "cross_tile", (), [SMEM] + [VMEM] * 4, [VMEM] * 2, pair, [sums],
        tile_flops, 2 * bytes_block)(pos, y, w, y_stat, w_stat)
    _, got_c = lax.optimization_barrier((send_d, got_c))
    got_d = send(send_d, across_active)

    held_c, to_z_c = call(far_strips_kernel, "far_strips", (), [SMEM] + [VMEM] * 2, [VMEM] * 2,
                          [shape(half, width)] * 2)(pos, keep_c, got_c)
    from_z_c = send(to_z_c, z_cross)
    got_b, to_z_c = lax.optimization_barrier((got_b, to_z_c))

    def near_strips(name, kind, keep, got):
        return call(near_strips_kernel, name, (), [SMEM] + [VMEM] * 2, [VMEM] * 2, [shape(half, width, dtype=kind)] * 2)(
            pos, keep, got)

    held_b, to_y_b = near_strips("near_strips", F32, keep_b, got_b)
    from_y_b = send(to_y_b, y_cross)
    got_d, to_y_b = lax.optimization_barrier((got_d, to_y_b))
    to_y_d, to_z_d = near_strips("cross_strips", CROSS, keep_d, got_d)
    from_y_d, from_z_d = send(to_y_d, y_cross), send(to_z_d, z_cross_active)

    from_z_c, from_y_d = lax.optimization_barrier((from_z_c, from_y_d))
    mine, sib = call(combine_kernel, "combine", (), [SMEM] + [VMEM] * 6, [VMEM] * 2, [shape(3, strip, width)] * 2)(
        pos, held_b, held_c, from_y_b, from_y_d, from_z_c, from_z_d)
    return call(finish_kernel, "finish", (), [SMEM] * 2 + [VMEM] * 4, [VMEM] * 2,
                [shape(1, SLOTS, strip, width, dtype=BF16), shape(1, 2, strip, width, dtype=BF16)])(
        pos, pair_offsets, diag_mine, diag_got, mine, send(sib, sibling))


def solution(mesh):
    in_specs = (P("samp", "var"), P("var", None), P("var"))
    out_specs = (P("var", None, "samp", None), P("var", None, "samp", None))
    return jax.shard_map(body, mesh=mesh, in_specs=in_specs, out_specs=out_specs, check_vma=False)
```

```python
import jax
import jax.numpy as jnp
from jax import lax
from jax.experimental import pallas as pl
from jax.experimental.pallas import tpu as pltpu
from jax.sharding import PartitionSpec as P

SLOTS = 3
AXES = ("var", "samp")
F32 = jnp.float32
BF16 = jnp.bfloat16
VMEM = pl.BlockSpec(memory_space=pltpu.VMEM)
SMEM = pl.BlockSpec(memory_space=pltpu.SMEM)
SOME = pltpu.CompilerParams(vmem_limit_bytes=24 << 20)
HALVES, CROSS = BF16, BF16


def dot(a, b):
    return jnp.dot(a, b, preferred_element_type=F32)


def standardized(raw, stat_ref):
    return ((raw.astype(F32) - stat_ref[0:1, :]) * stat_ref[1:2, :]).astype(BF16)


def local_kernel(steps, x_ref, out_ref, center, total, square):
    step = pl.program_id(0)
    rows, width = x_ref.shape
    group = min(64, rows)

    @pl.when(step == 0)
    def _():
        center[...] = jnp.mean(x_ref[:group, :].astype(F32), axis=0, keepdims=True)
        total[...] = jnp.zeros_like(total)
        square[...] = jnp.zeros_like(square)

    middle = center[...]

    def add(i, sums):
        x = x_ref[pl.ds(pl.multiple_of(i * group, group), group), :].astype(F32) - middle
        x = x.reshape(group // 8, 8, width)
        return sums[0] + jnp.sum(x, axis=0), sums[1] + jnp.sum(x * x, axis=0)

    sums = lax.fori_loop(0, rows // group, add, (total[...], square[...]))
    total[...], square[...] = sums

    @pl.when(step == steps - 1)
    def _():
        count = float(rows * steps)
        shift = jnp.sum(total[...], axis=0, keepdims=True) * (1.0 / count)
        around = jnp.sum(square[...], axis=0, keepdims=True) - shift * shift * count
        out_ref[0:1, :] = middle + shift
        out_ref[1:2, :] = jnp.maximum(around, 0.0)


def stat_kernel(pos_ref, live_ref, offsets_ref, own_ref, sib_ref, far_ref, cross_ref, stat_ref):
    width = own_ref.shape[1]
    samples = pos_ref[4].astype(F32)

    def merged(values):
        return (values[0] + values[1]) + (values[2] + values[3])

    groups = (own_ref, sib_ref, far_ref, cross_ref)
    mean = merged([ref[0:1, :] for ref in groups]) * 0.25
    between = merged([jnp.square(ref[0:1, :] - mean) for ref in groups]) * (samples * 0.25)
    spread = (merged([ref[1:2, :] for ref in groups]) + between) / samples
    live = lax.broadcasted_iota(jnp.int32, (1, width), 1) < live_ref[0]
    stat_ref[0:1, :] = mean
    stat_ref[1:2, :] = jnp.where(live, lax.rsqrt(spread + 1e-05), 0.0)
    for step in (1, 2):
        listed = offsets_ref[0, 0] == step
        for slot in range(1, SLOTS):
            listed = jnp.logical_or(listed, offsets_ref[0, slot] == step)
        stat_ref[1 + step:2 + step, :] = jnp.full((1, width), jnp.where(listed, 1.0, 0.0), F32)


def own_kernel(pos_ref, x_ref, stat_ref, turned_ref, keep_ref, send_ref, acc):
    step = pl.program_id(0)
    z = standardized(x_ref[...], stat_ref)
    zt = z.T
    turned_ref[...] = zt
    part = dot(zt, z)

    @pl.when(step == 0)
    def _():
        acc[...] = part

    @pl.when(step > 0)
    def _():
        acc[...] += part

    @pl.when(step == pl.num_programs(0) - 1)
    def _():
        rows = keep_ref.shape[1]
        for far in range(2):
            for core, out in ((pos_ref[2], keep_ref), (1 - pos_ref[2], send_ref)):
                out[far] = acc[pl.ds(pl.multiple_of((2 * far + core) * rows, rows), rows), :]


def diag_kernel(pos_ref, keep_ref, got_ref, mine_ref, send_ref):
    mine_ref[...] = keep_ref[pos_ref[0]] + got_ref[pos_ref[0]]
    send_ref[...] = keep_ref[1 - pos_ref[0]] + got_ref[1 - pos_ref[0]]


def put_quarters(x, source, scale, keep, send):
    half = keep.shape[-1]
    scale = scale[:, :half]
    for out, near in ((keep, x), (send, 1 - x)):
        for index, (row, col) in enumerate(((near, near), (near, 1 - near), (1 - near, near))):
            rows = pl.ds(pl.multiple_of(row * half, half), half)
            cols = pl.ds(pl.multiple_of(col * half, half), half)
            out[index] = (source[rows, cols] * scale).astype(out.dtype)


def fetched(source, parts, sems):
    rows = parts.shape[1]
    copies = [pltpu.make_async_copy(source.at[pl.ds(k * rows, rows), :], parts.at[k], sems.at[k])
              for k in range(parts.shape[0])]
    for copy in copies:
        copy.start()
    return [(slice(k * rows, (k + 1) * rows), copy.wait) for k, copy in enumerate(copies)]


def far_kernel(pos_ref, turned_ref, w_ref, stat_ref, wstat_ref, keep_ref, send_ref, w_out, acc, parts, sems):
    chunks = fetched(w_ref, parts, sems)

    def ready(k):
        rows, wait = chunks[k]
        wait()
        w_out[rows, :] = standardized(parts[k], wstat_ref)

    ready(0)
    for k, (rows, _) in enumerate(chunks):
        if k + 1 < len(chunks):
            ready(k + 1)
        part = dot(turned_ref[:, rows], w_out[rows, :])
        acc[...] = part if k == 0 else acc[...] + part
    listed = jnp.where(pos_ref[2] == 0, stat_ref[3:4, :], wstat_ref[3:4, :])
    put_quarters(pos_ref[0], acc, listed * (1.0 / pos_ref[4].astype(F32)), keep_ref, send_ref)


def near_kernel(pos_ref, turned_ref, y_ref, stat_ref, ystat_ref, keep_ref, send_ref, y_out, acc, parts, sems):
    @pl.when(pos_ref[1] == 1)
    def _():
        chunks = fetched(y_ref, parts, sems)

        def ready(k):
            rows, wait = chunks[k]
            wait()
            parts[k] = standardized(parts[k], ystat_ref)
            y_out[:, rows] = parts[k].T

        ready(0)
        for k, (rows, _) in enumerate(chunks):
            if k + 1 < len(chunks):
                ready(k + 1)
            part = dot(turned_ref[:, rows], parts[k])
            acc[...] = part if k == 0 else acc[...] + part
        listed = jnp.where(pos_ref[2] == 0, stat_ref[2:3, :], ystat_ref[2:3, :])
        put_quarters(pos_ref[0], acc, listed * (1.0 / pos_ref[4].astype(F32)), keep_ref, send_ref)


def cross_kernel(steps, pos_ref, y_ref, w_ref, ystat_ref, wstat_ref, keep_ref, send_ref, acc):
    @pl.when(pos_ref[1] == 1)
    def _():
        size = w_ref.shape[0] // steps
        for k in range(steps):
            rows = slice(k * size, (k + 1) * size)
            part = dot(y_ref[:, rows], w_ref[rows, :])
            acc[...] = part if k == 0 else acc[...] + part
        listed = jnp.where(pos_ref[2] == 0, ystat_ref[2:3, :], wstat_ref[2:3, :])
        put_quarters(pos_ref[0], acc, listed * (1.0 / pos_ref[4].astype(F32)), keep_ref, send_ref)


def add_halves(x, keep, got, rows_out, cols_out):
    half = keep.shape[-1]
    here = pl.ds(pl.multiple_of(x * half, half), half)
    there = pl.ds(pl.multiple_of((1 - x) * half, half), half)
    corner = keep[0] + got[0].astype(F32)
    rows_out[:, here] = corner.astype(rows_out.dtype)
    rows_out[:, there] = (keep[1] + got[1].astype(F32)).astype(rows_out.dtype)
    cols_out[:, here] = corner.T.astype(cols_out.dtype)
    cols_out[:, there] = (keep[2] + got[2].astype(F32)).T.astype(cols_out.dtype)


def far_strips_kernel(pos_ref, keep, got, held, to_z):
    add_halves(pos_ref[0], keep, got, held, to_z)


def near_strips_kernel(pos_ref, keep, got, rows_out, cols_out):
    @pl.when(pos_ref[1] == 1)
    def _():
        add_halves(pos_ref[0], keep, got, rows_out, cols_out)


def combine_kernel(pos_ref, held_b, held_c, from_y_b, from_y_d, from_z_c, from_z_d, mine, sib):
    rows = mine.shape[1]
    for core, out in ((pos_ref[2], mine), (1 - pos_ref[2], sib)):
        at = pl.ds(pl.multiple_of(core * rows, rows), rows)
        out[1] = held_c[at, :] + from_z_c[at, :]

        @pl.when(pos_ref[1] == 1)
        def _():
            out[0] = held_b[at, :] + from_y_b[at, :]
            out[2] = from_y_d[at, :].astype(F32)

        @pl.when(pos_ref[1] == 0)
        def _():
            out[2] = from_z_d[at, :].astype(F32)


def finish_kernel(pos_ref, offsets_ref, diag_mine, diag_got, mine, sib, upper, mirror):
    active = pos_ref[1] == 1
    first_core = pos_ref[2] == 0
    even = pos_ref[3] == 0
    pick = jnp.where
    near = pick(active, mine[0], sib[0])
    far = mine[2] + sib[2]
    upper_1 = pick(even, near, far)
    upper_2 = pick(first_core, mine[1], sib[1])
    mirror[0, 0] = pick(even, far, near).astype(BF16)
    mirror[0, 1] = pick(first_core, sib[1], mine[1]).astype(BF16)
    self_tile = (diag_mine[...] + diag_got[...]) * (1.0 / pos_ref[4].astype(F32))
    for slot in range(SLOTS):
        offset = offsets_ref[0, slot]
        tile = pick(offset == 0, self_tile, pick(offset == 1, upper_1, pick(offset == 2, upper_2, 0.0)))
        upper[0, slot] = tile.astype(BF16)


def body(dosage, pair_offsets, live_counts):
    n_var = lax.axis_size("var")
    n_samp = lax.axis_size("samp")
    depth, width = dosage.shape
    half = width // 2
    strip = width // n_samp
    samples_all = depth * n_samp
    v = lax.axis_index("var")
    s = lax.axis_index("samp")
    x, core, odd = s // 2, s % 2, v % 2
    active = (core == odd).astype(jnp.int32)

    def at(var, samp):
        return var * n_samp + samp

    def active_on(var, samp):
        return var % 2 == samp % 2

    def send(value, pairs):
        return lax.ppermute(value, AXES, pairs)

    def shape(*dims, dtype=F32):
        return jax.ShapeDtypeStruct(dims, dtype)

    everyone = [(var, samp) for var in range(n_var) for samp in range(n_samp)]
    z_main = [(at(a, b), at(a - 2 if b % 2 == 0 else a + 2, b)) for a, b in everyone
              if 0 <= (a - 2 if b % 2 == 0 else a + 2) < n_var]
    y_main = [(at(a, b), at(a ^ 1, b)) for a, b in everyone if not active_on(a, b)]
    z_step = [(a, b, a + 2 if b % 2 == 0 else a - 2) for a, b in everyone]
    z_cross = [(at(a, b), at(t, b ^ 1)) for a, b, t in z_step if 0 <= t < n_var]
    z_cross_active = [(at(a, b), at(t, b ^ 1)) for a, b, t in z_step if 0 <= t < n_var and active_on(a, b)]
    y_cross = [(at(a, b), at(a ^ 1, b ^ 1)) for a, b in everyone if active_on(a, b)]
    across = [(at(a, b), at(a, b ^ 2)) for a, b in everyone]
    across_active = [(at(a, b), at(a, b ^ 2)) for a, b in everyone if active_on(a, b)]
    sibling = [(at(a, b), at(a, b ^ 1)) for a, b in everyone]

    w_raw, y_raw = send(dosage, z_main), send(dosage, y_main)

    pos = jnp.stack([x, active, core, odd, jnp.int32(samples_all)]).astype(jnp.int32)
    step_rows = min(1024, depth)
    steps = depth // step_rows
    wide = pl.BlockSpec((step_rows, width), lambda k: (k, 0))
    flat = pl.BlockSpec((width, step_rows), lambda k: (0, k))
    whole = lambda *dims: pl.BlockSpec(dims, lambda k: (0,) * len(dims))

    def call(kernel, name, grid, in_specs, out_specs, out_shape, scratch=(), flops=0, moved=0):
        return pl.pallas_call(
            kernel, grid=grid, in_specs=in_specs, out_specs=out_specs, out_shape=out_shape, scratch_shapes=scratch,
            compiler_params=SOME, name=name,
            cost_estimate=pl.CostEstimate(flops=flops, bytes_accessed=moved, transcendentals=0))

    bytes_block, tile_flops = 2 * depth * width, 2 * depth * width * width
    local = call(lambda *refs: local_kernel(steps, *refs), "local_stats", (steps,), [wide], whole(2, width), shape(2, width),
                 [pltpu.VMEM((1, width), F32)] + [pltpu.VMEM((8, width), F32)] * 2, 5 * depth * width, bytes_block)(dosage)
    others = [send(local, [(at(a, b), at(a, b ^ flip)) for a, b in everyone]) for flip in (1, 2, 3)]
    stat = call(stat_kernel, "stats", (), [SMEM] * 3 + [VMEM] * 4, VMEM, shape(4, width))(
        pos, live_counts, pair_offsets, local, *others)
    w_stat, y_stat = send(stat, z_cross), send(stat, y_cross)

    turned, diag_keep, diag_send = call(
        own_kernel, "own_tile", (steps,), [SMEM, wide, whole(4, width)],
        [flat, whole(2, strip, width), whole(2, strip, width)],
        [shape(width, depth, dtype=BF16), shape(2, strip, width), shape(2, strip, width)],
        [pltpu.VMEM((width, width), F32)], tile_flops, 2 * bytes_block)(pos, dosage, stat)
    diag_mine, diag_other = call(diag_kernel, "own_tile_strips", (), [SMEM, VMEM, VMEM], [VMEM] * 2, [shape(strip, width)] * 2)(
        pos, diag_keep, send(diag_send, sibling))
    diag_got = send(diag_other, across)

    anywhere = pl.BlockSpec(memory_space=pl.ANY)
    parts = [pltpu.VMEM((steps, step_rows, width), BF16), pltpu.SemaphoreType.DMA((steps,))]
    sums = pltpu.VMEM((width, width), F32)
    pair = [shape(3, half, half), shape(3, half, half, dtype=HALVES)]
    keep_c, send_c, w = call(
        far_kernel, "far_tile", (), [SMEM, VMEM, anywhere, VMEM, VMEM], [VMEM] * 3,
        pair + [shape(depth, width, dtype=BF16)], [sums] + parts, tile_flops, 3 * bytes_block)(
        pos, turned, w_raw, stat, w_stat)
    send_c, diag_got = lax.optimization_barrier((send_c, diag_got))
    got_c = send(send_c, across)

    keep_b, send_b, y = call(
        near_kernel, "near_tile", (), [SMEM, VMEM, anywhere, VMEM, VMEM], [VMEM] * 3,
        pair + [shape(width, depth, dtype=BF16)], [sums] + parts, tile_flops, 3 * bytes_block)(
        pos, turned, y_raw, stat, y_stat)
    got_b = send(send_b, across_active)
    keep_d, send_d = call(
        lambda *refs: cross_kernel(steps, *refs), "cross_tile", (), [SMEM] + [VMEM] * 4, [VMEM] * 2, pair, [sums],
        tile_flops, 2 * bytes_block)(pos, y, w, y_stat, w_stat)
    _, got_c = lax.optimization_barrier((send_d, got_c))
    got_d = send(send_d, across_active)

    held_c, to_z_c = call(far_strips_kernel, "far_strips", (), [SMEM] + [VMEM] * 2, [VMEM] * 2,
                          [shape(half, width)] * 2)(pos, keep_c, got_c)
    from_z_c = send(to_z_c, z_cross)
    got_b, to_z_c = lax.optimization_barrier((got_b, to_z_c))

    def near_strips(name, kind, keep, got):
        return call(near_strips_kernel, name, (), [SMEM] + [VMEM] * 2, [VMEM] * 2, [shape(half, width, dtype=kind)] * 2)(
            pos, keep, got)

    held_b, to_y_b = near_strips("near_strips", F32, keep_b, got_b)
    from_y_b = send(to_y_b, y_cross)
    got_d, to_y_b = lax.optimization_barrier((got_d, to_y_b))
    to_y_d, to_z_d = near_strips("cross_strips", CROSS, keep_d, got_d)
    from_y_d, from_z_d = send(to_y_d, y_cross), send(to_z_d, z_cross_active)

    mine, sib = call(combine_kernel, "combine", (), [SMEM] + [VMEM] * 6, [VMEM] * 2, [shape(3, strip, width)] * 2)(
        pos, held_b, held_c, from_y_b, from_y_d, from_z_c, from_z_d)
    return call(finish_kernel, "finish", (), [SMEM] * 2 + [VMEM] * 4, [VMEM] * 2,
                [shape(1, SLOTS, strip, width, dtype=BF16), shape(1, 2, strip, width, dtype=BF16)])(
        pos, pair_offsets, diag_mine, diag_got, mine, send(sib, sibling))


def solution(mesh):
    in_specs = (P("samp", "var"), P("var", None), P("var"))
    out_specs = (P("var", None, "samp", None), P("var", None, "samp", None))
    return jax.shard_map(body, mesh=mesh, in_specs=in_specs, out_specs=out_specs, check_vma=False)
```

```python
import jax
import jax.numpy as jnp
from jax import lax
from jax.experimental import pallas as pl
from jax.experimental.pallas import tpu as pltpu
from jax.sharding import PartitionSpec as P

SLOTS = 3
AXES = ("var", "samp")
F32 = jnp.float32
BF16 = jnp.bfloat16
VMEM = pl.BlockSpec(memory_space=pltpu.VMEM)
SMEM = pl.BlockSpec(memory_space=pltpu.SMEM)
SOME = pltpu.CompilerParams(vmem_limit_bytes=24 << 20)
HALVES, STRIPS = BF16, BF16


def dot(a, b):
    return jnp.dot(a, b, preferred_element_type=F32)


def standardized(raw, stat_ref):
    return ((raw.astype(F32) - stat_ref[0:1, :]) * stat_ref[1:2, :]).astype(BF16)


def local_kernel(steps, x_ref, out_ref, center, total, square):
    step = pl.program_id(0)
    rows, width = x_ref.shape
    group = min(64, rows)

    @pl.when(step == 0)
    def _():
        center[...] = jnp.mean(x_ref[:group, :].astype(F32), axis=0, keepdims=True)
        total[...] = jnp.zeros_like(total)
        square[...] = jnp.zeros_like(square)

    middle = center[...]

    def add(i, sums):
        x = x_ref[pl.ds(pl.multiple_of(i * group, group), group), :].astype(F32) - middle
        x = x.reshape(group // 8, 8, width)
        return sums[0] + jnp.sum(x, axis=0), sums[1] + jnp.sum(x * x, axis=0)

    sums = lax.fori_loop(0, rows // group, add, (total[...], square[...]))
    total[...], square[...] = sums

    @pl.when(step == steps - 1)
    def _():
        count = float(rows * steps)
        shift = jnp.sum(total[...], axis=0, keepdims=True) * (1.0 / count)
        around = jnp.sum(square[...], axis=0, keepdims=True) - shift * shift * count
        out_ref[0:1, :] = middle + shift
        out_ref[1:2, :] = jnp.maximum(around, 0.0)


def stat_kernel(pos_ref, live_ref, offsets_ref, own_ref, sib_ref, far_ref, cross_ref, stat_ref):
    width = own_ref.shape[1]
    samples = pos_ref[4].astype(F32)

    def merged(values):
        return (values[0] + values[1]) + (values[2] + values[3])

    groups = (own_ref, sib_ref, far_ref, cross_ref)
    mean = merged([ref[0:1, :] for ref in groups]) * 0.25
    between = merged([jnp.square(ref[0:1, :] - mean) for ref in groups]) * (samples * 0.25)
    spread = (merged([ref[1:2, :] for ref in groups]) + between) / samples
    live = lax.broadcasted_iota(jnp.int32, (1, width), 1) < live_ref[0]
    stat_ref[0:1, :] = mean
    stat_ref[1:2, :] = jnp.where(live, lax.rsqrt(spread + 1e-05), 0.0)
    for step in (1, 2):
        listed = offsets_ref[0, 0] == step
        for slot in range(1, SLOTS):
            listed = jnp.logical_or(listed, offsets_ref[0, slot] == step)
        stat_ref[1 + step:2 + step, :] = jnp.full((1, width), jnp.where(listed, 1.0, 0.0), F32)


def own_kernel(pos_ref, x_ref, stat_ref, turned_ref, keep_ref, send_ref, acc):
    step = pl.program_id(0)
    z = standardized(x_ref[...], stat_ref)
    zt = z.T
    turned_ref[...] = zt
    part = dot(zt, z)

    @pl.when(step == 0)
    def _():
        acc[...] = part

    @pl.when(step > 0)
    def _():
        acc[...] += part

    @pl.when(step == pl.num_programs(0) - 1)
    def _():
        rows = keep_ref.shape[1]
        for far in range(2):
            for core, out in ((pos_ref[2], keep_ref), (1 - pos_ref[2], send_ref)):
                out[far] = acc[pl.ds(pl.multiple_of((2 * far + core) * rows, rows), rows), :]


def diag_kernel(pos_ref, keep_ref, got_ref, mine_ref, send_ref):
    mine_ref[...] = keep_ref[pos_ref[0]] + got_ref[pos_ref[0]]
    send_ref[...] = keep_ref[1 - pos_ref[0]] + got_ref[1 - pos_ref[0]]


def put_quarters(x, source, scale, keep, send):
    half = keep.shape[-1]
    scale = scale[:, :half]
    for out, near in ((keep, x), (send, 1 - x)):
        for index, (row, col) in enumerate(((near, near), (near, 1 - near), (1 - near, near))):
            rows = pl.ds(pl.multiple_of(row * half, half), half)
            cols = pl.ds(pl.multiple_of(col * half, half), half)
            out[index] = (source[rows, cols] * scale).astype(out.dtype)


def fetched(source, parts, sems):
    rows = parts.shape[1]
    copies = [pltpu.make_async_copy(source.at[pl.ds(k * rows, rows), :], parts.at[k], sems.at[k])
              for k in range(parts.shape[0])]
    for copy in copies:
        copy.start()
    return [(slice(k * rows, (k + 1) * rows), copy.wait) for k, copy in enumerate(copies)]


def far_kernel(pos_ref, turned_ref, w_ref, stat_ref, wstat_ref, keep_ref, send_ref, w_out, acc, parts, sems):
    for k, (rows, wait) in enumerate(fetched(w_ref, parts, sems)):
        wait()
        w = standardized(parts[k], wstat_ref)
        w_out[rows, :] = w
        part = dot(turned_ref[:, rows], w)
        acc[...] = part if k == 0 else acc[...] + part
    listed = jnp.where(pos_ref[2] == 0, stat_ref[3:4, :], wstat_ref[3:4, :])
    put_quarters(pos_ref[0], acc, listed * (1.0 / pos_ref[4].astype(F32)), keep_ref, send_ref)


def near_kernel(pos_ref, turned_ref, y_ref, stat_ref, ystat_ref, keep_ref, send_ref, y_out, acc, parts, sems):
    @pl.when(pos_ref[1] == 1)
    def _():
        for k, (rows, wait) in enumerate(fetched(y_ref, parts, sems)):
            wait()
            y = standardized(parts[k], ystat_ref)
            y_out[:, rows] = y.T
            part = dot(turned_ref[:, rows], y)
            acc[...] = part if k == 0 else acc[...] + part
        listed = jnp.where(pos_ref[2] == 0, stat_ref[2:3, :], ystat_ref[2:3, :])
        put_quarters(pos_ref[0], acc, listed * (1.0 / pos_ref[4].astype(F32)), keep_ref, send_ref)


def cross_kernel(steps, pos_ref, y_ref, w_ref, ystat_ref, wstat_ref, keep_ref, send_ref, acc):
    @pl.when(pos_ref[1] == 1)
    def _():
        size = w_ref.shape[0] // steps
        for k in range(steps):
            rows = slice(k * size, (k + 1) * size)
            part = dot(y_ref[:, rows], w_ref[rows, :])
            acc[...] = part if k == 0 else acc[...] + part
        listed = jnp.where(pos_ref[2] == 0, ystat_ref[2:3, :], wstat_ref[2:3, :])
        put_quarters(pos_ref[0], acc, listed * (1.0 / pos_ref[4].astype(F32)), keep_ref, send_ref)


def add_halves(x, keep, got, rows_out, cols_out):
    half = keep.shape[-1]
    here = pl.ds(pl.multiple_of(x * half, half), half)
    there = pl.ds(pl.multiple_of((1 - x) * half, half), half)
    corner = keep[0] + got[0].astype(F32)
    rows_out[:, here] = corner.astype(rows_out.dtype)
    rows_out[:, there] = (keep[1] + got[1].astype(F32)).astype(rows_out.dtype)
    cols_out[:, here] = corner.T.astype(cols_out.dtype)
    cols_out[:, there] = (keep[2] + got[2].astype(F32)).T.astype(cols_out.dtype)


def far_strips_kernel(pos_ref, keep, got, held, to_z):
    add_halves(pos_ref[0], keep, got, held, to_z)


def near_strips_kernel(pos_ref, keep, got, rows_out, cols_out):
    @pl.when(pos_ref[1] == 1)
    def _():
        add_halves(pos_ref[0], keep, got, rows_out, cols_out)


def combine_kernel(pos_ref, held_b, held_c, from_y_b, from_y_d, from_z_c, from_z_d, mine, sib):
    rows = mine.shape[1]
    for core, out in ((pos_ref[2], mine), (1 - pos_ref[2], sib)):
        at = pl.ds(pl.multiple_of(core * rows, rows), rows)
        out[1] = held_c[at, :] + from_z_c[at, :].astype(F32)

        @pl.when(pos_ref[1] == 1)
        def _():
            out[0] = held_b[at, :] + from_y_b[at, :]
            out[2] = from_y_d[at, :].astype(F32)

        @pl.when(pos_ref[1] == 0)
        def _():
            out[2] = from_z_d[at, :].astype(F32)


def finish_kernel(pos_ref, offsets_ref, diag_mine, diag_got, mine, sib, upper, mirror):
    active = pos_ref[1] == 1
    first_core = pos_ref[2] == 0
    even = pos_ref[3] == 0
    pick = jnp.where
    near = pick(active, mine[0], sib[0])
    far = mine[2] + sib[2]
    upper_1 = pick(even, near, far)
    upper_2 = pick(first_core, mine[1], sib[1])
    mirror[0, 0] = pick(even, far, near).astype(BF16)
    mirror[0, 1] = pick(first_core, sib[1], mine[1]).astype(BF16)
    self_tile = (diag_mine[...] + diag_got[...]) * (1.0 / pos_ref[4].astype(F32))
    for slot in range(SLOTS):
        offset = offsets_ref[0, slot]
        tile = pick(offset == 0, self_tile, pick(offset == 1, upper_1, pick(offset == 2, upper_2, 0.0)))
        upper[0, slot] = tile.astype(BF16)


def body(dosage, pair_offsets, live_counts):
    n_var = lax.axis_size("var")
    n_samp = lax.axis_size("samp")
    depth, width = dosage.shape
    half = width // 2
    strip = width // n_samp
    samples_all = depth * n_samp
    v = lax.axis_index("var")
    s = lax.axis_index("samp")
    x, core, odd = s // 2, s % 2, v % 2
    active = (core == odd).astype(jnp.int32)

    def at(var, samp):
        return var * n_samp + samp

    def active_on(var, samp):
        return var % 2 == samp % 2

    def send(value, pairs):
        return lax.ppermute(value, AXES, pairs)

    def shape(*dims, dtype=F32):
        return jax.ShapeDtypeStruct(dims, dtype)

    everyone = [(var, samp) for var in range(n_var) for samp in range(n_samp)]
    z_main = [(at(a, b), at(a - 2 if b % 2 == 0 else a + 2, b)) for a, b in everyone
              if 0 <= (a - 2 if b % 2 == 0 else a + 2) < n_var]
    y_main = [(at(a, b), at(a ^ 1, b)) for a, b in everyone if not active_on(a, b)]
    z_step = [(a, b, a + 2 if b % 2 == 0 else a - 2) for a, b in everyone]
    z_cross = [(at(a, b), at(t, b ^ 1)) for a, b, t in z_step if 0 <= t < n_var]
    z_cross_active = [(at(a, b), at(t, b ^ 1)) for a, b, t in z_step if 0 <= t < n_var and active_on(a, b)]
    y_cross = [(at(a, b), at(a ^ 1, b ^ 1)) for a, b in everyone if active_on(a, b)]
    across = [(at(a, b), at(a, b ^ 2)) for a, b in everyone]
    across_active = [(at(a, b), at(a, b ^ 2)) for a, b in everyone if active_on(a, b)]
    sibling = [(at(a, b), at(a, b ^ 1)) for a, b in everyone]

    w_raw, y_raw = send(dosage, z_main), send(dosage, y_main)

    pos = jnp.stack([x, active, core, odd, jnp.int32(samples_all)]).astype(jnp.int32)
    step_rows = min(1024, depth)
    steps = depth // step_rows
    wide = pl.BlockSpec((step_rows, width), lambda k: (k, 0))
    flat = pl.BlockSpec((width, step_rows), lambda k: (0, k))
    whole = lambda *dims: pl.BlockSpec(dims, lambda k: (0,) * len(dims))

    def call(kernel, name, grid, in_specs, out_specs, out_shape, scratch=(), flops=0, moved=0):
        return pl.pallas_call(
            kernel, grid=grid, in_specs=in_specs, out_specs=out_specs, out_shape=out_shape, scratch_shapes=scratch,
            compiler_params=SOME, name=name,
            cost_estimate=pl.CostEstimate(flops=flops, bytes_accessed=moved, transcendentals=0))

    bytes_block, tile_flops = 2 * depth * width, 2 * depth * width * width
    local = call(lambda *refs: local_kernel(steps, *refs), "local_stats", (steps,), [wide], whole(2, width), shape(2, width),
                 [pltpu.VMEM((1, width), F32)] + [pltpu.VMEM((8, width), F32)] * 2, 5 * depth * width, bytes_block)(dosage)
    others = [send(local, [(at(a, b), at(a, b ^ flip)) for a, b in everyone]) for flip in (1, 2, 3)]
    stat = call(stat_kernel, "stats", (), [SMEM] * 3 + [VMEM] * 4, VMEM, shape(4, width))(
        pos, live_counts, pair_offsets, local, *others)
    w_stat, y_stat = send(stat, z_cross), send(stat, y_cross)

    turned, diag_keep, diag_send = call(
        own_kernel, "own_tile", (steps,), [SMEM, wide, whole(4, width)],
        [flat, whole(2, strip, width), whole(2, strip, width)],
        [shape(width, depth, dtype=BF16), shape(2, strip, width), shape(2, strip, width)],
        [pltpu.VMEM((width, width), F32)], tile_flops, 2 * bytes_block)(pos, dosage, stat)
    diag_mine, diag_other = call(diag_kernel, "own_tile_strips", (), [SMEM, VMEM, VMEM], [VMEM] * 2, [shape(strip, width)] * 2)(
        pos, diag_keep, send(diag_send, sibling))
    diag_got = send(diag_other, across)

    anywhere = pl.BlockSpec(memory_space=pl.ANY)
    parts = [pltpu.VMEM((steps, step_rows, width), BF16), pltpu.SemaphoreType.DMA((steps,))]
    sums = pltpu.VMEM((width, width), F32)
    pair = [shape(3, half, half), shape(3, half, half, dtype=HALVES)]
    keep_c, send_c, w = call(
        far_kernel, "far_tile", (), [SMEM, VMEM, anywhere, VMEM, VMEM], [VMEM] * 3,
        pair + [shape(depth, width, dtype=BF16)], [sums] + parts, tile_flops, 3 * bytes_block)(
        pos, turned, w_raw, stat, w_stat)
    send_c, diag_got = lax.optimization_barrier((send_c, diag_got))
    got_c = send(send_c, across)

    keep_b, send_b, y = call(
        near_kernel, "near_tile", (), [SMEM, VMEM, anywhere, VMEM, VMEM], [VMEM] * 3,
        pair + [shape(width, depth, dtype=BF16)], [sums] + parts, tile_flops, 3 * bytes_block)(
        pos, turned, y_raw, stat, y_stat)
    got_b = send(send_b, across_active)
    keep_d, send_d = call(
        lambda *refs: cross_kernel(steps, *refs), "cross_tile", (), [SMEM] + [VMEM] * 4, [VMEM] * 2, pair, [sums],
        tile_flops, 2 * bytes_block)(pos, y, w, y_stat, w_stat)
    send_d, got_c = lax.optimization_barrier((send_d, got_c))
    got_d = send(send_d, across_active)

    held_c, to_z_c = call(far_strips_kernel, "far_strips", (), [SMEM] + [VMEM] * 2, [VMEM] * 2,
                          [shape(half, width), shape(half, width, dtype=STRIPS)])(pos, keep_c, got_c)
    from_z_c = send(to_z_c, z_cross)
    got_b, to_z_c = lax.optimization_barrier((got_b, to_z_c))

    def near_strips(name, kind, keep, got):
        return call(near_strips_kernel, name, (), [SMEM] + [VMEM] * 2, [VMEM] * 2, [shape(half, width, dtype=kind)] * 2)(
            pos, keep, got)

    held_b, to_y_b = near_strips("near_strips", F32, keep_b, got_b)
    from_y_b = send(to_y_b, y_cross)
    got_d, to_y_b = lax.optimization_barrier((got_d, to_y_b))
    to_y_d, to_z_d = near_strips("cross_strips", STRIPS, keep_d, got_d)
    from_y_d, from_z_d = send(to_y_d, y_cross), send(to_z_d, z_cross_active)

    mine, sib = call(combine_kernel, "combine", (), [SMEM] + [VMEM] * 6, [VMEM] * 2, [shape(3, strip, width)] * 2)(
        pos, held_b, held_c, from_y_b, from_y_d, from_z_c, from_z_d)
    return call(finish_kernel, "finish", (), [SMEM] * 2 + [VMEM] * 4, [VMEM] * 2,
                [shape(1, SLOTS, strip, width, dtype=BF16), shape(1, 2, strip, width, dtype=BF16)])(
        pos, pair_offsets, diag_mine, diag_got, mine, send(sib, sibling))


def solution(mesh):
    in_specs = (P("samp", "var"), P("var", None), P("var"))
    out_specs = (P("var", None, "samp", None), P("var", None, "samp", None))
    return jax.shard_map(body, mesh=mesh, in_specs=in_specs, out_specs=out_specs, check_vma=False)
```

```python
import jax
import jax.numpy as jnp
from jax import lax
from jax.experimental import pallas as pl
from jax.experimental.pallas import tpu as pltpu
from jax.sharding import PartitionSpec as P

SLOTS = 3
AXES = ("var", "samp")
F32 = jnp.float32
BF16 = jnp.bfloat16
VMEM = pl.BlockSpec(memory_space=pltpu.VMEM)
SMEM = pl.BlockSpec(memory_space=pltpu.SMEM)
SOME = pltpu.CompilerParams(vmem_limit_bytes=24 << 20)
HALVES, STRIPS = BF16, BF16


def dot(a, b):
    return jnp.dot(a, b, preferred_element_type=F32)


def standardized(raw, stat_ref):
    return ((raw.astype(F32) - stat_ref[0:1, :]) * stat_ref[1:2, :]).astype(BF16)


def local_kernel(steps, x_ref, out_ref, center, total, square):
    step = pl.program_id(0)
    rows, width = x_ref.shape
    group = min(64, rows)

    @pl.when(step == 0)
    def _():
        center[...] = jnp.mean(x_ref[:group, :].astype(F32), axis=0, keepdims=True)
        total[...] = jnp.zeros_like(total)
        square[...] = jnp.zeros_like(square)

    middle = center[...]

    def add(i, sums):
        x = x_ref[pl.ds(pl.multiple_of(i * group, group), group), :].astype(F32) - middle
        x = x.reshape(group // 8, 8, width)
        return sums[0] + jnp.sum(x, axis=0), sums[1] + jnp.sum(x * x, axis=0)

    sums = lax.fori_loop(0, rows // group, add, (total[...], square[...]))
    total[...], square[...] = sums

    @pl.when(step == steps - 1)
    def _():
        count = float(rows * steps)
        shift = jnp.sum(total[...], axis=0, keepdims=True) * (1.0 / count)
        around = jnp.sum(square[...], axis=0, keepdims=True) - shift * shift * count
        out_ref[0:1, :] = middle + shift
        out_ref[1:2, :] = jnp.maximum(around, 0.0)


def stat_kernel(pos_ref, live_ref, offsets_ref, own_ref, sib_ref, far_ref, cross_ref, stat_ref):
    width = own_ref.shape[1]
    samples = pos_ref[4].astype(F32)

    def merged(values):
        return (values[0] + values[1]) + (values[2] + values[3])

    groups = (own_ref, sib_ref, far_ref, cross_ref)
    mean = merged([ref[0:1, :] for ref in groups]) * 0.25
    between = merged([jnp.square(ref[0:1, :] - mean) for ref in groups]) * (samples * 0.25)
    spread = (merged([ref[1:2, :] for ref in groups]) + between) / samples
    live = lax.broadcasted_iota(jnp.int32, (1, width), 1) < live_ref[0]
    stat_ref[0:1, :] = mean
    stat_ref[1:2, :] = jnp.where(live, lax.rsqrt(spread + 1e-05), 0.0)
    for step in (1, 2):
        listed = offsets_ref[0, 0] == step
        for slot in range(1, SLOTS):
            listed = jnp.logical_or(listed, offsets_ref[0, slot] == step)
        stat_ref[1 + step:2 + step, :] = jnp.full((1, width), jnp.where(listed, 1.0, 0.0), F32)


def own_kernel(pos_ref, x_ref, stat_ref, turned_ref, keep_ref, send_ref, acc):
    step = pl.program_id(0)
    z = standardized(x_ref[...], stat_ref)
    zt = z.T
    turned_ref[...] = zt
    part = dot(zt, z)

    @pl.when(step == 0)
    def _():
        acc[...] = part

    @pl.when(step > 0)
    def _():
        acc[...] += part

    @pl.when(step == pl.num_programs(0) - 1)
    def _():
        rows = keep_ref.shape[1]
        for far in range(2):
            for core, out in ((pos_ref[2], keep_ref), (1 - pos_ref[2], send_ref)):
                out[far] = acc[pl.ds(pl.multiple_of((2 * far + core) * rows, rows), rows), :]


def diag_kernel(pos_ref, keep_ref, got_ref, mine_ref, send_ref):
    mine_ref[...] = keep_ref[pos_ref[0]] + got_ref[pos_ref[0]]
    send_ref[...] = keep_ref[1 - pos_ref[0]] + got_ref[1 - pos_ref[0]]


def put_quarters(x, source, scale, keep, send):
    half = keep.shape[-1]
    scale = scale[:, :half]
    for out, near in ((keep, x), (send, 1 - x)):
        for index, (row, col) in enumerate(((near, near), (near, 1 - near), (1 - near, near))):
            rows = pl.ds(pl.multiple_of(row * half, half), half)
            cols = pl.ds(pl.multiple_of(col * half, half), half)
            out[index] = (source[rows, cols] * scale).astype(out.dtype)


def fetched(source, parts, sems):
    rows = parts.shape[1]
    copies = [pltpu.make_async_copy(source.at[pl.ds(k * rows, rows), :], parts.at[k], sems.at[k])
              for k in range(parts.shape[0])]
    for copy in copies:
        copy.start()
    return [(slice(k * rows, (k + 1) * rows), copy.wait) for k, copy in enumerate(copies)]


def far_kernel(pos_ref, turned_ref, w_ref, stat_ref, wstat_ref, keep_ref, send_ref, w_out, acc, parts, sems):
    for k, (rows, wait) in enumerate(fetched(w_ref, parts, sems)):
        wait()
        w = standardized(parts[k], wstat_ref)
        w_out[rows, :] = w
        part = dot(turned_ref[:, rows], w)
        acc[...] = part if k == 0 else acc[...] + part
    listed = jnp.where(pos_ref[2] == 0, stat_ref[3:4, :], wstat_ref[3:4, :])
    put_quarters(pos_ref[0], acc, listed * (1.0 / pos_ref[4].astype(F32)), keep_ref, send_ref)


def near_kernel(pos_ref, turned_ref, y_ref, stat_ref, ystat_ref, keep_ref, send_ref, y_out, acc, parts, sems):
    @pl.when(pos_ref[1] == 1)
    def _():
        for k, (rows, wait) in enumerate(fetched(y_ref, parts, sems)):
            wait()
            y = standardized(parts[k], ystat_ref)
            y_out[:, rows] = y.T
            part = dot(turned_ref[:, rows], y)
            acc[...] = part if k == 0 else acc[...] + part
        listed = jnp.where(pos_ref[2] == 0, stat_ref[2:3, :], ystat_ref[2:3, :])
        put_quarters(pos_ref[0], acc, listed * (1.0 / pos_ref[4].astype(F32)), keep_ref, send_ref)


def cross_kernel(steps, pos_ref, y_ref, w_ref, ystat_ref, wstat_ref, keep_ref, send_ref, acc):
    @pl.when(pos_ref[1] == 1)
    def _():
        size = w_ref.shape[0] // steps
        for k in range(steps):
            rows = slice(k * size, (k + 1) * size)
            part = dot(y_ref[:, rows], w_ref[rows, :])
            acc[...] = part if k == 0 else acc[...] + part
        listed = jnp.where(pos_ref[2] == 0, ystat_ref[2:3, :], wstat_ref[2:3, :])
        put_quarters(pos_ref[0], acc, listed * (1.0 / pos_ref[4].astype(F32)), keep_ref, send_ref)


def add_halves(x, keep, got, rows_out, cols_out):
    half = keep.shape[-1]
    here = pl.ds(pl.multiple_of(x * half, half), half)
    there = pl.ds(pl.multiple_of((1 - x) * half, half), half)
    corner = keep[0] + got[0].astype(F32)
    rows_out[:, here] = corner.astype(rows_out.dtype)
    rows_out[:, there] = (keep[1] + got[1].astype(F32)).astype(rows_out.dtype)
    cols_out[:, here] = corner.T.astype(cols_out.dtype)
    cols_out[:, there] = (keep[2] + got[2].astype(F32)).T.astype(cols_out.dtype)


def far_strips_kernel(pos_ref, keep, got, held, to_z):
    add_halves(pos_ref[0], keep, got, held, to_z)


def near_strips_kernel(pos_ref, keep, got, rows_out, cols_out):
    @pl.when(pos_ref[1] == 1)
    def _():
        add_halves(pos_ref[0], keep, got, rows_out, cols_out)


def combine_kernel(pos_ref, held_b, held_c, from_y_b, from_y_d, from_z_c, from_z_d, mine, sib):
    rows = mine.shape[1]
    for core, out in ((pos_ref[2], mine), (1 - pos_ref[2], sib)):
        at = pl.ds(pl.multiple_of(core * rows, rows), rows)
        out[1] = held_c[at, :] + from_z_c[at, :].astype(F32)

        @pl.when(pos_ref[1] == 1)
        def _():
            out[0] = held_b[at, :] + from_y_b[at, :]
            out[2] = from_y_d[at, :].astype(F32)

        @pl.when(pos_ref[1] == 0)
        def _():
            out[2] = from_z_d[at, :].astype(F32)


def finish_kernel(pos_ref, offsets_ref, diag_mine, diag_got, mine, sib, upper, mirror):
    active = pos_ref[1] == 1
    first_core = pos_ref[2] == 0
    even = pos_ref[3] == 0
    pick = jnp.where
    near = pick(active, mine[0], sib[0])
    far = mine[2] + sib[2]
    upper_1 = pick(even, near, far)
    upper_2 = pick(first_core, mine[1], sib[1])
    mirror[0, 0] = pick(even, far, near).astype(BF16)
    mirror[0, 1] = pick(first_core, sib[1], mine[1]).astype(BF16)
    self_tile = (diag_mine[...] + diag_got[...]) * (1.0 / pos_ref[4].astype(F32))
    for slot in range(SLOTS):
        offset = offsets_ref[0, slot]
        tile = pick(offset == 0, self_tile, pick(offset == 1, upper_1, pick(offset == 2, upper_2, 0.0)))
        upper[0, slot] = tile.astype(BF16)


def body(dosage, pair_offsets, live_counts):
    n_var = lax.axis_size("var")
    n_samp = lax.axis_size("samp")
    depth, width = dosage.shape
    half = width // 2
    strip = width // n_samp
    samples_all = depth * n_samp
    v = lax.axis_index("var")
    s = lax.axis_index("samp")
    x, core, odd = s // 2, s % 2, v % 2
    active = (core == odd).astype(jnp.int32)

    def at(var, samp):
        return var * n_samp + samp

    def active_on(var, samp):
        return var % 2 == samp % 2

    def send(value, pairs):
        return lax.ppermute(value, AXES, pairs)

    def shape(*dims, dtype=F32):
        return jax.ShapeDtypeStruct(dims, dtype)

    everyone = [(var, samp) for var in range(n_var) for samp in range(n_samp)]
    z_main = [(at(a, b), at(a - 2 if b % 2 == 0 else a + 2, b)) for a, b in everyone
              if 0 <= (a - 2 if b % 2 == 0 else a + 2) < n_var]
    y_main = [(at(a, b), at(a ^ 1, b)) for a, b in everyone if not active_on(a, b)]
    z_step = [(a, b, a + 2 if b % 2 == 0 else a - 2) for a, b in everyone]
    z_cross = [(at(a, b), at(t, b ^ 1)) for a, b, t in z_step if 0 <= t < n_var]
    z_cross_active = [(at(a, b), at(t, b ^ 1)) for a, b, t in z_step if 0 <= t < n_var and active_on(a, b)]
    y_cross = [(at(a, b), at(a ^ 1, b ^ 1)) for a, b in everyone if active_on(a, b)]
    across = [(at(a, b), at(a, b ^ 2)) for a, b in everyone]
    across_active = [(at(a, b), at(a, b ^ 2)) for a, b in everyone if active_on(a, b)]
    sibling = [(at(a, b), at(a, b ^ 1)) for a, b in everyone]

    w_raw, y_raw = send(dosage, z_main), send(dosage, y_main)

    pos = jnp.stack([x, active, core, odd, jnp.int32(samples_all)]).astype(jnp.int32)
    step_rows = min(1024, depth)
    steps = depth // step_rows
    wide = pl.BlockSpec((step_rows, width), lambda k: (k, 0))
    flat = pl.BlockSpec((width, step_rows), lambda k: (0, k))
    whole = lambda *dims: pl.BlockSpec(dims, lambda k: (0,) * len(dims))

    def call(kernel, name, grid, in_specs, out_specs, out_shape, scratch=(), flops=0, moved=0):
        return pl.pallas_call(
            kernel, grid=grid, in_specs=in_specs, out_specs=out_specs, out_shape=out_shape, scratch_shapes=scratch,
            compiler_params=SOME, name=name,
            cost_estimate=pl.CostEstimate(flops=flops, bytes_accessed=moved, transcendentals=0))

    bytes_block, tile_flops = 2 * depth * width, 2 * depth * width * width
    local = call(lambda *refs: local_kernel(steps, *refs), "local_stats", (steps,), [wide], whole(2, width), shape(2, width),
                 [pltpu.VMEM((1, width), F32)] + [pltpu.VMEM((8, width), F32)] * 2, 5 * depth * width, bytes_block)(dosage)
    others = [send(local, [(at(a, b), at(a, b ^ flip)) for a, b in everyone]) for flip in (1, 2, 3)]
    stat = call(stat_kernel, "stats", (), [SMEM] * 3 + [VMEM] * 4, VMEM, shape(4, width))(
        pos, live_counts, pair_offsets, local, *others)
    w_stat, y_stat = send(stat, z_cross), send(stat, y_cross)

    turned, diag_keep, diag_send = call(
        own_kernel, "own_tile", (steps,), [SMEM, wide, whole(4, width)],
        [flat, whole(2, strip, width), whole(2, strip, width)],
        [shape(width, depth, dtype=BF16), shape(2, strip, width), shape(2, strip, width)],
        [pltpu.VMEM((width, width), F32)], tile_flops, 2 * bytes_block)(pos, dosage, stat)
    diag_mine, diag_other = call(diag_kernel, "own_tile_strips", (), [SMEM, VMEM, VMEM], [VMEM] * 2, [shape(strip, width)] * 2)(
        pos, diag_keep, send(diag_send, sibling))
    diag_got = send(diag_other, across)

    anywhere = pl.BlockSpec(memory_space=pl.ANY)
    parts = [pltpu.VMEM((steps, step_rows, width), BF16), pltpu.SemaphoreType.DMA((steps,))]
    sums = pltpu.VMEM((width, width), F32)
    pair = [shape(3, half, half), shape(3, half, half, dtype=HALVES)]
    keep_c, send_c, w = call(
        far_kernel, "far_tile", (), [SMEM, VMEM, anywhere, VMEM, VMEM], [VMEM] * 3,
        pair + [shape(depth, width, dtype=BF16)], [sums] + parts, tile_flops, 3 * bytes_block)(
        pos, turned, w_raw, stat, w_stat)
    send_c, diag_got = lax.optimization_barrier((send_c, diag_got))
    got_c = send(send_c, across)

    keep_b, send_b, y = call(
        near_kernel, "near_tile", (), [SMEM, VMEM, anywhere, VMEM, VMEM], [VMEM] * 3,
        pair + [shape(width, depth, dtype=BF16)], [sums] + parts, tile_flops, 3 * bytes_block)(
        pos, turned, y_raw, stat, y_stat)
    got_b = send(send_b, across_active)
    keep_d, send_d = call(
        lambda *refs: cross_kernel(steps, *refs), "cross_tile", (), [SMEM] + [VMEM] * 4, [VMEM] * 2, pair, [sums],
        tile_flops, 2 * bytes_block)(pos, y, w, y_stat, w_stat)
    send_d, got_c = lax.optimization_barrier((send_d, got_c))
    got_d = send(send_d, across_active)

    held_c, to_z_c = call(far_strips_kernel, "far_strips", (), [SMEM] + [VMEM] * 2, [VMEM] * 2,
                          [shape(half, width), shape(half, width, dtype=STRIPS)])(pos, keep_c, got_c)
    from_z_c = send(to_z_c, z_cross)
    got_b, to_z_c = lax.optimization_barrier((got_b, to_z_c))

    def near_strips(name, kind, keep, got):
        return call(near_strips_kernel, name, (), [SMEM] + [VMEM] * 2, [VMEM] * 2, [shape(half, width, dtype=kind)] * 2)(
            pos, keep, got)

    held_b, to_y_b = near_strips("near_strips", F32, keep_b, got_b)
    from_y_b = send(to_y_b, y_cross)
    got_d, to_y_b = lax.optimization_barrier((got_d, to_y_b))
    to_y_d, to_z_d = near_strips("cross_strips", STRIPS, keep_d, got_d)
    from_y_d, from_z_d = send(to_y_d, y_cross), send(to_z_d, z_cross_active)

    from_z_d, from_z_c = lax.optimization_barrier((from_z_d, from_z_c))
    mine, sib = call(combine_kernel, "combine", (), [SMEM] + [VMEM] * 6, [VMEM] * 2, [shape(3, strip, width)] * 2)(
        pos, held_b, held_c, from_y_b, from_y_d, from_z_c, from_z_d)
    return call(finish_kernel, "finish", (), [SMEM] * 2 + [VMEM] * 4, [VMEM] * 2,
                [shape(1, SLOTS, strip, width, dtype=BF16), shape(1, 2, strip, width, dtype=BF16)])(
        pos, pair_offsets, diag_mine, diag_got, mine, send(sib, sibling))


def solution(mesh):
    in_specs = (P("samp", "var"), P("var", None), P("var"))
    out_specs = (P("var", None, "samp", None), P("var", None, "samp", None))
    return jax.shard_map(body, mesh=mesh, in_specs=in_specs, out_specs=out_specs, check_vma=False)
```

```python
import jax
import jax.numpy as jnp
from jax import lax
from jax.experimental import pallas as pl
from jax.experimental.pallas import tpu as pltpu
from jax.sharding import PartitionSpec as P

SLOTS = 3
AXES = ("var", "samp")
F32 = jnp.float32
BF16 = jnp.bfloat16
VMEM = pl.BlockSpec(memory_space=pltpu.VMEM)
SMEM = pl.BlockSpec(memory_space=pltpu.SMEM)
SOME = pltpu.CompilerParams(vmem_limit_bytes=24 << 20)
HALVES, STRIPS = BF16, BF16


def dot(a, b):
    return jnp.dot(a, b, preferred_element_type=F32)


def standardized(raw, stat_ref):
    return ((raw.astype(F32) - stat_ref[0:1, :]) * stat_ref[1:2, :]).astype(BF16)


def local_kernel(steps, x_ref, out_ref, center, total, square):
    step = pl.program_id(0)
    rows, width = x_ref.shape
    group = min(64, rows)

    @pl.when(step == 0)
    def _():
        center[...] = jnp.mean(x_ref[:group, :].astype(F32), axis=0, keepdims=True)
        total[...] = jnp.zeros_like(total)
        square[...] = jnp.zeros_like(square)

    middle = center[...]

    def add(i, sums):
        x = x_ref[pl.ds(pl.multiple_of(i * group, group), group), :].astype(F32) - middle
        x = x.reshape(group // 8, 8, width)
        return sums[0] + jnp.sum(x, axis=0), sums[1] + jnp.sum(x * x, axis=0)

    sums = lax.fori_loop(0, rows // group, add, (total[...], square[...]))
    total[...], square[...] = sums

    @pl.when(step == steps - 1)
    def _():
        count = float(rows * steps)
        shift = jnp.sum(total[...], axis=0, keepdims=True) * (1.0 / count)
        around = jnp.sum(square[...], axis=0, keepdims=True) - shift * shift * count
        out_ref[0:1, :] = middle + shift
        out_ref[1:2, :] = jnp.maximum(around, 0.0)


def stat_kernel(pos_ref, live_ref, offsets_ref, own_ref, sib_ref, far_ref, cross_ref, stat_ref):
    width = own_ref.shape[1]
    samples = pos_ref[4].astype(F32)

    def merged(values):
        return (values[0] + values[1]) + (values[2] + values[3])

    groups = (own_ref, sib_ref, far_ref, cross_ref)
    mean = merged([ref[0:1, :] for ref in groups]) * 0.25
    between = merged([jnp.square(ref[0:1, :] - mean) for ref in groups]) * (samples * 0.25)
    spread = (merged([ref[1:2, :] for ref in groups]) + between) / samples
    live = lax.broadcasted_iota(jnp.int32, (1, width), 1) < live_ref[0]
    stat_ref[0:1, :] = mean
    stat_ref[1:2, :] = jnp.where(live, lax.rsqrt(spread + 1e-05), 0.0)
    for step in (1, 2):
        listed = offsets_ref[0, 0] == step
        for slot in range(1, SLOTS):
            listed = jnp.logical_or(listed, offsets_ref[0, slot] == step)
        stat_ref[1 + step:2 + step, :] = jnp.full((1, width), jnp.where(listed, 1.0, 0.0), F32)


def own_kernel(pos_ref, x_ref, stat_ref, turned_ref, keep_ref, send_ref, acc):
    step = pl.program_id(0)
    z = standardized(x_ref[...], stat_ref)
    zt = z.T
    turned_ref[...] = zt
    part = dot(zt, z)

    @pl.when(step == 0)
    def _():
        acc[...] = part

    @pl.when(step > 0)
    def _():
        acc[...] += part

    @pl.when(step == pl.num_programs(0) - 1)
    def _():
        rows = keep_ref.shape[1]
        for far in range(2):
            for core, out in ((pos_ref[2], keep_ref), (1 - pos_ref[2], send_ref)):
                out[far] = acc[pl.ds(pl.multiple_of((2 * far + core) * rows, rows), rows), :]


def diag_kernel(pos_ref, keep_ref, got_ref, mine_ref, send_ref):
    mine_ref[...] = keep_ref[pos_ref[0]] + got_ref[pos_ref[0]]
    send_ref[...] = keep_ref[1 - pos_ref[0]] + got_ref[1 - pos_ref[0]]


def put_quarters(x, source, scale, keep, send):
    half = keep.shape[-1]
    scale = scale[:, :half]
    for out, near in ((keep, x), (send, 1 - x)):
        for index, (row, col) in enumerate(((near, near), (near, 1 - near), (1 - near, near))):
            rows = pl.ds(pl.multiple_of(row * half, half), half)
            cols = pl.ds(pl.multiple_of(col * half, half), half)
            out[index] = (source[rows, cols] * scale).astype(out.dtype)


def fetched(source, parts, sems):
    rows = parts.shape[1]
    copies = [pltpu.make_async_copy(source.at[pl.ds(k * rows, rows), :], parts.at[k], sems.at[k])
              for k in range(parts.shape[0])]
    for copy in copies:
        copy.start()
    return [(slice(k * rows, (k + 1) * rows), copy.wait) for k, copy in enumerate(copies)]


def far_kernel(pos_ref, turned_ref, w_ref, stat_ref, wstat_ref, keep_ref, send_ref, w_out, acc, parts, sems):
    for k, (rows, wait) in enumerate(fetched(w_ref, parts, sems)):
        wait()
        w = standardized(parts[k], wstat_ref)
        w_out[rows, :] = w
        part = dot(turned_ref[:, rows], w)
        acc[...] = part if k == 0 else acc[...] + part
    listed = jnp.where(pos_ref[2] == 0, stat_ref[3:4, :], wstat_ref[3:4, :])
    put_quarters(pos_ref[0], acc, listed * (1.0 / pos_ref[4].astype(F32)), keep_ref, send_ref)


def near_kernel(pos_ref, turned_ref, y_ref, stat_ref, ystat_ref, keep_ref, send_ref, y_out, acc, parts, sems):
    @pl.when(pos_ref[1] == 1)
    def _():
        for k, (rows, wait) in enumerate(fetched(y_ref, parts, sems)):
            wait()
            y = standardized(parts[k], ystat_ref)
            y_out[:, rows] = y.T
            part = dot(turned_ref[:, rows], y)
            acc[...] = part if k == 0 else acc[...] + part
        listed = jnp.where(pos_ref[2] == 0, stat_ref[2:3, :], ystat_ref[2:3, :])
        put_quarters(pos_ref[0], acc, listed * (1.0 / pos_ref[4].astype(F32)), keep_ref, send_ref)


def cross_kernel(steps, pos_ref, y_ref, w_ref, ystat_ref, wstat_ref, keep_ref, send_ref, acc):
    @pl.when(pos_ref[1] == 1)
    def _():
        size = w_ref.shape[0] // steps
        for k in range(steps):
            rows = slice(k * size, (k + 1) * size)
            part = dot(y_ref[:, rows], w_ref[rows, :])
            acc[...] = part if k == 0 else acc[...] + part
        listed = jnp.where(pos_ref[2] == 0, ystat_ref[2:3, :], wstat_ref[2:3, :])
        put_quarters(pos_ref[0], acc, listed * (1.0 / pos_ref[4].astype(F32)), keep_ref, send_ref)


def add_halves(x, keep, got, rows_out, cols_out):
    half = keep.shape[-1]
    here = pl.ds(pl.multiple_of(x * half, half), half)
    there = pl.ds(pl.multiple_of((1 - x) * half, half), half)
    corner = keep[0] + got[0].astype(F32)
    rows_out[:, here] = corner.astype(rows_out.dtype)
    rows_out[:, there] = (keep[1] + got[1].astype(F32)).astype(rows_out.dtype)
    cols_out[:, here] = corner.T.astype(cols_out.dtype)
    cols_out[:, there] = (keep[2] + got[2].astype(F32)).T.astype(cols_out.dtype)


def far_strips_kernel(pos_ref, keep, got, held, to_z):
    add_halves(pos_ref[0], keep, got, held, to_z)


def near_strips_kernel(pos_ref, keep, got, rows_out, cols_out):
    @pl.when(pos_ref[1] == 1)
    def _():
        add_halves(pos_ref[0], keep, got, rows_out, cols_out)


def combine_kernel(pos_ref, held_b, held_c, from_y_b, from_y_d, from_z_c, from_z_d, mine, sib):
    rows = mine.shape[1]
    for core, out in ((pos_ref[2], mine), (1 - pos_ref[2], sib)):
        at = pl.ds(pl.multiple_of(core * rows, rows), rows)
        out[1] = held_c[at, :] + from_z_c[at, :].astype(F32)

        @pl.when(pos_ref[1] == 1)
        def _():
            out[0] = held_b[at, :] + from_y_b[at, :]
            out[2] = from_y_d[at, :].astype(F32)

        @pl.when(pos_ref[1] == 0)
        def _():
            out[2] = from_z_d[at, :].astype(F32)


def finish_kernel(pos_ref, offsets_ref, diag_mine, diag_got, mine, sib, upper, mirror):
    active = pos_ref[1] == 1
    first_core = pos_ref[2] == 0
    even = pos_ref[3] == 0
    pick = jnp.where
    near = pick(active, mine[0], sib[0])
    far = mine[2] + sib[2]
    upper_1 = pick(even, near, far)
    upper_2 = pick(first_core, mine[1], sib[1])
    mirror[0, 0] = pick(even, far, near).astype(BF16)
    mirror[0, 1] = pick(first_core, sib[1], mine[1]).astype(BF16)
    self_tile = (diag_mine[...] + diag_got[...]) * (1.0 / pos_ref[4].astype(F32))
    for slot in range(SLOTS):
        offset = offsets_ref[0, slot]
        tile = pick(offset == 0, self_tile, pick(offset == 1, upper_1, pick(offset == 2, upper_2, 0.0)))
        upper[0, slot] = tile.astype(BF16)


def body(dosage, pair_offsets, live_counts):
    n_var = lax.axis_size("var")
    n_samp = lax.axis_size("samp")
    depth, width = dosage.shape
    half = width // 2
    strip = width // n_samp
    samples_all = depth * n_samp
    v = lax.axis_index("var")
    s = lax.axis_index("samp")
    x, core, odd = s // 2, s % 2, v % 2
    active = (core == odd).astype(jnp.int32)

    def at(var, samp):
        return var * n_samp + samp

    def active_on(var, samp):
        return var % 2 == samp % 2

    def send(value, pairs):
        return lax.ppermute(value, AXES, pairs)

    def shape(*dims, dtype=F32):
        return jax.ShapeDtypeStruct(dims, dtype)

    everyone = [(var, samp) for var in range(n_var) for samp in range(n_samp)]
    z_main = [(at(a, b), at(a - 2 if b % 2 == 0 else a + 2, b)) for a, b in everyone
              if 0 <= (a - 2 if b % 2 == 0 else a + 2) < n_var]
    y_main = [(at(a, b), at(a ^ 1, b)) for a, b in everyone if not active_on(a, b)]
    z_step = [(a, b, a + 2 if b % 2 == 0 else a - 2) for a, b in everyone]
    z_cross = [(at(a, b), at(t, b ^ 1)) for a, b, t in z_step if 0 <= t < n_var]
    z_cross_active = [(at(a, b), at(t, b ^ 1)) for a, b, t in z_step if 0 <= t < n_var and active_on(a, b)]
    y_cross = [(at(a, b), at(a ^ 1, b ^ 1)) for a, b in everyone if active_on(a, b)]
    across = [(at(a, b), at(a, b ^ 2)) for a, b in everyone]
    across_active = [(at(a, b), at(a, b ^ 2)) for a, b in everyone if active_on(a, b)]
    sibling = [(at(a, b), at(a, b ^ 1)) for a, b in everyone]

    w_raw, y_raw = send(dosage, z_main), send(dosage, y_main)

    pos = jnp.stack([x, active, core, odd, jnp.int32(samples_all)]).astype(jnp.int32)
    step_rows = min(1024, depth)
    steps = depth // step_rows
    wide = pl.BlockSpec((step_rows, width), lambda k: (k, 0))
    flat = pl.BlockSpec((width, step_rows), lambda k: (0, k))
    whole = lambda *dims: pl.BlockSpec(dims, lambda k: (0,) * len(dims))

    def call(kernel, name, grid, in_specs, out_specs, out_shape, scratch=(), flops=0, moved=0):
        return pl.pallas_call(
            kernel, grid=grid, in_specs=in_specs, out_specs=out_specs, out_shape=out_shape, scratch_shapes=scratch,
            compiler_params=SOME, name=name,
            cost_estimate=pl.CostEstimate(flops=flops, bytes_accessed=moved, transcendentals=0))

    bytes_block, tile_flops = 2 * depth * width, 2 * depth * width * width
    local = call(lambda *refs: local_kernel(steps, *refs), "local_stats", (steps,), [wide], whole(2, width), shape(2, width),
                 [pltpu.VMEM((1, width), F32)] + [pltpu.VMEM((8, width), F32)] * 2, 5 * depth * width, bytes_block)(dosage)
    others = [send(local, [(at(a, b), at(a, b ^ flip)) for a, b in everyone]) for flip in (1, 2, 3)]
    stat = call(stat_kernel, "stats", (), [SMEM] * 3 + [VMEM] * 4, VMEM, shape(4, width))(
        pos, live_counts, pair_offsets, local, *others)
    w_stat, y_stat = send(stat, z_cross), send(stat, y_cross)

    turned, diag_keep, diag_send = call(
        own_kernel, "own_tile", (steps,), [SMEM, wide, whole(4, width)],
        [flat, whole(2, strip, width), whole(2, strip, width)],
        [shape(width, depth, dtype=BF16), shape(2, strip, width), shape(2, strip, width)],
        [pltpu.VMEM((width, width), F32)], tile_flops, 2 * bytes_block)(pos, dosage, stat)
    diag_mine, diag_other = call(diag_kernel, "own_tile_strips", (), [SMEM, VMEM, VMEM], [VMEM] * 2, [shape(strip, width)] * 2)(
        pos, diag_keep, send(diag_send, sibling))
    diag_got = send(diag_other, across)

    anywhere = pl.BlockSpec(memory_space=pl.ANY)
    parts = [pltpu.VMEM((2 * steps, step_rows // 2, width), BF16), pltpu.SemaphoreType.DMA((2 * steps,))]
    sums = pltpu.VMEM((width, width), F32)
    pair = [shape(3, half, half), shape(3, half, half, dtype=HALVES)]
    keep_c, send_c, w = call(
        far_kernel, "far_tile", (), [SMEM, VMEM, anywhere, VMEM, VMEM], [VMEM] * 3,
        pair + [shape(depth, width, dtype=BF16)], [sums] + parts, tile_flops, 3 * bytes_block)(
        pos, turned, w_raw, stat, w_stat)
    send_c, diag_got = lax.optimization_barrier((send_c, diag_got))
    got_c = send(send_c, across)

    keep_b, send_b, y = call(
        near_kernel, "near_tile", (), [SMEM, VMEM, anywhere, VMEM, VMEM], [VMEM] * 3,
        pair + [shape(width, depth, dtype=BF16)], [sums] + parts, tile_flops, 3 * bytes_block)(
        pos, turned, y_raw, stat, y_stat)
    got_b = send(send_b, across_active)
    keep_d, send_d = call(
        lambda *refs: cross_kernel(steps, *refs), "cross_tile", (), [SMEM] + [VMEM] * 4, [VMEM] * 2, pair, [sums],
        tile_flops, 2 * bytes_block)(pos, y, w, y_stat, w_stat)
    send_d, got_c = lax.optimization_barrier((send_d, got_c))
    got_d = send(send_d, across_active)

    held_c, to_z_c = call(far_strips_kernel, "far_strips", (), [SMEM] + [VMEM] * 2, [VMEM] * 2,
                          [shape(half, width), shape(half, width, dtype=STRIPS)])(pos, keep_c, got_c)
    from_z_c = send(to_z_c, z_cross)
    got_b, to_z_c = lax.optimization_barrier((got_b, to_z_c))

    def near_strips(name, kind, keep, got):
        return call(near_strips_kernel, name, (), [SMEM] + [VMEM] * 2, [VMEM] * 2, [shape(half, width, dtype=kind)] * 2)(
            pos, keep, got)

    held_b, to_y_b = near_strips("near_strips", F32, keep_b, got_b)
    from_y_b = send(to_y_b, y_cross)
    got_d, to_y_b = lax.optimization_barrier((got_d, to_y_b))
    to_y_d, to_z_d = near_strips("cross_strips", STRIPS, keep_d, got_d)
    from_y_d, from_z_d = send(to_y_d, y_cross), send(to_z_d, z_cross_active)

    mine, sib = call(combine_kernel, "combine", (), [SMEM] + [VMEM] * 6, [VMEM] * 2, [shape(3, strip, width)] * 2)(
        pos, held_b, held_c, from_y_b, from_y_d, from_z_c, from_z_d)
    return call(finish_kernel, "finish", (), [SMEM] * 2 + [VMEM] * 4, [VMEM] * 2,
                [shape(1, SLOTS, strip, width, dtype=BF16), shape(1, 2, strip, width, dtype=BF16)])(
        pos, pair_offsets, diag_mine, diag_got, mine, send(sib, sibling))


def solution(mesh):
    in_specs = (P("samp", "var"), P("var", None), P("var"))
    out_specs = (P("var", None, "samp", None), P("var", None, "samp", None))
    return jax.shard_map(body, mesh=mesh, in_specs=in_specs, out_specs=out_specs, check_vma=False)
```

```python
import jax
import jax.numpy as jnp
from jax import lax
from jax.experimental import pallas as pl
from jax.experimental.pallas import tpu as pltpu
from jax.sharding import PartitionSpec as P

SLOTS = 3
AXES = ("var", "samp")
F32 = jnp.float32
BF16 = jnp.bfloat16
VMEM = pl.BlockSpec(memory_space=pltpu.VMEM)
SMEM = pl.BlockSpec(memory_space=pltpu.SMEM)
SOME = pltpu.CompilerParams(vmem_limit_bytes=24 << 20)
HALVES, STRIPS = BF16, BF16


def dot(a, b):
    return jnp.dot(a, b, preferred_element_type=F32)


def standardized(raw, stat_ref):
    return ((raw.astype(F32) - stat_ref[0:1, :]) * stat_ref[1:2, :]).astype(BF16)


def local_kernel(steps, x_ref, out_ref, center, total, square):
    step = pl.program_id(0)
    rows, width = x_ref.shape
    group = min(64, rows)

    @pl.when(step == 0)
    def _():
        center[...] = jnp.mean(x_ref[:group, :].astype(F32), axis=0, keepdims=True)
        total[...] = jnp.zeros_like(total)
        square[...] = jnp.zeros_like(square)

    middle = center[...]

    def add(i, sums):
        x = x_ref[pl.ds(pl.multiple_of(i * group, group), group), :].astype(F32) - middle
        x = x.reshape(group // 8, 8, width)
        return sums[0] + jnp.sum(x, axis=0), sums[1] + jnp.sum(x * x, axis=0)

    sums = lax.fori_loop(0, rows // group, add, (total[...], square[...]))
    total[...], square[...] = sums

    @pl.when(step == steps - 1)
    def _():
        count = float(rows * steps)
        shift = jnp.sum(total[...], axis=0, keepdims=True) * (1.0 / count)
        around = jnp.sum(square[...], axis=0, keepdims=True) - shift * shift * count
        out_ref[0:1, :] = middle + shift
        out_ref[1:2, :] = jnp.maximum(around, 0.0)


def stat_kernel(pos_ref, live_ref, offsets_ref, own_ref, sib_ref, far_ref, cross_ref, stat_ref):
    width = own_ref.shape[1]
    samples = pos_ref[4].astype(F32)

    def merged(values):
        return (values[0] + values[1]) + (values[2] + values[3])

    groups = (own_ref, sib_ref, far_ref, cross_ref)
    mean = merged([ref[0:1, :] for ref in groups]) * 0.25
    between = merged([jnp.square(ref[0:1, :] - mean) for ref in groups]) * (samples * 0.25)
    spread = (merged([ref[1:2, :] for ref in groups]) + between) / samples
    live = lax.broadcasted_iota(jnp.int32, (1, width), 1) < live_ref[0]
    stat_ref[0:1, :] = mean
    stat_ref[1:2, :] = jnp.where(live, lax.rsqrt(spread + 1e-05), 0.0)
    for step in (1, 2):
        listed = offsets_ref[0, 0] == step
        for slot in range(1, SLOTS):
            listed = jnp.logical_or(listed, offsets_ref[0, slot] == step)
        stat_ref[1 + step:2 + step, :] = jnp.full((1, width), jnp.where(listed, 1.0, 0.0), F32)


def own_kernel(pos_ref, x_ref, stat_ref, turned_ref, keep_ref, send_ref, acc):
    step = pl.program_id(0)
    z = standardized(x_ref[...], stat_ref)
    zt = z.T
    turned_ref[...] = zt
    part = dot(zt, z)

    @pl.when(step == 0)
    def _():
        acc[...] = part

    @pl.when(step > 0)
    def _():
        acc[...] += part

    @pl.when(step == pl.num_programs(0) - 1)
    def _():
        rows = keep_ref.shape[1]
        for far in range(2):
            for core, out in ((pos_ref[2], keep_ref), (1 - pos_ref[2], send_ref)):
                out[far] = acc[pl.ds(pl.multiple_of((2 * far + core) * rows, rows), rows), :]


def diag_kernel(pos_ref, keep_ref, got_ref, mine_ref, send_ref):
    mine_ref[...] = keep_ref[pos_ref[0]] + got_ref[pos_ref[0]]
    send_ref[...] = keep_ref[1 - pos_ref[0]] + got_ref[1 - pos_ref[0]]


def put_quarters(x, source, scale, keep, send):
    half = keep.shape[-1]
    scale = scale[:, :half]
    for out, near in ((keep, x), (send, 1 - x)):
        for index, (row, col) in enumerate(((near, near), (near, 1 - near), (1 - near, near))):
            rows = pl.ds(pl.multiple_of(row * half, half), half)
            cols = pl.ds(pl.multiple_of(col * half, half), half)
            out[index] = (source[rows, cols] * scale).astype(out.dtype)


def fetched(source, parts, sems):
    rows = parts.shape[1]
    copies = [pltpu.make_async_copy(source.at[pl.ds(k * rows, rows), :], parts.at[k], sems.at[k])
              for k in range(parts.shape[0])]
    for copy in copies:
        copy.start()
    return [(slice(k * rows, (k + 1) * rows), copy.wait) for k, copy in enumerate(copies)]


def far_kernel(pos_ref, turned_ref, w_ref, stat_ref, wstat_ref, keep_ref, send_ref, w_out, acc, parts, sems):
    for k, (rows, wait) in enumerate(fetched(w_ref, parts, sems)):
        wait()
        w = standardized(parts[k], wstat_ref)
        w_out[rows, :] = w
        part = dot(turned_ref[:, rows], w)
        acc[...] = part if k == 0 else acc[...] + part
    listed = jnp.where(pos_ref[2] == 0, stat_ref[3:4, :], wstat_ref[3:4, :])
    put_quarters(pos_ref[0], acc, listed * (1.0 / pos_ref[4].astype(F32)), keep_ref, send_ref)


def near_kernel(pos_ref, turned_ref, y_ref, stat_ref, ystat_ref, keep_ref, send_ref, y_out, acc, parts, sems):
    @pl.when(pos_ref[1] == 1)
    def _():
        for k, (rows, wait) in enumerate(fetched(y_ref, parts, sems)):
            wait()
            y = standardized(parts[k], ystat_ref)
            y_out[:, rows] = y.T
            part = dot(turned_ref[:, rows], y)
            acc[...] = part if k == 0 else acc[...] + part
        listed = jnp.where(pos_ref[2] == 0, stat_ref[2:3, :], ystat_ref[2:3, :])
        put_quarters(pos_ref[0], acc, listed * (1.0 / pos_ref[4].astype(F32)), keep_ref, send_ref)


def cross_kernel(steps, pos_ref, y_ref, w_ref, ystat_ref, wstat_ref, keep_ref, send_ref, acc):
    @pl.when(pos_ref[1] == 1)
    def _():
        size = w_ref.shape[0] // steps
        for k in range(steps):
            rows = slice(k * size, (k + 1) * size)
            part = dot(y_ref[:, rows], w_ref[rows, :])
            acc[...] = part if k == 0 else acc[...] + part
        listed = jnp.where(pos_ref[2] == 0, ystat_ref[2:3, :], wstat_ref[2:3, :])
        put_quarters(pos_ref[0], acc, listed * (1.0 / pos_ref[4].astype(F32)), keep_ref, send_ref)


def add_halves(x, keep, got, rows_out, cols_out):
    half = keep.shape[-1]
    here = pl.ds(pl.multiple_of(x * half, half), half)
    there = pl.ds(pl.multiple_of((1 - x) * half, half), half)
    corner = keep[0] + got[0].astype(F32)
    rows_out[:, here] = corner.astype(rows_out.dtype)
    rows_out[:, there] = (keep[1] + got[1].astype(F32)).astype(rows_out.dtype)
    cols_out[:, here] = corner.T.astype(cols_out.dtype)
    cols_out[:, there] = (keep[2] + got[2].astype(F32)).T.astype(cols_out.dtype)


def far_strips_kernel(pos_ref, keep, got, held, to_z):
    add_halves(pos_ref[0], keep, got, held, to_z)


def near_strips_kernel(pos_ref, keep, got, rows_out, cols_out):
    @pl.when(pos_ref[1] == 1)
    def _():
        add_halves(pos_ref[0], keep, got, rows_out, cols_out)


def combine_kernel(pos_ref, held_b, held_c, from_y_b, from_y_d, from_z_c, from_z_d, mine, sib):
    rows = mine.shape[1]
    for core, out in ((pos_ref[2], mine), (1 - pos_ref[2], sib)):
        at = pl.ds(pl.multiple_of(core * rows, rows), rows)
        out[1] = held_c[at, :] + from_z_c[at, :].astype(F32)

        @pl.when(pos_ref[1] == 1)
        def _():
            out[0] = held_b[at, :] + from_y_b[at, :]
            out[2] = from_y_d[at, :].astype(F32)

        @pl.when(pos_ref[1] == 0)
        def _():
            out[2] = from_z_d[at, :].astype(F32)


def finish_kernel(pos_ref, offsets_ref, diag_mine, diag_got, mine, sib, upper, mirror):
    active = pos_ref[1] == 1
    first_core = pos_ref[2] == 0
    even = pos_ref[3] == 0
    pick = jnp.where
    near = pick(active, mine[0], sib[0])
    far = mine[2] + sib[2]
    upper_1 = pick(even, near, far)
    upper_2 = pick(first_core, mine[1], sib[1])
    mirror[0, 0] = pick(even, far, near).astype(BF16)
    mirror[0, 1] = pick(first_core, sib[1], mine[1]).astype(BF16)
    self_tile = (diag_mine[...] + diag_got[...]) * (1.0 / pos_ref[4].astype(F32))
    for slot in range(SLOTS):
        offset = offsets_ref[0, slot]
        tile = pick(offset == 0, self_tile, pick(offset == 1, upper_1, pick(offset == 2, upper_2, 0.0)))
        upper[0, slot] = tile.astype(BF16)


def body(dosage, pair_offsets, live_counts):
    n_var = lax.axis_size("var")
    n_samp = lax.axis_size("samp")
    depth, width = dosage.shape
    half = width // 2
    strip = width // n_samp
    samples_all = depth * n_samp
    v = lax.axis_index("var")
    s = lax.axis_index("samp")
    x, core, odd = s // 2, s % 2, v % 2
    active = (core == odd).astype(jnp.int32)

    def at(var, samp):
        return var * n_samp + samp

    def active_on(var, samp):
        return var % 2 == samp % 2

    def send(value, pairs):
        return lax.ppermute(value, AXES, pairs)

    def shape(*dims, dtype=F32):
        return jax.ShapeDtypeStruct(dims, dtype)

    everyone = [(var, samp) for var in range(n_var) for samp in range(n_samp)]
    z_main = [(at(a, b), at(a - 2 if b % 2 == 0 else a + 2, b)) for a, b in everyone
              if 0 <= (a - 2 if b % 2 == 0 else a + 2) < n_var]
    y_main = [(at(a, b), at(a ^ 1, b)) for a, b in everyone if not active_on(a, b)]
    z_step = [(a, b, a + 2 if b % 2 == 0 else a - 2) for a, b in everyone]
    z_cross = [(at(a, b), at(t, b ^ 1)) for a, b, t in z_step if 0 <= t < n_var]
    z_cross_active = [(at(a, b), at(t, b ^ 1)) for a, b, t in z_step if 0 <= t < n_var and active_on(a, b)]
    y_cross = [(at(a, b), at(a ^ 1, b ^ 1)) for a, b in everyone if active_on(a, b)]
    across = [(at(a, b), at(a, b ^ 2)) for a, b in everyone]
    across_active = [(at(a, b), at(a, b ^ 2)) for a, b in everyone if active_on(a, b)]
    sibling = [(at(a, b), at(a, b ^ 1)) for a, b in everyone]

    w_raw, y_raw = send(dosage, z_main), send(dosage, y_main)

    pos = jnp.stack([x, active, core, odd, jnp.int32(samples_all)]).astype(jnp.int32)
    step_rows = min(1024, depth)
    steps = depth // step_rows
    wide = pl.BlockSpec((step_rows, width), lambda k: (k, 0))
    flat = pl.BlockSpec((width, step_rows), lambda k: (0, k))
    whole = lambda *dims: pl.BlockSpec(dims, lambda k: (0,) * len(dims))

    def call(kernel, name, grid, in_specs, out_specs, out_shape, scratch=(), flops=0, moved=0):
        return pl.pallas_call(
            kernel, grid=grid, in_specs=in_specs, out_specs=out_specs, out_shape=out_shape, scratch_shapes=scratch,
            compiler_params=SOME, name=name,
            cost_estimate=pl.CostEstimate(flops=flops, bytes_accessed=moved, transcendentals=0))

    bytes_block, tile_flops = 2 * depth * width, 2 * depth * width * width
    local = call(lambda *refs: local_kernel(steps, *refs), "local_stats", (steps,), [wide], whole(2, width), shape(2, width),
                 [pltpu.VMEM((1, width), F32)] + [pltpu.VMEM((8, width), F32)] * 2, 5 * depth * width, bytes_block)(dosage)
    others = [send(local, [(at(a, b), at(a, b ^ flip)) for a, b in everyone]) for flip in (1, 2, 3)]
    stat = call(stat_kernel, "stats", (), [SMEM] * 3 + [VMEM] * 4, VMEM, shape(4, width))(
        pos, live_counts, pair_offsets, local, *others)
    w_stat, y_stat = send(stat, z_cross), send(stat, y_cross)

    turned, diag_keep, diag_send = call(
        own_kernel, "own_tile", (steps,), [SMEM, wide, whole(4, width)],
        [flat, whole(2, strip, width), whole(2, strip, width)],
        [shape(width, depth, dtype=BF16), shape(2, strip, width), shape(2, strip, width)],
        [pltpu.VMEM((width, width), F32)], tile_flops, 2 * bytes_block)(pos, dosage, stat)
    diag_mine, diag_other = call(diag_kernel, "own_tile_strips", (), [SMEM, VMEM, VMEM], [VMEM] * 2, [shape(strip, width)] * 2)(
        pos, diag_keep, send(diag_send, sibling))
    diag_got = send(diag_other, across)

    anywhere = pl.BlockSpec(memory_space=pl.ANY)
    halves = max(steps // 2, 1)
    parts = [pltpu.VMEM((halves, depth // halves, width), BF16), pltpu.SemaphoreType.DMA((halves,))]
    sums = pltpu.VMEM((width, width), F32)
    pair = [shape(3, half, half), shape(3, half, half, dtype=HALVES)]
    keep_c, send_c, w = call(
        far_kernel, "far_tile", (), [SMEM, VMEM, anywhere, VMEM, VMEM], [VMEM] * 3,
        pair + [shape(depth, width, dtype=BF16)], [sums] + parts, tile_flops, 3 * bytes_block)(
        pos, turned, w_raw, stat, w_stat)
    send_c, diag_got = lax.optimization_barrier((send_c, diag_got))
    got_c = send(send_c, across)

    keep_b, send_b, y = call(
        near_kernel, "near_tile", (), [SMEM, VMEM, anywhere, VMEM, VMEM], [VMEM] * 3,
        pair + [shape(width, depth, dtype=BF16)], [sums] + parts, tile_flops, 3 * bytes_block)(
        pos, turned, y_raw, stat, y_stat)
    got_b = send(send_b, across_active)
    keep_d, send_d = call(
        lambda *refs: cross_kernel(steps, *refs), "cross_tile", (), [SMEM] + [VMEM] * 4, [VMEM] * 2, pair, [sums],
        tile_flops, 2 * bytes_block)(pos, y, w, y_stat, w_stat)
    send_d, got_c = lax.optimization_barrier((send_d, got_c))
    got_d = send(send_d, across_active)

    held_c, to_z_c = call(far_strips_kernel, "far_strips", (), [SMEM] + [VMEM] * 2, [VMEM] * 2,
                          [shape(half, width), shape(half, width, dtype=STRIPS)])(pos, keep_c, got_c)
    from_z_c = send(to_z_c, z_cross)
    got_b, to_z_c = lax.optimization_barrier((got_b, to_z_c))

    def near_strips(name, kind, keep, got):
        return call(near_strips_kernel, name, (), [SMEM] + [VMEM] * 2, [VMEM] * 2, [shape(half, width, dtype=kind)] * 2)(
            pos, keep, got)

    held_b, to_y_b = near_strips("near_strips", F32, keep_b, got_b)
    from_y_b = send(to_y_b, y_cross)
    got_d, to_y_b = lax.optimization_barrier((got_d, to_y_b))
    to_y_d, to_z_d = near_strips("cross_strips", STRIPS, keep_d, got_d)
    from_y_d, from_z_d = send(to_y_d, y_cross), send(to_z_d, z_cross_active)

    mine, sib = call(combine_kernel, "combine", (), [SMEM] + [VMEM] * 6, [VMEM] * 2, [shape(3, strip, width)] * 2)(
        pos, held_b, held_c, from_y_b, from_y_d, from_z_c, from_z_d)
    return call(finish_kernel, "finish", (), [SMEM] * 2 + [VMEM] * 4, [VMEM] * 2,
                [shape(1, SLOTS, strip, width, dtype=BF16), shape(1, 2, strip, width, dtype=BF16)])(
        pos, pair_offsets, diag_mine, diag_got, mine, send(sib, sibling))


def solution(mesh):
    in_specs = (P("samp", "var"), P("var", None), P("var"))
    out_specs = (P("var", None, "samp", None), P("var", None, "samp", None))
    return jax.shard_map(body, mesh=mesh, in_specs=in_specs, out_specs=out_specs, check_vma=False)
```
